128 devices in a mesh: section: 2 (over core), seq: 4 (over y), shard: 16 (over z, x).
Axes of the slice: x: 4, y: 4, z: 4, core: 2. Of those that a mesh axis runs over, the one named last changes fastest.
Arguments:
- images_in: bfloat16 [2, 16, 576, 768], P(None, 'shard', 'seq'), may hold values from -6 to 6
- out_grad: bfloat16 [2, 16, 576, 768], P(None, 'shard', 'seq'), may hold values from -6 to 6
- routes: int32 [2, 2, 16, 576, 2], P('section', None, 'shard', 'seq'), may hold values from 0 to 3, all different within a row; in each aligned block of 144 rows (0 to 143, 144 to 287, ..., all dimensions but the last counted through in order) at most 80 rows name the same one
- w_qkv: bfloat16 [2, 768, 2304], P('section', ('seq', 'shard')), may hold values from -0.21875 to 0.21875
- w_proj: bfloat16 [2, 768, 768], P('section', ('seq', 'shard')), may hold values from -2.5 to 2.5
- w_route: bfloat16 [2, 768, 4], P('section', ('seq', 'shard')), may hold values from -0.21875 to 0.21875
- gain_attn: bfloat16 [2, 768], P('section', ('seq', 'shard')), may hold values from 0.5 to 1.5
- gain_ffn: bfloat16 [2, 768], P('section', ('seq', 'shard')), may hold values from 0.5 to 1.5
- w_in: bfloat16 [2, 4, 768, 3072], P('section', 'seq', 'shard'), may hold values from -0.21875 to 0.21875
- w_out: bfloat16 [2, 4, 3072, 768], P('section', 'seq', 'shard'), may hold values from -0.21875 to 0.21875
Outputs:
- layer_out: bfloat16 [2, 2, 16, 576, 768], P('section', None, 'shard', 'seq')
- in_grad: bfloat16 [2, 2, 16, 576, 768], P('section', None, 'shard', 'seq')
- grad_qkv: float32 [2, 768, 2304], P('section', ('seq', 'shard'))
- grad_proj: float32 [2, 768, 768], P('section', ('seq', 'shard'))
- grad_route: float32 [2, 768, 4], P('section', ('seq', 'shard'))
- grad_gain_attn: float32 [2, 768], P('section', ('seq', 'shard'))
- grad_gain_ffn: float32 [2, 768], P('section', ('seq', 'shard'))
- grad_expert_in: float32 [2, 4, 768, 3072], P('section', 'seq', 'shard')
- grad_expert_out: float32 [2, 4, 3072, 768], P('section', 'seq', 'shard')
The draws below stay inside these ranges and needn't reach their ends.
Inputs may be any that keep to these rules, and one draw needn't show every extreme that they name: `routes`: within the tokens of one image on one index of seq (aligned blocks of rows), no expert is named more than 80 times, and the two experts of a token differ.
All inputs are finite; a program needn't handle non-finite values.
Results may differ from the reference program's by a relative error of at most 0.02.
Values may be sent and summed in bfloat16 or wider, within the bound.
No kernel may reach another device: no remote copies, remote signals or barrier semaphores. Data moves between devices by JAX's collectives and lax.ppermute only.
A program may use at most 320 MiB of HBM per device.

```python
import math
import jax
import jax.numpy as jnp
import numpy as np
from jax import lax

D = 768
FF = 3072
HEADS = 12
HEAD_DIM = 64
SEQ = 576
CAP = 80
MICRO = 2
EXPERTS = 4
IMAGES = 16
N_SECTION = 2
N_SEQ = 4


def shard_levels(stream_key, extent, shards, least, largest):
    def one(dim, blocks):
        heights = jax.random.uniform(jax.random.fold_in(jax.random.fold_in(stream_key, 6), dim), (blocks,), jnp.float32, least / len(shards), largest / len(shards))
        return jnp.repeat(jnp.exp(heights), extent[dim] // blocks).reshape((-1,) + (1,) * (len(extent) - dim - 1))

    loudness = one(*shards[0])
    for cut in shards[1:]:
        loudness = loudness * one(*cut)
    return loudness


def deal_out(stream_key, own, number, rows, count, top, reach, lean):
    order = jax.random.permutation(stream_key, count)
    crowded, usual = load_shares(count, rows * top, reach, lean, True), load_shares(count, rows * top, reach, lean, False)
    places = jnp.arange(count)

    def named(lengths, turn):
        used = int((lengths > 0).sum())
        fixed = max(1, used // 4)
        passed = fixed + (places - fixed + turn * (used - fixed)) % max(1, count - fixed)
        return jnp.zeros((count,), jnp.int32).at[order[jnp.where(places < fixed, places, passed)]].set(jnp.asarray(lengths, jnp.int32))

    lengths = jnp.where(number % 4 == 0, named(crowded, number // 4), named(usual, number - number // 4 - 1))
    mixed = jax.random.permutation(jax.random.fold_in(own, 3), count)
    giver, sink = mixed[0:count // 2 * 2:2], mixed[1:count // 2 * 2:2]
    room = jnp.minimum(lengths[giver] - 1, reach - lengths[sink]) // 2
    room = jnp.where((giver == order[0]) | (sink == order[0]) | (lengths[sink] == 0), 0, jnp.maximum(room, 0))
    passed = jax.random.randint(jax.random.fold_in(own, 4), (count // 2,), 0, 1 << 20) % (room + 1)
    lengths = lengths.at[giver].add(-passed).at[sink].add(passed)
    labels = jnp.searchsorted(jnp.cumsum(lengths), jnp.arange(rows * top), side="right").astype(jnp.int32)
    grid = labels.reshape(top, rows).T
    grid = grid[jax.random.permutation(jax.random.fold_in(own, 1), rows)]
    turn = jax.random.randint(jax.random.fold_in(own, 2), (rows, 1), 0, top)
    return jnp.take_along_axis(grid, (jnp.arange(top)[None, :] + turn) % top, axis=1)


def load_shares(number_of, total, reach, lean, full):
    portions = [(1 << 20) // math.isqrt(rank ** lean) + 1 for rank in range(1, number_of + 1)]
    largest = reach if full else min(reach, max(-(-total // number_of), total * portions[0] // sum(portions)))
    least = 1 if total - largest >= number_of - 1 else 0
    given, spare = [largest] + [least] * (number_of - 1), total - largest - least * (number_of - 1)
    while spare > 0:
        candidates = [i for i in range(1, number_of) if given[i] < largest] or [i for i in range(1, number_of) if given[i] < reach]
        pool, budget = sum([portions[i] for i in candidates]), spare
        for i in candidates:
            more = min(reach - given[i], max(1, budget * portions[i] // pool), spare)
            given[i] = given[i] + more
            spare = spare - more
    return np.array(given)


def normal_values(own_key, dims, spread, reach, cuts=(), kind=jnp.bfloat16):
    array = jax.random.normal(own_key, dims, jnp.float32) * spread
    if len(cuts) > 0:
        array = shard_levels(own_key, dims, cuts, -0.22, 0.18) * array
    return jnp.clip(array, min=-reach, max=reach).astype(kind)


def setup_inputs(seed: int = 0) -> dict:
    arg_keys = jax.random.split(jax.random.key(seed), 11)
    images_in = normal_values(arg_keys[0], (MICRO, IMAGES, SEQ, D), 1.0, 6.0, ((1, 16), (2, 4)))
    out_grad = normal_values(arg_keys[1], (MICRO, IMAGES, SEQ, D), 1.0, 6.0, ((1, 16), (2, 4)))
    routes_keys = jax.random.split(jax.random.fold_in(arg_keys[2], 1), N_SECTION * MICRO * IMAGES * SEQ // (SEQ // N_SEQ))
    routes_turns = jax.random.permutation(jax.random.fold_in(arg_keys[2], 3), N_SECTION * MICRO * IMAGES * SEQ // (SEQ // N_SEQ))
    routes = jax.vmap(lambda own, number: deal_out(jax.random.fold_in(arg_keys[2], 2), own, number, SEQ // N_SEQ, EXPERTS, 2, CAP, 0))(routes_keys, routes_turns).reshape((N_SECTION, MICRO, IMAGES, SEQ, 2))
    w_qkv = normal_values(arg_keys[3], (N_SECTION, D, 3 * D), D ** -0.5, 0.21875, ((0, 2), (1, 64)))
    w_proj = normal_values(arg_keys[4], (N_SECTION, D, D), (max(D // 128, 1)) ** -0.5, 2.5, ((0, 2), (1, 64)))
    w_route = normal_values(arg_keys[5], (N_SECTION, D, EXPERTS), D ** -0.5, 0.21875, ((0, 2), (1, 64)))
    gain_attn = jnp.clip(1.0 + 0.1 * jax.random.normal(arg_keys[6], (N_SECTION, D), jnp.float32), 0.5, 1.5).astype(jnp.bfloat16)
    gain_ffn = jnp.clip(1.0 + 0.1 * jax.random.normal(arg_keys[7], (N_SECTION, D), jnp.float32), 0.5, 1.5).astype(jnp.bfloat16)
    w_in = normal_values(arg_keys[8], (N_SECTION, EXPERTS, D, FF), D ** -0.5, 0.21875, ((0, 2), (1, 4), (2, 16)))
    w_out = normal_values(arg_keys[9], (N_SECTION, EXPERTS, FF, D), (FF // 4) ** -0.5, 0.21875, ((0, 2), (1, 4), (2, 16)))
    return dict(images_in=images_in, out_grad=out_grad, routes=routes, w_qkv=w_qkv, w_proj=w_proj, w_route=w_route, gain_attn=gain_attn, gain_ffn=gain_ffn, w_in=w_in, w_out=w_out)


EPSILON = 1e-06
HIGHEST = lax.Precision.HIGHEST

@jax.custom_vjp
def low(v):
    return lax.optimization_barrier(v.astype(jnp.bfloat16)).astype(jnp.float32)

@jax.custom_vjp
def low_back(v):
    return v

def low_keep(v):
    return (low(v), None)

def low_pass(kept, grad):
    return (grad,)

def back_keep(v):
    return (v, None)

def back_low(kept, grad):
    return (low(grad),)
low.defvjp(low_keep, low_pass)
low_back.defvjp(back_keep, back_low)

def product(left_side, right_side):
    return jnp.dot(left_side, right_side, precision=HIGHEST)

def norm_rows(values, gain_vec):
    centred = values - lax.optimization_barrier(jnp.mean(values, axis=-1, keepdims=True))
    inverse = lax.rsqrt(lax.optimization_barrier(jnp.mean(centred * centred, axis=-1, keepdims=True)) + EPSILON)
    return centred * inverse * gain_vec

def slot_numbers(route_ids):
    block_len = SEQ // N_SEQ
    flattened = route_ids.reshape(N_SEQ, block_len * 2)
    expert_ids = jnp.arange(EXPERTS, dtype=jnp.int32)
    matches = (flattened[:, :, None] == expert_ids).astype(jnp.int32)
    before = jnp.cumsum(matches, axis=1).astype(jnp.int32) - matches
    ranking = lax.optimization_barrier(jnp.sum(before * matches, axis=2)).astype(jnp.int32)
    offsets = jnp.arange(N_SEQ, dtype=jnp.int32)[:, None] * CAP
    return (flattened * (N_SEQ * CAP) + offsets + ranking).reshape(SEQ * 2).astype(jnp.int32)

def layer_image(tokens, route_ids, params):
    w_mix, w_back, w_router, gain_one, gain_two, w_first, w_second = params
    normed = low(norm_rows(tokens, gain_one))
    packed = low_back(low(product(normed, w_mix)))
    divided = packed.reshape(SEQ, 3, HEADS, HEAD_DIM)
    queries = divided[:, 0]
    key_rows = divided[:, 1]
    value_rows = divided[:, 2]
    scores = low_back(jnp.einsum('qhd,khd->hqk', queries, key_rows, precision=HIGHEST) * HEAD_DIM ** (-0.5))
    attention = jax.nn.softmax(scores, axis=-1)
    mixture = jnp.einsum('hqk,khd->qhd', low(attention), value_rows, precision=HIGHEST)
    mixture = low_back(low(mixture)).reshape(SEQ, D)
    residual = tokens + low_back(product(mixture, w_back))
    normed_two = low(norm_rows(residual, gain_two))
    gate_probs = jax.nn.softmax(product(normed_two, w_router), axis=-1)
    chosen = jnp.take_along_axis(gate_probs, route_ids, axis=1)
    slot_ids = slot_numbers(route_ids)
    total_slots = EXPERTS * N_SEQ * CAP
    filled = jnp.zeros((total_slots,), jnp.float32).at[slot_ids].set(1.0)
    source = jnp.zeros((total_slots,), jnp.int32).at[slot_ids].set(jnp.arange(SEQ * 2, dtype=jnp.int32) // 2)
    slab_rows = low_back(normed_two[source] * filled[:, None]).reshape(EXPERTS, N_SEQ * CAP, D)
    hidden = low_back(jnp.einsum('erd,edf->erf', slab_rows, w_first, precision=HIGHEST))
    active = low(jax.nn.gelu(hidden, approximate=False))
    result = low_back(low(jnp.einsum('erf,efd->erd', active, w_second, precision=HIGHEST)))
    picked = result.reshape(total_slots, D)[slot_ids].reshape(SEQ, 2, D)
    return residual + lax.optimization_barrier(jnp.sum(chosen[:, :, None] * picked, axis=1))

def reference(images_in, out_grad, routes, w_qkv, w_proj, w_route, gain_attn, gain_ffn, w_in, w_out):
    params = tuple((weight.astype(jnp.float32) for weight in (w_qkv, w_proj, w_route, gain_attn, gain_ffn, w_in, w_out)))
    image_count = MICRO * IMAGES
    inputs = images_in.astype(jnp.float32).reshape(image_count, SEQ, D)
    seed_grad = out_grad.astype(jnp.float32).reshape(image_count, SEQ, D)
    route_all = routes.reshape(N_SECTION, image_count, SEQ, 2)
    margin = jnp.zeros((N_SECTION, image_count, SEQ, D), jnp.float32)
    stepper = jax.checkpoint(layer_image)

    def run_section(current, route_set, layer_params):
        return lax.map(lambda paired: stepper(paired[0], paired[1], layer_params), (current, route_set))

    def whole(margin_arg, param_arg):
        outputs = []
        current = inputs + margin_arg[0]
        for layer_num in range(N_SECTION):
            if layer_num > 0:
                current = low_back(low(outputs[-1])) + margin_arg[layer_num]
            layer_params = tuple((weight[layer_num] for weight in param_arg))
            outputs.append(run_section(current, route_all[layer_num], layer_params))
        return jnp.stack(outputs)
    stacked, pullback = jax.vjp(whole, margin, params)
    seeded = jnp.zeros_like(stacked).at[N_SECTION - 1].set(seed_grad)
    d_margin, d_params = pullback(seeded)
    shape_out = (N_SECTION, MICRO, IMAGES, SEQ, D)
    return (stacked.reshape(shape_out).astype(jnp.bfloat16), d_margin.reshape(shape_out).astype(jnp.bfloat16), d_params[0], d_params[1], d_params[2], d_params[3], d_params[4], d_params[5], d_params[6])
```

```python
from functools import partial

import jax
import jax.numpy as jnp
from jax import lax
from jax.sharding import PartitionSpec as P

D = 768
FF = 3072
HEAD_DIM = 64
CAP = 80
N_SEQ = 4
N_SHARD = 16
GROUP = 3
ROWS = 144
SEQ = 576
WIDE = 896
EPSILON = 1e-06
F32 = jnp.float32
BF16 = jnp.bfloat16


def dot(a, b, ca, cb):
    return lax.dot_general(a, b, (((ca,), (cb,)), ((), ())), preferred_element_type=F32)


def swap(v):
    return lax.ppermute(v, "section", [(0, 1), (1, 0)])


def turn(v, d):
    return lax.ppermute(v, "seq", [(i, (i + d) % N_SEQ) for i in range(N_SEQ)])


def hop(v, axis, d):
    route = []
    for z in range(4):
        for x in range(4):
            to = ((z + d) % 4) * 4 + x if axis == "z" else z * 4 + (x + d) % 4
            route.append((z * 4 + x, to))
    return lax.ppermute(v, "shard", route)


def place(axis):
    i = lax.axis_index("shard")
    return i // 4 if axis == "z" else lax.rem(i, 4)


def pick(v, i):
    return lax.dynamic_index_in_dim(v, i, 0, keepdims=False)


def gather_four(v, axis):
    blocks = [v] + [hop(v, axis, -d) for d in (1, 2, 3)]
    joined = jnp.stack(blocks + blocks[:3])
    return lax.dynamic_slice_in_dim(joined, lax.rem(4 - place(axis), 4), 4, 0)


def gather_shard(v):
    along = gather_four(v, "x")
    return gather_four(along, "z").reshape((N_SHARD,) + v.shape)


def scatter_four(v, axis):
    me = place(axis)
    total = pick(v, me).astype(F32)
    for d in (1, 2, 3):
        total = total + hop(pick(v, lax.rem(me + d, 4)), axis, d).astype(F32)
    return total


def scatter_shard(v):
    parts = v.reshape((4, 4) + v.shape[1:])
    first = scatter_four(parts[:, :, 0].swapaxes(0, 1), "x").astype(BF16)
    second = scatter_four(parts[:, :, 1], "z").astype(BF16)
    return jnp.stack([scatter_four(first, "z"), scatter_four(second, "x")])


def norm_parts(values):
    centred = values - jnp.mean(values, axis=-1, keepdims=True)
    inverse = lax.rsqrt(jnp.mean(centred * centred, axis=-1, keepdims=True) + EPSILON)
    return centred * inverse, inverse


def norm_back(n, inverse, gain, dy):
    gdy = dy * gain
    return (
        gdy
        - jnp.mean(gdy, axis=-1, keepdims=True)
        - n * jnp.mean(gdy * n, axis=-1, keepdims=True)
    ) * inverse


def gather_tokens(x):
    return jnp.concatenate([x] + [turn(x, -d) for d in (1, 2, 3)], axis=0)


def attend(x_all, w_mix, gain):
    normed = (norm_parts(x_all.astype(F32))[0] * gain).astype(BF16)
    packed = dot(normed, w_mix, 1, 0).astype(BF16)
    heads = packed.reshape(SEQ, 3, GROUP, HEAD_DIM)
    scores = jnp.einsum("qhd,khd->hqk", heads[:, 0], heads[:, 1], preferred_element_type=F32)
    scores = scores * HEAD_DIM ** (-0.5)
    top = jnp.max(scores, axis=-1, keepdims=True)
    exponent = jnp.exp(scores - top)
    totals = jnp.sum(exponent, axis=-1, keepdims=True)
    attention = (exponent / totals).astype(BF16)
    mixture = jnp.einsum("hqk,khd->qhd", attention, heads[:, 2], preferred_element_type=F32)
    return mixture.astype(BF16).reshape(SEQ, GROUP * HEAD_DIM), normed, packed, top + jnp.log(totals)


def attend_back(packed, log_total, d_mixture):
    heads = packed.reshape(SEQ, 3, GROUP, HEAD_DIM)
    scores = jnp.einsum("qhd,khd->hqk", heads[:, 0], heads[:, 1], preferred_element_type=F32)
    attention = jnp.exp(scores * HEAD_DIM ** (-0.5) - log_total)
    d_out = d_mixture.reshape(SEQ, GROUP, HEAD_DIM)
    d_values = jnp.einsum(
        "hqk,qhd->khd", attention.astype(BF16), d_out, preferred_element_type=F32
    )
    d_att = jnp.einsum("qhd,khd->hqk", d_out, heads[:, 2], preferred_element_type=F32)
    centre = jnp.sum(attention * d_att, axis=-1, keepdims=True)
    d_scores = (attention * (d_att - centre)).astype(BF16) * jnp.asarray(HEAD_DIM ** (-0.5), BF16)
    d_queries = jnp.einsum("hqk,khd->qhd", d_scores, heads[:, 1], preferred_element_type=F32)
    d_keys = jnp.einsum("hqk,qhd->khd", d_scores, heads[:, 0], preferred_element_type=F32)
    return jnp.stack([d_queries, d_keys, d_values], axis=1).reshape(SEQ, 576).astype(BF16)


def exchange_mixture(mixture):
    blocks = [mixture[ROWS * d : ROWS * (d + 1)] for d in range(N_SEQ)]
    return jnp.concatenate([blocks[0]] + [turn(blocks[d], d) for d in (1, 2, 3)], axis=1)


def selector_of(route_ids, me):
    relative = lax.rem(route_ids - me + N_SEQ, N_SEQ)
    experts = jnp.arange(N_SEQ, dtype=jnp.int32)
    named = (relative[:, 0:1] == experts) | (relative[:, 1:2] == experts)
    rank = jnp.cumsum(named.astype(jnp.int32), axis=0) - 1
    slots = jnp.arange(CAP, dtype=jnp.int32)
    chosen = named[:, :, None] & (rank[:, :, None] == slots)
    return chosen.reshape(ROWS, N_SEQ * CAP)


def two_parts(v):
    high = v.astype(BF16)
    return high, (v - high.astype(F32)).astype(BF16)


def middle(x, gathered, w_back, w_router, gain, route_ids, me):
    residual = x.astype(F32) + dot(gathered, w_back, 1, 0)
    n, inverse = norm_parts(residual)
    normed = (n * gain).astype(BF16)
    logits = dot(normed, w_router, 1, 0)
    gate_probs = jax.nn.softmax(logits, axis=-1)
    chosen = selector_of(route_ids, me)
    relative_gates = jnp.concatenate([gate_probs, gate_probs], axis=1)
    relative_gates = lax.dynamic_slice_in_dim(relative_gates, me, N_SEQ, 1)
    spread = jnp.broadcast_to(relative_gates[:, :, None], (ROWS, N_SEQ, CAP)).reshape(ROWS, -1)
    weights = two_parts(jnp.where(chosen, spread, 0.0))
    chosen = chosen.astype(BF16)
    buffer = dot(chosen, normed, 0, 0).astype(BF16)
    return residual, normed, gate_probs, chosen, weights, buffer


def send_out(buffer):
    blocks = [buffer[CAP * d : CAP * (d + 1)] for d in range(N_SEQ)]
    return jnp.concatenate([blocks[0]] + [turn(blocks[d], d) for d in (1, 2, 3)], axis=0)


def send_back(buffer):
    blocks = [buffer[CAP * d : CAP * (d + 1)] for d in range(N_SEQ)]
    return jnp.concatenate([blocks[0]] + [turn(blocks[d], -d) for d in (1, 2, 3)], axis=0)


def gelu_parts(h):
    cdf = 0.5 * (1.0 + lax.erf(h * 0.7071067811865476))
    return cdf


def expert_run(rows, packs):
    total = 0.0
    for pack in packs:
        for i in range(2):
            first = pack[:, 2 * i].reshape(D, 768)
            second = pack[:, 2 * i + 1].reshape(768, D)
            hidden = dot(rows, first, 1, 0)
            active = (hidden * gelu_parts(hidden)).astype(BF16)
            total = total + dot(active, second, 1, 0)
    return total.astype(BF16)


def expert_back(rows, d_result, packs):
    d_rows = 0.0
    grads = []
    for pack in packs:
        blocks = []
        for i in range(2):
            first = pack[:, 2 * i].reshape(D, 768)
            second = pack[:, 2 * i + 1].reshape(768, D)
            hidden = dot(rows, first, 1, 0)
            cdf = gelu_parts(hidden)
            active = (hidden * cdf).astype(BF16)
            slope = cdf + hidden * jnp.exp(-0.5 * hidden * hidden) * 0.3989422804014327
            d_active = dot(d_result, second, 1, 1)
            d_hidden = (d_active * slope).astype(BF16)
            d_rows = d_rows + dot(d_hidden, first, 1, 1)
            blocks.append(dot(rows, d_hidden, 0, 0).astype(BF16).reshape(N_SHARD, 48, 768))
            blocks.append(dot(active, d_result, 0, 0).astype(BF16).reshape(N_SHARD, 48, 768))
        grads.append(jnp.stack(blocks, axis=1))
    return d_rows.astype(BF16), grads


def combine(residual, weights, returned):
    return residual + dot(weights[0], returned, 1, 0) + dot(weights[1], returned, 1, 0)


def router_back(d_out, returned, chosen, gate_probs, me):
    products = jnp.where(chosen > 0, dot(d_out, returned, 1, 1), 0.0)
    d_gates = jnp.sum(products.reshape(ROWS, N_SEQ, CAP), axis=-1)
    d_gates = jnp.concatenate([d_gates, d_gates], axis=1)
    d_gates = lax.dynamic_slice_in_dim(d_gates, lax.rem(N_SEQ - me, N_SEQ), N_SEQ, 1)
    return gate_probs * (d_gates - jnp.sum(gate_probs * d_gates, axis=-1, keepdims=True))


def middle_back(d_out, d_returned, chosen, d_logits, w_router, residual, normed, gain, gathered, w_back):
    d_normed = dot(chosen, d_returned, 1, 0)
    for e in range(4):
        d_normed = d_normed + d_logits[:, e : e + 1] * w_router[:, e].astype(F32)[None, :]
    n, inverse = norm_parts(residual)
    d_residual = d_out.astype(F32) + norm_back(n, inverse, gain, d_normed)
    grad_gain = jnp.sum(d_normed * n, axis=0)
    high, low = two_parts(d_logits)
    grad_router = dot(normed, high, 0, 0) + dot(normed, low, 0, 0)
    d_branch = d_residual.astype(BF16)
    grad_back = dot(gathered, d_branch, 0, 0)
    d_mixture = dot(d_branch, w_back, 1, 1).astype(BF16)
    return d_residual, grad_gain, grad_router, grad_back, d_mixture


def exchange_d_mixture(d_mixture):
    blocks = [d_mixture[:, 192 * d : 192 * (d + 1)] for d in range(N_SEQ)]
    return jnp.concatenate([blocks[0]] + [turn(blocks[d], -d) for d in (1, 2, 3)], axis=0)


def attention_weights(w_qkv, w_proj, w_route, gain_attn, gain_ffn):
    mine = w_qkv.reshape(12, 3, N_SEQ, 192).transpose(2, 0, 1, 3).reshape(N_SEQ, 12, 576)
    small = jnp.concatenate(
        [w_route, gain_attn[:, None], gain_ffn[:, None], jnp.zeros((12, 122), BF16)], axis=1
    )
    mine = jnp.concatenate([mine, jnp.broadcast_to(small, (N_SEQ, 12, 128))], axis=2)
    arrived = lax.all_to_all(mine, "seq", 0, 0, tiled=True)
    back = w_proj.reshape(12, N_SEQ, 192).transpose(1, 0, 2)
    pack = jnp.concatenate([arrived[:, :, :576], back, arrived[:, :, 576:]], axis=2)
    whole = gather_shard(pack)
    other = swap(whole)
    core = lax.axis_index("section")
    layers = []
    for s in range(2):
        both = jnp.where(core == s, whole, other)
        rows = both.swapaxes(0, 1).reshape(D, WIDE)
        back_rows = both[:, :, :, 576:768].transpose(0, 2, 1, 3).reshape(192, D)
        layers.append((rows, back_rows))
    out = []
    for rows, back_rows in layers:
        w_back = jnp.concatenate([back_rows] + [turn(back_rows, d) for d in (1, 2, 3)], axis=0)
        out.append(
            (
                rows[:, :576],
                w_back,
                rows[:, 768:772],
                rows[:, 772].astype(F32),
                rows[:, 773].astype(F32),
            )
        )
    return out


def expert_weights(w_in, w_out):
    core = lax.axis_index("section")
    first = w_in.reshape(48, N_SHARD, 4, 48).transpose(2, 0, 1, 3).reshape(4, 48, 768)
    second = w_out.reshape(4, 48, 768)
    quarters = jnp.stack([first, second], axis=1).reshape(2, 4, 48, 768)
    mine = pick(quarters, core)
    arrived = swap(pick(quarters, 1 - core))
    out = []
    for s in range(2):
        own = jnp.where(core == s, mine, arrived)
        whole = lax.all_gather(own, "shard", axis=0, tiled=False)
        out.append((whole, swap(whole)))
    return out


def finish_experts(grads):
    own, other = grads
    total = (own.astype(F32) + swap(other).astype(F32)).astype(BF16)
    return scatter_shard(total.reshape(N_SHARD, 2, 2, 48, 768))


def finish_attention(grad_mix, small, grad_back):
    core = lax.axis_index("section")
    blocks = [grad_back[192 * d : 192 * (d + 1)] for d in range(N_SEQ)]
    back = blocks[0]
    for d in (1, 2, 3):
        back = back + turn(blocks[d].astype(BF16), -d).astype(F32)
    back = back.reshape(N_SHARD, 12, N_SEQ, 192).transpose(2, 0, 1, 3)
    rows = jnp.concatenate([grad_mix, small], axis=1).reshape(N_SEQ, N_SHARD, 12, 704)
    pack = jnp.concatenate([rows, back], axis=3).astype(BF16)
    pack = pack.reshape(2, 2, N_SHARD, 12, WIDE)
    total = pick(pack, core).astype(F32) + swap(pick(pack, 1 - core)).astype(F32)
    total = total.astype(BF16).transpose(1, 0, 2, 3)
    return scatter_shard(total)


def shards(images_in, out_grad, routes, w_qkv, w_proj, w_route, gain_attn, gain_ffn, w_in, w_out):
    core = lax.axis_index("section")
    me = lax.axis_index("seq")
    own_routes = routes[0, :, 0]
    mine = pick(own_routes, core)
    arrived = swap(pick(own_routes, 1 - core))
    route_of = (jnp.where(core == 0, mine, arrived), jnp.where(core == 0, arrived, mine))
    x0 = pick(images_in, core)[0]
    d_last = pick(out_grad, core)[0]
    attn = attention_weights(w_qkv[0], w_proj[0], w_route[0], gain_attn[0], gain_ffn[0])
    experts = expert_weights(w_in[0, 0], w_out[0, 0])

    saved = []
    x = x0
    layer_outs = []
    for s in range(2):
        w_mix, w_back, w_router, gain_one, gain_two = attn[s]
        x_all = gather_tokens(x)
        mixture, normed_one, packed, log_total = attend(x_all, w_mix, gain_one)
        gathered = exchange_mixture(mixture)
        residual, normed_two, gates, chosen, weights, buffer = middle(
            x, gathered, w_back, w_router, gain_two, route_of[s], me
        )
        rows = send_out(buffer)
        result = expert_run(rows, experts[s])
        returned = send_back(result)
        output = combine(residual, weights, returned).astype(BF16)
        saved.append(
            (x, normed_one, packed, log_total, gathered, residual, normed_two, gates, chosen, weights, rows, returned)
        )
        layer_outs.append(output)
        x = output

    d_out = d_last
    in_grads = [None, None]
    finished = [None, None]
    for s in (1, 0):
        w_mix, w_back, w_router, gain_one, gain_two = attn[s]
        (x, normed_one, packed, log_total, gathered, residual, normed_two, gates, chosen, weights, rows, returned) = saved[s]
        d_buffer = (dot(weights[0], d_out, 0, 0) + dot(weights[1], d_out, 0, 0)).astype(BF16)
        d_result = send_out(d_buffer)
        d_rows, expert_grads = expert_back(rows, d_result, experts[s])
        d_returned = send_back(d_rows)
        d_logits = router_back(d_out, returned, chosen, gates, me)
        d_residual, grad_gain_two, grad_router, grad_back, d_mixture = middle_back(
            d_out, d_returned, chosen, d_logits, w_router, residual, normed_two, gain_two, gathered, w_back
        )
        expert_total = finish_experts(expert_grads)
        d_heads = exchange_d_mixture(d_mixture)
        d_packed = attend_back(packed, log_total, d_heads)
        d_normed_all = dot(d_packed, w_mix, 1, 1)
        d_normed = d_normed_all[:ROWS]
        for d in (1, 2, 3):
            d_normed = d_normed + turn(d_normed_all[ROWS * d : ROWS * (d + 1)].astype(BF16), d).astype(F32)
        grad_mix = dot(normed_one, d_packed, 0, 0)
        n, inverse = norm_parts(x.astype(F32))
        d_out = (d_residual + norm_back(n, inverse, gain_one, d_normed)).astype(BF16)
        grad_gain_one = jnp.sum(d_normed * n, axis=0)
        small = jnp.concatenate(
            [grad_router, grad_gain_one[:, None], grad_gain_two[:, None], jnp.zeros((D, 122), F32)], axis=1
        )
        attn_total = finish_attention(grad_mix, small, grad_back)
        in_grads[s] = d_out
        finished[s] = (expert_total, attn_total)

    def settle(pair):
        keep = jnp.where(core == 0, pair[0], pair[1])
        give = jnp.where(core == 0, pair[1], pair[0])
        return keep, swap(give)

    def in_order(keep, got):
        return jnp.where(core == 0, jnp.stack([keep, got]), jnp.stack([got, keep]))

    layer_out = in_order(*settle(layer_outs))
    in_grad = in_order(*settle(in_grads))
    expert_sum = in_order(*settle([finished[s][0] for s in range(2)]))
    attn_sum = in_order(*settle([finished[s][1] for s in range(2)]))
    quarters = expert_sum.reshape(4, 2, 48, 768)
    grad_in = quarters[:, 0].reshape(4, 48, N_SHARD, 48).transpose(1, 2, 0, 3).reshape(48, FF)
    grad_out = quarters[:, 1].reshape(192, D)
    attn_sum = attn_sum.reshape(N_SEQ, 12, WIDE)
    back = attn_sum[:, :, 704:].transpose(1, 0, 2).reshape(12, D)
    mix = lax.all_to_all(attn_sum[:, :, :704].astype(BF16), "seq", 0, 0, tiled=True).astype(F32)
    grad_qkv = mix[:, :, :576].reshape(N_SEQ, 12, 3, 192).transpose(1, 2, 0, 3).reshape(12, 3 * D)
    small = jnp.sum(mix[:, :, 576:], axis=0)
    return (
        layer_out[None, :, None],
        in_grad[None, :, None],
        grad_qkv[None],
        back[None],
        small[None, :, 0:4],
        small[None, :, 4],
        small[None, :, 5],
        grad_in[None],
        grad_out[None],
    )


def solution(mesh):
    def run(*args):
        outs = shards(*args)
        outs = list(outs)
        outs[7] = outs[7][:, None]
        outs[8] = outs[8][:, None]
        return tuple(outs)

    return jax.shard_map(
        run,
        mesh=mesh,
        in_specs=(
            P(None, "shard", "seq", None),
            P(None, "shard", "seq", None),
            P("section", None, "shard", "seq", None),
            P("section", ("seq", "shard"), None),
            P("section", ("seq", "shard"), None),
            P("section", ("seq", "shard"), None),
            P("section", ("seq", "shard")),
            P("section", ("seq", "shard")),
            P("section", "seq", "shard", None),
            P("section", "seq", "shard", None),
        ),
        out_specs=(
            P("section", None, "shard", "seq", None),
            P("section", None, "shard", "seq", None),
            P("section", ("seq", "shard"), None),
            P("section", ("seq", "shard"), None),
            P("section", ("seq", "shard"), None),
            P("section", ("seq", "shard")),
            P("section", ("seq", "shard")),
            P("section", "seq", "shard", None),
            P("section", "seq", "shard", None),
        ),
        check_vma=False,
    )
```

```python
from functools import partial

import jax
import jax.numpy as jnp
from jax import lax
from jax.sharding import PartitionSpec as P

D = 768
FF = 3072
HEAD_DIM = 64
CAP = 80
N_SEQ = 4
N_SHARD = 16
GROUP = 3
ROWS = 144
SEQ = 576
WIDE = 896
EPSILON = 1e-06
F32 = jnp.float32
BF16 = jnp.bfloat16


def dot(a, b, ca, cb):
    return lax.dot_general(a, b, (((ca,), (cb,)), ((), ())), preferred_element_type=F32)


def swap(v):
    return lax.ppermute(v, "section", [(0, 1), (1, 0)])


def turn(v, d):
    return lax.ppermute(v, "seq", [(i, (i + d) % N_SEQ) for i in range(N_SEQ)])


def hop(v, axis, d):
    route = []
    for z in range(4):
        for x in range(4):
            to = ((z + d) % 4) * 4 + x if axis == "z" else z * 4 + (x + d) % 4
            route.append((z * 4 + x, to))
    return lax.ppermute(v, "shard", route)


def place(axis):
    i = lax.axis_index("shard")
    return i // 4 if axis == "z" else lax.rem(i, 4)


def pick(v, i):
    return lax.dynamic_index_in_dim(v, i, 0, keepdims=False)


def tie(value, other):
    return lax.optimization_barrier((value, other))[0]


def norm_parts(values):
    centred = values - jnp.mean(values, axis=-1, keepdims=True)
    inverse = lax.rsqrt(jnp.mean(centred * centred, axis=-1, keepdims=True) + EPSILON)
    return centred * inverse, inverse


def norm_back(n, inverse, gain, dy):
    gdy = dy * gain
    return (
        gdy
        - jnp.mean(gdy, axis=-1, keepdims=True)
        - n * jnp.mean(gdy * n, axis=-1, keepdims=True)
    ) * inverse


def gather_tokens(x):
    return jnp.concatenate([x] + [turn(x, -d) for d in (1, 2, 3)], axis=0)


def attend(x_all, w_mix, gain):
    normed = (norm_parts(x_all.astype(F32))[0] * gain).astype(BF16)
    packed = dot(normed, w_mix, 1, 0).astype(BF16)
    heads = packed.reshape(SEQ, 3, GROUP, HEAD_DIM)
    scores = jnp.einsum("qhd,khd->hqk", heads[:, 0], heads[:, 1], preferred_element_type=F32)
    scores = scores * HEAD_DIM ** (-0.5)
    top = jnp.max(scores, axis=-1, keepdims=True)
    exponent = jnp.exp(scores - top)
    totals = jnp.sum(exponent, axis=-1, keepdims=True)
    attention = (exponent / totals).astype(BF16)
    mixture = jnp.einsum("hqk,khd->qhd", attention, heads[:, 2], preferred_element_type=F32)
    return mixture.astype(BF16).reshape(SEQ, GROUP * HEAD_DIM), normed, packed, top + jnp.log(totals)


def attend_back(packed, log_total, d_mixture):
    heads = packed.reshape(SEQ, 3, GROUP, HEAD_DIM)
    scores = jnp.einsum("qhd,khd->hqk", heads[:, 0], heads[:, 1], preferred_element_type=F32)
    attention = jnp.exp(scores * HEAD_DIM ** (-0.5) - log_total)
    d_out = d_mixture.reshape(SEQ, GROUP, HEAD_DIM)
    d_values = jnp.einsum(
        "hqk,qhd->khd", attention.astype(BF16), d_out, preferred_element_type=F32
    )
    d_att = jnp.einsum("qhd,khd->hqk", d_out, heads[:, 2], preferred_element_type=F32)
    centre = jnp.sum(attention * d_att, axis=-1, keepdims=True)
    d_scores = (attention * (d_att - centre)).astype(BF16) * jnp.asarray(HEAD_DIM ** (-0.5), BF16)
    d_queries = jnp.einsum("hqk,khd->qhd", d_scores, heads[:, 1], preferred_element_type=F32)
    d_keys = jnp.einsum("hqk,qhd->khd", d_scores, heads[:, 0], preferred_element_type=F32)
    return jnp.stack([d_queries, d_keys, d_values], axis=1).reshape(SEQ, 576).astype(BF16)


def exchange_mixture(mixture):
    blocks = [mixture[ROWS * d : ROWS * (d + 1)] for d in range(N_SEQ)]
    return jnp.concatenate([blocks[0]] + [turn(blocks[d], d) for d in (1, 2, 3)], axis=1)


def selector_of(route_ids, me):
    relative = lax.rem(route_ids - me + N_SEQ, N_SEQ)
    experts = jnp.arange(N_SEQ, dtype=jnp.int32)
    named = (relative[:, 0:1] == experts) | (relative[:, 1:2] == experts)
    rank = jnp.cumsum(named.astype(jnp.int32), axis=0) - 1
    slots = jnp.arange(CAP, dtype=jnp.int32)
    chosen = named[:, :, None] & (rank[:, :, None] == slots)
    return chosen.reshape(ROWS, N_SEQ * CAP)


def two_parts(v):
    high = v.astype(BF16)
    return high, (v - high.astype(F32)).astype(BF16)


def middle(x, gathered, w_back, w_router, gain, route_ids, me):
    residual = x.astype(F32) + dot(gathered, w_back, 1, 0)
    n, inverse = norm_parts(residual)
    normed = (n * gain).astype(BF16)
    logits = dot(normed, w_router, 1, 0)
    gate_probs = jax.nn.softmax(logits, axis=-1)
    chosen = selector_of(route_ids, me)
    relative_gates = jnp.concatenate([gate_probs, gate_probs], axis=1)
    relative_gates = lax.dynamic_slice_in_dim(relative_gates, me, N_SEQ, 1)
    spread = jnp.broadcast_to(relative_gates[:, :, None], (ROWS, N_SEQ, CAP)).reshape(ROWS, -1)
    weights = two_parts(jnp.where(chosen, spread, 0.0))
    chosen = chosen.astype(BF16)
    buffer = dot(chosen, normed, 0, 0).astype(BF16)
    return residual, normed, gate_probs, chosen, weights, buffer


def send_out(buffer, height=CAP):
    blocks = [buffer[height * d : height * (d + 1)] for d in range(N_SEQ)]
    return jnp.concatenate([blocks[0]] + [turn(blocks[d], d) for d in (1, 2, 3)], axis=0)


def send_back(buffer, height=CAP):
    blocks = [buffer[height * d : height * (d + 1)] for d in range(N_SEQ)]
    return jnp.concatenate([blocks[0]] + [turn(blocks[d], -d) for d in (1, 2, 3)], axis=0)


def gelu_parts(h):
    cdf = 0.5 * (1.0 + lax.erf(h * 0.7071067811865476))
    return cdf


def expert_run(rows, packs):
    total = 0.0
    for pack in packs:
        for i in range(2):
            first = pack[:, 2 * i].reshape(D, 768)
            second = pack[:, 2 * i + 1].reshape(768, D)
            hidden = dot(rows, first, 1, 0)
            active = (hidden * gelu_parts(hidden)).astype(BF16)
            total = total + dot(active, second, 1, 0)
    return total.astype(BF16)


def expert_back(rows, d_result, packs, forward):
    d_rows = 0.0
    result = 0.0
    grads = []
    for pack in packs:
        blocks = []
        for i in range(2):
            first = pack[:, 2 * i].reshape(D, 768)
            second = pack[:, 2 * i + 1].reshape(768, D)
            hidden = dot(rows, first, 1, 0)
            cdf = gelu_parts(hidden)
            active = (hidden * cdf).astype(BF16)
            slope = cdf + hidden * jnp.exp(-0.5 * hidden * hidden) * 0.3989422804014327
            if forward:
                result = result + dot(active, second, 1, 0)
            d_active = dot(d_result, second, 1, 1)
            d_hidden = (d_active * slope).astype(BF16)
            d_rows = d_rows + dot(d_hidden, first, 1, 1)
            blocks.append(dot(rows, d_hidden, 0, 0).astype(BF16).reshape(N_SHARD, 48, 768))
            blocks.append(dot(active, d_result, 0, 0).astype(BF16).reshape(N_SHARD, 48, 768))
        grads.append(jnp.stack(blocks, axis=1))
    if forward:
        return result.astype(BF16), d_rows.astype(BF16), grads
    return d_rows.astype(BF16), grads


def combine(residual, weights, returned):
    return residual + dot(weights[0], returned, 1, 0) + dot(weights[1], returned, 1, 0)


def router_back(d_out, returned, chosen, gate_probs, me):
    products = jnp.where(chosen > 0, dot(d_out, returned, 1, 1), 0.0)
    d_gates = jnp.sum(products.reshape(ROWS, N_SEQ, CAP), axis=-1)
    d_gates = jnp.concatenate([d_gates, d_gates], axis=1)
    d_gates = lax.dynamic_slice_in_dim(d_gates, lax.rem(N_SEQ - me, N_SEQ), N_SEQ, 1)
    return gate_probs * (d_gates - jnp.sum(gate_probs * d_gates, axis=-1, keepdims=True))


def middle_back(d_out, d_returned, chosen, d_logits, w_router, residual, normed, gain, gathered, w_back):
    d_normed = dot(chosen, d_returned, 1, 0)
    for e in range(4):
        d_normed = d_normed + d_logits[:, e : e + 1] * w_router[:, e].astype(F32)[None, :]
    n, inverse = norm_parts(residual)
    d_residual = d_out.astype(F32) + norm_back(n, inverse, gain, d_normed)
    grad_gain = jnp.sum(d_normed * n, axis=0)
    high, low = two_parts(d_logits)
    grad_router = dot(normed, high, 0, 0) + dot(normed, low, 0, 0)
    d_branch = d_residual.astype(BF16)
    grad_back = dot(gathered, d_branch, 0, 0)
    d_mixture = dot(d_branch, w_back, 1, 1).astype(BF16)
    return d_residual, grad_gain, grad_router, grad_back, d_mixture


def exchange_d_mixture(d_mixture):
    blocks = [d_mixture[:, 192 * d : 192 * (d + 1)] for d in range(N_SEQ)]
    return jnp.concatenate([blocks[0]] + [turn(blocks[d], -d) for d in (1, 2, 3)], axis=0)


def attention_weights(w_qkv, w_proj, w_route, gain_attn, gain_ffn):
    core = lax.axis_index("section")
    mine = w_qkv.reshape(12, 3, N_SEQ, 192).transpose(2, 0, 1, 3).reshape(N_SEQ, 12, 576)
    small = jnp.concatenate(
        [w_route, gain_attn[:, None], gain_ffn[:, None], jnp.zeros((12, 58), BF16)], axis=1
    )
    mine = jnp.concatenate([mine, jnp.broadcast_to(small, (N_SEQ, 12, 64))], axis=2)
    spread = jnp.broadcast_to(mine[:, None], (N_SEQ, N_SHARD, 12, 640))
    spread = spread.reshape(N_SEQ * N_SHARD, 12, 640)
    whole = lax.all_to_all(spread, ("seq", "shard"), 0, 0, tiled=True).reshape(D, 640)
    other = swap(whole)
    spread = jnp.broadcast_to(w_proj[None], (N_SHARD, 12, D))
    back_rows = lax.all_to_all(spread, "shard", 0, 0, tiled=True).reshape(192, D)
    w_back = jnp.concatenate([back_rows] + [turn(back_rows, d) for d in (1, 2, 3)], axis=0)
    other_back = swap(w_back)
    out = []
    for s in range(2):
        rows = jnp.where(core == s, whole, other)
        out.append(
            (
                rows[:, :576],
                jnp.where(core == s, w_back, other_back),
                rows[:, 576:580],
                rows[:, 580].astype(F32),
                rows[:, 581].astype(F32),
            )
        )
    return out


def expert_weights(w_in, w_out):
    core = lax.axis_index("section")
    first = w_in.reshape(48, N_SHARD, 4, 48).transpose(2, 0, 1, 3).reshape(4, 48, 768)
    second = w_out.reshape(4, 48, 768)
    quarters = jnp.stack([first, second], axis=1).reshape(2, 4, 48, 768)
    mine = pick(quarters, core)
    arrived = swap(pick(quarters, 1 - core))
    out = []
    for s in range(2):
        own = jnp.where(core == s, mine, arrived)
        whole = lax.all_gather(own, "shard", axis=0, tiled=False)
        out.append((whole, swap(whole)))
    return out


def join_experts(grads):
    own, other = grads
    return (own.astype(F32) + swap(other).astype(F32)).astype(BF16)


def scatter_now(v):
    arrived = lax.all_to_all(v, "shard", 0, 0, tiled=True)
    return jnp.sum(arrived.astype(F32), axis=0)


def scatter_beside(v):
    return lax.psum_scatter(v, "shard", scatter_dimension=0, tiled=True)[0].astype(F32)


def join_attention(grad_mix, small, grad_back, me):
    core = lax.axis_index("section")
    mix = jnp.concatenate([grad_mix, small], axis=1).astype(BF16)
    twice = jnp.concatenate([grad_back, grad_back], axis=0).astype(BF16)
    turned = [
        lax.dynamic_slice_in_dim(twice, 192 * lax.rem(me - g + N_SEQ, N_SEQ), 192, 0)
        for g in range(N_SEQ)
    ]
    back = jnp.concatenate(turned, axis=0)
    keep = jnp.where(core == 0, mix, back)
    give = jnp.where(core == 0, back, mix)
    return (keep.astype(F32) + swap(give).astype(F32)).astype(BF16)


def scatter_attention(total):
    arrived = lax.all_to_all(
        total.reshape(N_SEQ * N_SHARD, 12, D), ("seq", "shard"), 0, 0, tiled=True
    )
    return jnp.sum(arrived.reshape(N_SEQ, N_SHARD, 12, D).astype(F32), axis=1)


def shards(images_in, out_grad, routes, w_qkv, w_proj, w_route, gain_attn, gain_ffn, w_in, w_out):
    core = lax.axis_index("section")
    me = lax.axis_index("seq")
    own_routes = routes[0, :, 0]
    mine = pick(own_routes, core)
    arrived = swap(pick(own_routes, 1 - core))
    route_of = (jnp.where(core == 0, mine, arrived), jnp.where(core == 0, arrived, mine))
    x0 = pick(images_in, core)[0]
    d_last = pick(out_grad, core)[0]
    attn = attention_weights(w_qkv[0], w_proj[0], w_route[0], gain_attn[0], gain_ffn[0])
    experts = expert_weights(w_in[0, 0], w_out[0, 0])

    saved = []
    x = x0
    layer_outs = []
    for s in range(2):
        w_mix, w_back, w_router, gain_one, gain_two = attn[s]
        x_all = gather_tokens(x)
        mixture, normed_one, packed, log_total = attend(x_all, w_mix, gain_one)
        gathered = exchange_mixture(mixture)
        residual, normed_two, gates, chosen, weights, buffer = middle(
            x, gathered, w_back, w_router, gain_two, route_of[s], me
        )
        kept = (x, normed_one, packed, log_total, gathered, residual, normed_two, gates, chosen, weights)
        if s == 0:
            rows = send_out(buffer)
            result = expert_run(rows, experts[s])
            returned = send_back(result)
            x = combine(residual, weights, returned).astype(BF16)
            layer_outs.append(x)
            saved.append(kept + (rows, returned))
        else:
            saved.append(kept + (buffer,))

    d_out = d_last
    in_grads = [None, None]
    expert_sums = [None, None]
    attn_sums = [None, None]
    for s in (1, 0):
        w_mix, w_back, w_router, gain_one, gain_two = attn[s]
        (x, normed_one, packed, log_total, gathered, residual, normed_two, gates, chosen, weights) = saved[s][:10]
        d_buffer = (dot(weights[0], d_out, 0, 0) + dot(weights[1], d_out, 0, 0)).astype(BF16)
        if s == 1:
            both = jnp.stack([saved[s][10].reshape(4, CAP, D), d_buffer.reshape(4, CAP, D)], axis=1)
            both = send_out(both.reshape(8 * CAP, D), 2 * CAP).reshape(4, 2, CAP, D)
            rows = both[:, 0].reshape(4 * CAP, D)
            d_result = both[:, 1].reshape(4 * CAP, D)
            result, d_rows, expert_grads = expert_back(rows, d_result, experts[s], True)
            both = jnp.stack([result.reshape(4, CAP, D), d_rows.reshape(4, CAP, D)], axis=1)
            both = send_back(both.reshape(8 * CAP, D), 2 * CAP).reshape(4, 2, CAP, D)
            returned = both[:, 0].reshape(4 * CAP, D)
            d_returned = both[:, 1].reshape(4 * CAP, D)
            layer_outs.append(combine(residual, weights, returned).astype(BF16))
        else:
            rows, returned = saved[s][10:]
            d_result = send_out(d_buffer)
            d_rows, expert_grads = expert_back(rows, d_result, experts[s], False)
            d_returned = send_back(d_rows)
        joined = join_experts(expert_grads)
        if s == 1:
            expert_sums[s] = scatter_beside(joined)
        else:
            expert_sums[s] = scatter_now(joined)
        d_logits = router_back(d_out, returned, chosen, gates, me)
        d_residual, grad_gain_two, grad_router, grad_back, d_mixture = middle_back(
            d_out, d_returned, chosen, d_logits, w_router, residual, normed_two, gain_two, gathered, w_back
        )
        d_heads = exchange_d_mixture(d_mixture)
        if s == 0:
            d_heads, expert_sums[1], attn_sums[1] = lax.optimization_barrier(
                (d_heads, expert_sums[1], attn_sums[1])
            )
        d_packed = attend_back(packed, log_total, d_heads)
        d_normed_all = dot(d_packed, w_mix, 1, 1)
        d_normed = d_normed_all[:ROWS]
        for d in (1, 2, 3):
            d_normed = d_normed + turn(d_normed_all[ROWS * d : ROWS * (d + 1)].astype(BF16), d).astype(F32)
        grad_mix = dot(normed_one, d_packed, 0, 0)
        n, inverse = norm_parts(x.astype(F32))
        d_out = (d_residual + norm_back(n, inverse, gain_one, d_normed)).astype(BF16)
        grad_gain_one = jnp.sum(d_normed * n, axis=0)
        small = jnp.concatenate(
            [grad_router, grad_gain_one[:, None], grad_gain_two[:, None], jnp.zeros((D, 186), F32)], axis=1
        )
        attn_sums[s] = scatter_attention(join_attention(grad_mix, small, grad_back, me))
        in_grads[s] = d_out

    def settle(pair):
        keep = jnp.where(core == 0, pair[0], pair[1])
        give = jnp.where(core == 0, pair[1], pair[0])
        return keep, swap(give)

    def in_order(keep, got):
        return jnp.where(core == 0, jnp.stack([keep, got]), jnp.stack([got, keep]))

    layer_out = in_order(*settle(layer_outs))
    in_grad = in_order(*settle(in_grads))
    expert_sum = in_order(*settle(expert_sums))
    attn_sum = in_order(*settle(attn_sums))
    quarters = expert_sum.reshape(4, 2, 48, 768)
    grad_in = quarters[:, 0].reshape(4, 48, N_SHARD, 48).transpose(1, 2, 0, 3).reshape(48, FF)
    grad_out = quarters[:, 1].reshape(192, D)
    mix = attn_sum[0]
    back = jnp.sum(attn_sum[1], axis=0)
    grad_qkv = mix[:, :, :576].reshape(N_SEQ, 12, 3, 192).transpose(1, 2, 0, 3).reshape(12, 3 * D)
    small = jnp.sum(mix[:, :, 576:], axis=0)
    return (
        layer_out[None, :, None],
        in_grad[None, :, None],
        grad_qkv[None],
        back[None],
        small[None, :, 0:4],
        small[None, :, 4],
        small[None, :, 5],
        grad_in[None],
        grad_out[None],
    )


def solution(mesh):
    def run(*args):
        outs = shards(*args)
        outs = list(outs)
        outs[7] = outs[7][:, None]
        outs[8] = outs[8][:, None]
        return tuple(outs)

    return jax.shard_map(
        run,
        mesh=mesh,
        in_specs=(
            P(None, "shard", "seq", None),
            P(None, "shard", "seq", None),
            P("section", None, "shard", "seq", None),
            P("section", ("seq", "shard"), None),
            P("section", ("seq", "shard"), None),
            P("section", ("seq", "shard"), None),
            P("section", ("seq", "shard")),
            P("section", ("seq", "shard")),
            P("section", "seq", "shard", None),
            P("section", "seq", "shard", None),
        ),
        out_specs=(
            P("section", None, "shard", "seq", None),
            P("section", None, "shard", "seq", None),
            P("section", ("seq", "shard"), None),
            P("section", ("seq", "shard"), None),
            P("section", ("seq", "shard"), None),
            P("section", ("seq", "shard")),
            P("section", ("seq", "shard")),
            P("section", "seq", "shard", None),
            P("section", "seq", "shard", None),
        ),
        check_vma=False,
    )
```

```python
import math
from functools import partial

import jax
import jax.numpy as jnp
from jax import lax
from jax.experimental import pallas as pl
from jax.experimental.pallas import tpu as pltpu
from jax.sharding import PartitionSpec as P

D = 768
FF = 3072
HEAD_DIM = 64
CAP = 80
N_SEQ = 4
N_SHARD = 16
GROUP = 3
ROWS = 144
SEQ = 576
WIDE = 1472
LIMIT = 56 * 1024 * 1024
EPSILON = 1e-06
F32 = jnp.float32
BF16 = jnp.bfloat16


def dot(a, b, ca, cb):
    return lax.dot_general(a, b, (((ca,), (cb,)), ((), ())), preferred_element_type=F32)


def swap(v):
    return lax.ppermute(v, "section", [(0, 1), (1, 0)])


def turn(v, d):
    return lax.ppermute(v, "seq", [(i, (i + d) % N_SEQ) for i in range(N_SEQ)])


def hop(v, axis, d):
    route = []
    for z in range(4):
        for x in range(4):
            to = ((z + d) % 4) * 4 + x if axis == "z" else z * 4 + (x + d) % 4
            route.append((z * 4 + x, to))
    return lax.ppermute(v, "shard", route)


def place(axis):
    i = lax.axis_index("shard")
    return i // 4 if axis == "z" else lax.rem(i, 4)


def pick(v, i):
    return lax.dynamic_index_in_dim(v, i, 0, keepdims=False)


def tie(value, other):
    return lax.optimization_barrier((value, other))[0]


def norm_parts(values):
    centred = values - jnp.mean(values, axis=-1, keepdims=True)
    inverse = lax.rsqrt(jnp.mean(centred * centred, axis=-1, keepdims=True) + EPSILON)
    return centred * inverse, inverse


def norm_back(n, inverse, gain, dy):
    gdy = dy * gain
    return (
        gdy
        - jnp.mean(gdy, axis=-1, keepdims=True)
        - n * jnp.mean(gdy * n, axis=-1, keepdims=True)
    ) * inverse


def two_parts(v):
    high = v.astype(BF16)
    return high, (v - high.astype(F32)).astype(BF16)


def gather_tokens(x):
    return jnp.concatenate([x] + [turn(x, -d) for d in (1, 2, 3)], axis=0)


def send_out(blocks):
    return [blocks[0]] + [turn(blocks[d], d) for d in (1, 2, 3)]


def send_back(blocks):
    return [blocks[0]] + [turn(blocks[d], -d) for d in (1, 2, 3)]


def vmem():
    return pl.BlockSpec(memory_space=pltpu.VMEM)


def smem():
    return pl.BlockSpec(memory_space=pltpu.SMEM)


def shape(dims, kind):
    return jax.ShapeDtypeStruct(dims, kind)


def call(body, outs, ins, name, flops, scalars=0, scratch=()):
    specs = [smem()] * scalars + [vmem()] * (len(ins) - scalars)
    moved = sum(math.prod(v.shape) * v.dtype.itemsize for v in list(ins) + list(outs))
    return pl.pallas_call(
        body,
        out_shape=outs,
        in_specs=specs,
        out_specs=[vmem()] * len(outs),
        scratch_shapes=list(scratch),
        name=name,
        cost_estimate=pl.CostEstimate(flops=int(flops), bytes_accessed=moved, transcendentals=0),
        compiler_params=pltpu.CompilerParams(vmem_limit_bytes=LIMIT),
    )(*ins)


def attend_kernel(x_ref, w_ref, gain_ref, mix_ref, packed_ref, log_ref):
    n, _ = norm_parts(x_ref[...].astype(F32))
    normed = (n * gain_ref[4:5, :]).astype(BF16)
    packed_ref[...] = dot(normed, w_ref[...], 1, 0).astype(BF16)
    lane = lax.broadcasted_iota(jnp.int32, (SEQ, 128), 1)
    logs = jnp.zeros((SEQ, 128), F32)
    outs = []
    for h in range(GROUP):
        query = packed_ref[:, 64 * h : 64 * h + 64]
        key = packed_ref[:, 192 + 64 * h : 256 + 64 * h]
        value = packed_ref[:, 384 + 64 * h : 448 + 64 * h]
        scores = dot(query, key, 1, 1) * HEAD_DIM ** (-0.5)
        top = jnp.max(scores, axis=1, keepdims=True)
        exponent = jnp.exp(scores - top)
        total = jnp.sum(exponent, axis=1, keepdims=True)
        outs.append((dot(exponent.astype(BF16), value, 1, 0) / total).astype(BF16))
        logs = jnp.where(lane == h, top + jnp.log(total), logs)
    log_ref[...] = logs
    mixture = jnp.concatenate(outs, axis=1)
    for d in range(N_SEQ):
        mix_ref[d] = mixture[ROWS * d : ROWS * (d + 1)]


def attend(x_all, w_mix, gains):
    return call(
        attend_kernel,
        [shape((N_SEQ, ROWS, 192), BF16), shape((SEQ, 576), BF16), shape((SEQ, 128), F32)],
        [x_all, w_mix, gains],
        "attention",
        2 * SEQ * D * 576 + 3 * 4 * SEQ * SEQ * 64,
    )


def attend_back_kernel(
    x_ref, w_ref, gain_ref, packed_ref, log_ref, d0, d1, d2, d3, small_ref,
    d_normed_ref, grad_ref, d_packed_ref, d_mix_ref,
):
    for d, ref in enumerate((d0, d1, d2, d3)):
        d_mix_ref[ROWS * d : ROWS * (d + 1)] = ref[...]
    scaling = HEAD_DIM ** (-0.5)
    parts = [[], [], []]
    for h in range(GROUP):
        query = packed_ref[:, 64 * h : 64 * h + 64]
        key = packed_ref[:, 192 + 64 * h : 256 + 64 * h]
        value = packed_ref[:, 384 + 64 * h : 448 + 64 * h]
        d_out = d_mix_ref[:, 64 * h : 64 * h + 64]
        attention = jnp.exp(dot(query, key, 1, 1) * scaling - log_ref[:, h : h + 1])
        parts[2].append(dot(attention.astype(BF16), d_out, 0, 0).astype(BF16))
        d_att = dot(d_out, value, 1, 1)
        centre = jnp.sum(attention * d_att, axis=1, keepdims=True)
        d_scores = (attention * (d_att - centre) * scaling).astype(BF16)
        parts[0].append(dot(d_scores, key, 1, 0).astype(BF16))
        parts[1].append(dot(d_scores, query, 0, 0).astype(BF16))
    d_packed_ref[...] = jnp.concatenate(parts[0] + parts[1] + parts[2], axis=1)
    n, _ = norm_parts(x_ref[...].astype(F32))
    normed = (n * gain_ref[4:5, :]).astype(BF16)
    d_packed = d_packed_ref[...]
    d_normed = dot(d_packed, w_ref[...], 1, 1)
    for d in range(N_SEQ):
        d_normed_ref[d] = d_normed[ROWS * d : ROWS * (d + 1)].astype(BF16)
    column = (lax.broadcasted_iota(jnp.int32, (SEQ, 64), 1) == 4).astype(BF16)
    high, low = two_parts(d_normed * n)
    small = small_ref[...] + dot(high, column, 0, 0) + dot(low, column, 0, 0)
    grad = dot(normed, d_packed, 0, 0)
    grad = jnp.concatenate([grad, small, jnp.zeros((D, 128), F32)], axis=1)
    grad_ref[...] = grad.astype(BF16)


def attend_back(x_all, w_mix, gains, packed, logs, d_heads, small):
    return call(
        attend_back_kernel,
        [shape((N_SEQ, ROWS, D), BF16), shape((D, D), BF16)],
        [x_all, w_mix, gains, packed, logs, *d_heads, small],
        "attention_back",
        4 * SEQ * D * 576 + 3 * 10 * SEQ * SEQ * 64,
        scratch=[pltpu.VMEM((SEQ, 576), BF16), pltpu.VMEM((SEQ, 192), BF16)],
    )


def middle_kernel(
    extra, me_ref, x_ref, g0, g1, g2, g3, w_ref, router_ref, gain_ref, route_ref, *refs
):
    me = me_ref[0]
    if extra:
        d_out_ref, *refs = refs
    residual_ref, normed_ref, gates_ref, chosen_ref, high_ref, low_ref, buffer_ref = refs[:7]
    residual = x_ref[...].astype(F32)
    for d, ref in enumerate((g0, g1, g2, g3)):
        residual = residual + dot(ref[...], w_ref[lax.rem(me - d + N_SEQ, N_SEQ)], 1, 0)
    residual_ref[...] = residual
    n, _ = norm_parts(residual)
    normed = (n * gain_ref[5:6, :]).astype(BF16)
    normed_ref[...] = normed
    lane = lax.broadcasted_iota(jnp.int32, (ROWS, 128), 1)
    logits = jnp.where(lane < 4, dot(normed, router_ref[...], 1, 0), -1e30)
    logits = logits - jnp.max(logits, axis=1, keepdims=True)
    gates = jnp.exp(logits)
    gates = gates / jnp.sum(gates, axis=1, keepdims=True)
    gates_ref[...] = gates
    routes = route_ref[...]
    relative = lax.rem(routes - me + N_SEQ, N_SEQ)
    named = (lane == relative[:, 0:1]) | (lane == relative[:, 1:2])
    row = lax.broadcasted_iota(jnp.int32, (ROWS, ROWS), 0)
    column = lax.broadcasted_iota(jnp.int32, (ROWS, ROWS), 1)
    before = (row > column).astype(BF16)
    rank = dot(before, named.astype(BF16), 1, 0)
    slot = lax.broadcasted_iota(jnp.int32, (ROWS, 320), 1)
    own = jnp.where(slot >= 160, jnp.where(slot >= 240, 3, 2), jnp.where(slot >= 80, 1, 0))
    place = (slot - CAP * own).astype(F32)
    wanted = jnp.full((ROWS, 320), -1.0, F32)
    spread = jnp.zeros((ROWS, 320), F32)
    position = jnp.where(named, rank, -1.0)
    for e in range(N_SEQ):
        wanted = jnp.where(own == e, position[:, e : e + 1], wanted)
        spread = jnp.where(lax.rem(own + me, N_SEQ) == e, gates[:, e : e + 1], spread)
    taken = wanted == place
    chosen = taken.astype(BF16)
    high, low = two_parts(jnp.where(taken, spread, 0.0))
    chosen_ref[...] = chosen
    high_ref[...] = high
    low_ref[...] = low
    buffer = dot(chosen, normed, 0, 0).astype(BF16)
    if not extra:
        for d in range(N_SEQ):
            buffer_ref[d] = buffer[CAP * d : CAP * (d + 1)]
    else:
        d_out = d_out_ref[...]
        d_buffer = (dot(high, d_out, 0, 0) + dot(low, d_out, 0, 0)).astype(BF16)
        for d in range(N_SEQ):
            buffer_ref[d, 0] = buffer[CAP * d : CAP * (d + 1)]
            buffer_ref[d, 1] = d_buffer[CAP * d : CAP * (d + 1)]


def middle(me, x, gathered, w_back, router, gains, route_ids, d_out):
    extra = d_out is not None
    sent = (N_SEQ, 2, CAP, D) if extra else (N_SEQ, CAP, D)
    return call(
        partial(middle_kernel, extra),
        [
            shape((ROWS, D), F32),
            shape((ROWS, D), BF16),
            shape((ROWS, 128), F32),
            shape((ROWS, 320), BF16),
            shape((ROWS, 320), BF16),
            shape((ROWS, 320), BF16),
            shape(sent, BF16),
        ],
        [me, x, *gathered, w_back, router, gains, route_ids] + ([d_out] if extra else []),
        "middle",
        2 * ROWS * D * (D + 320),
        scalars=1,
    )


def gelu_of(hidden):
    cdf = 0.5 + 0.5 * lax.erf(hidden * 0.7071067811865476)
    return hidden * cdf, cdf


def quarter(ref, i):
    return ref[:, i].reshape(768, D)


def expert_kernel(r0, r1, r2, r3, own_ref, other_ref, out_ref, rows_ref, total):
    @pl.when(pl.program_id(0) == 0)
    def _():
        for d, ref in enumerate((r0, r1, r2, r3)):
            rows_ref[CAP * d : CAP * (d + 1)] = ref[...]
        total[...] = jnp.zeros_like(total)

    rows = rows_ref[...]
    for pack in (own_ref, other_ref):
        hidden = dot(rows, quarter(pack, 0), 1, 0)
        active = gelu_of(hidden)[0].astype(BF16)
        total[...] += dot(active, quarter(pack, 1), 1, 0)

    @pl.when(pl.program_id(0) == 1)
    def _():
        for d in range(N_SEQ):
            out_ref[d] = total[CAP * d : CAP * (d + 1)].astype(BF16)


def whole_block(dims):
    return pl.BlockSpec(dims, lambda i: (0,) * len(dims))


def pack_block():
    return pl.BlockSpec((N_SHARD, 2, 48, 768), lambda i: (0, i, 0, 0))


def grid_call(body, outs, out_specs, ins, in_specs, name, flops, scratch):
    moved = sum(math.prod(v.shape) * v.dtype.itemsize for v in list(ins) + outs)
    return pl.pallas_call(
        body,
        grid=(2,),
        out_shape=outs,
        in_specs=in_specs,
        out_specs=out_specs,
        scratch_shapes=scratch,
        name=name,
        cost_estimate=pl.CostEstimate(flops=flops, bytes_accessed=moved, transcendentals=0),
        compiler_params=pltpu.CompilerParams(
            vmem_limit_bytes=LIMIT, dimension_semantics=("arbitrary",)
        ),
    )(*ins)


def expert_run(blocks, packs):
    return grid_call(
        expert_kernel,
        [shape((N_SEQ, CAP, D), BF16)],
        [whole_block((N_SEQ, CAP, D))],
        [*blocks, *packs],
        [whole_block((CAP, D))] * 4 + [pack_block()] * 2,
        "expert",
        4 * 320 * D * FF,
        [pltpu.VMEM((320, D), BF16), pltpu.VMEM((320, D), F32)],
    )[0]


def expert_back_kernel(forward, *refs):
    ins, (own_ref, other_ref), refs = refs[: 4 if forward else 8], refs[4 if forward else 8 :][:2], refs[6 if forward else 10 :]
    out_ref, rows_out, d_result_out, act_own, act_other, dh_own, dh_other, d_total, total = refs
    step = pl.program_id(0)

    @pl.when(step == 0)
    def _():
        for d in range(N_SEQ):
            there = pl.ds(CAP * d, CAP)
            rows_out[there] = ins[d][0] if forward else ins[d][...]
            d_result_out[there] = ins[d][1] if forward else ins[4 + d][...]
        d_total[...] = jnp.zeros_like(d_total)
        if forward:
            total[...] = jnp.zeros_like(total)

    rows = rows_out[...]
    d_result = d_result_out[...]
    for pack, act_ref, dh_ref in ((own_ref, act_own, dh_own), (other_ref, act_other, dh_other)):
        hidden = dot(rows, quarter(pack, 0), 1, 0)
        value, cdf = gelu_of(hidden)
        active = value.astype(BF16)
        act_ref[...] = active
        slope = cdf + hidden * jnp.exp(-0.5 * hidden * hidden) * 0.3989422804014327
        d_hidden = (dot(d_result, quarter(pack, 1), 1, 1) * slope).astype(BF16)
        dh_ref[...] = d_hidden
        d_total[...] += dot(d_hidden, quarter(pack, 0), 1, 1)
        if forward:
            total[...] += dot(active, quarter(pack, 1), 1, 0)

    @pl.when(step == 1)
    def _():
        for d in range(N_SEQ):
            there = pl.ds(CAP * d, CAP)
            if forward:
                out_ref[d, 0] = total[there].astype(BF16)
                out_ref[d, 1] = d_total[there].astype(BF16)
            else:
                out_ref[d] = d_total[there].astype(BF16)


def expert_back(blocks, packs, forward):
    sent = (N_SEQ, 2, CAP, D) if forward else (N_SEQ, CAP, D)
    half = pl.BlockSpec((320, 768), lambda i: (0, i))
    block = whole_block((2, CAP, D)) if forward else whole_block((CAP, D))
    return grid_call(
        partial(expert_back_kernel, forward),
        [shape(sent, BF16)] + [shape((320, D), BF16)] * 2 + [shape((320, 1536), BF16)] * 4,
        [whole_block(sent)] + [whole_block((320, D))] * 2 + [half] * 4,
        [*blocks, *packs],
        [block] * len(blocks) + [pack_block()] * 2,
        "expert_back",
        8 * 320 * D * FF,
        [pltpu.VMEM((320, D), F32)] * 2,
    )


def expert_grad_kernel(rows_ref, d_result_ref, act_ref, dh_ref, out_ref):
    grad = dot(rows_ref[...], dh_ref[...], 0, 0).astype(BF16)
    out_ref[:, 0] = grad.reshape(N_SHARD, 48, 768)
    grad = dot(act_ref[...], d_result_ref[...], 0, 0).astype(BF16)
    out_ref[:, 1] = grad.reshape(N_SHARD, 48, 768)


def expert_grad(rows, d_result, active, d_hidden):
    half = pl.BlockSpec((320, 768), lambda i: (0, i))
    return grid_call(
        expert_grad_kernel,
        [shape((N_SHARD, 4, 48, 768), BF16)],
        [pack_block()],
        [rows, d_result, active, d_hidden],
        [whole_block((320, D))] * 2 + [half] * 2,
        "expert_grad",
        2 * 320 * D * FF,
        [],
    )[0]


def combine_kernel(residual_ref, high_ref, low_ref, r0, r1, r2, r3, out_ref, rows_ref):
    for d, ref in enumerate((r0, r1, r2, r3)):
        rows_ref[CAP * d : CAP * (d + 1)] = ref[...]
    rows = rows_ref[...]
    total = residual_ref[...] + dot(high_ref[...], rows, 1, 0) + dot(low_ref[...], rows, 1, 0)
    out_ref[...] = total.astype(BF16)


def combine(residual, high, low, blocks):
    return call(
        combine_kernel,
        [shape((ROWS, D), BF16)],
        [residual, high, low, *blocks],
        "combine",
        4 * ROWS * D * 320,
        scratch=[pltpu.VMEM((320, D), BF16)],
    )[0]


def send_grad_kernel(d_out_ref, high_ref, low_ref, out_ref):
    d_out = d_out_ref[...]
    total = dot(high_ref[...], d_out, 0, 0) + dot(low_ref[...], d_out, 0, 0)
    for d in range(N_SEQ):
        out_ref[d] = total[CAP * d : CAP * (d + 1)].astype(BF16)


def send_grad(d_out, high, low):
    return call(
        send_grad_kernel, [shape((N_SEQ, CAP, D), BF16)], [d_out, high, low], "send_grad", 4 * ROWS * D * 320
    )[0]


def middle_back_kernel(paired, me_ref, d_out_ref, *refs):
    me = me_ref[0]
    count = 4 if paired else 8
    blocks, refs = refs[:count], refs[count:]
    gathered, refs = refs[:4], refs[4:]
    (
        chosen_ref, gates_ref, residual_ref, normed_ref, gain_ref, w_ref,
        d_residual_ref, small_ref, grad_ref, d_mix_ref, rows_ref, d_rows_ref,
    ) = refs
    for d in range(N_SEQ):
        there = pl.ds(CAP * d, CAP)
        rows_ref[there] = blocks[d][0] if paired else blocks[d][...]
        d_rows_ref[there] = blocks[d][1] if paired else blocks[4 + d][...]
    d_out = d_out_ref[...]
    chosen = chosen_ref[...]
    gates = gates_ref[...]
    products = dot(d_out, rows_ref[...], 1, 1) * chosen.astype(F32)
    slot = lax.broadcasted_iota(jnp.int32, (ROWS, 320), 1)
    own = jnp.where(slot >= 160, jnp.where(slot >= 240, 3, 2), jnp.where(slot >= 80, 1, 0))
    own = lax.rem(own + me, N_SEQ)
    lane = lax.broadcasted_iota(jnp.int32, (ROWS, 128), 1)
    d_gates = jnp.zeros((ROWS, 128), F32)
    for e in range(N_SEQ):
        part = jnp.sum(jnp.where(own == e, products, 0.0), axis=1, keepdims=True)
        d_gates = jnp.where(lane == e, part, d_gates)
    d_logits = gates * (d_gates - jnp.sum(gates * d_gates, axis=1, keepdims=True))
    d_normed = dot(chosen, d_rows_ref[...], 1, 0)
    for e in range(N_SEQ):
        d_normed = d_normed + d_logits[:, e : e + 1] * gain_ref[e : e + 1, :]
    n, inverse = norm_parts(residual_ref[...])
    d_residual = d_out.astype(F32) + norm_back(n, inverse, gain_ref[5:6, :], d_normed)
    d_residual_ref[...] = d_residual
    d_branch = d_residual.astype(BF16)
    for d in range(N_SEQ):
        group = lax.rem(me - d + N_SEQ, N_SEQ)
        d_mix_ref[d] = dot(d_branch, w_ref[group], 1, 1).astype(BF16)
        grad_ref[group] = dot(gathered[d][...], d_branch, 0, 0).astype(BF16)
    high, low = two_parts(d_logits)
    small = dot(normed_ref[...], high, 0, 0) + dot(normed_ref[...], low, 0, 0)
    column = (lax.broadcasted_iota(jnp.int32, (ROWS, 128), 1) == 5).astype(BF16)
    high, low = two_parts(d_normed * n)
    small = small + dot(high, column, 0, 0) + dot(low, column, 0, 0)
    small_ref[...] = small[:, 0:64]


def middle_back(me, d_out, blocks, gathered, chosen, gates, residual, normed, gains, w_back, paired):
    return call(
        partial(middle_back_kernel, paired),
        [
            shape((ROWS, D), F32),
            shape((D, 64), F32),
            shape((N_SEQ, 192, D), BF16),
            shape((N_SEQ, ROWS, 192), BF16),
        ],
        [me, d_out, *blocks, *gathered, chosen, gates, residual, normed, gains, w_back],
        "middle_back",
        2 * ROWS * D * (2 * D + 640),
        scalars=1,
        scratch=[pltpu.VMEM((320, D), BF16)] * 2,
    )


def finish_kernel(d_residual_ref, x_ref, gain_ref, b0, b1, b2, b3, out_ref):
    d_normed = b0[...].astype(F32) + b1[...].astype(F32) + b2[...].astype(F32) + b3[...].astype(F32)
    n, inverse = norm_parts(x_ref[...].astype(F32))
    total = d_residual_ref[...] + norm_back(n, inverse, gain_ref[4:5, :], d_normed)
    out_ref[...] = total.astype(BF16)


def finish(d_residual, x, gains, blocks):
    return call(
        finish_kernel, [shape((ROWS, D), BF16)], [d_residual, x, gains, *blocks], "finish", 20 * ROWS * D
    )[0]


def attention_weights(w_qkv, w_proj, w_route, gain_attn, gain_ffn):
    core = lax.axis_index("section")
    mine = w_qkv.reshape(12, 3, N_SEQ, 192).transpose(2, 0, 1, 3).reshape(N_SEQ, 12, 576)
    small = jnp.concatenate(
        [w_route, gain_attn[:, None], gain_ffn[:, None], jnp.zeros((12, 122), BF16)], axis=1
    )
    whole = jnp.broadcast_to(w_proj, (N_SEQ, 12, D))
    mine = jnp.concatenate([whole, mine, jnp.broadcast_to(small, (N_SEQ, 12, 128))], axis=2)
    spread = jnp.broadcast_to(mine[:, None], (N_SEQ, N_SHARD, 12, WIDE))
    spread = spread.reshape(N_SEQ * N_SHARD, 12, WIDE)
    whole = lax.all_to_all(spread, ("seq", "shard"), 0, 0, tiled=True).reshape(D, WIDE)
    other = swap(whole)
    out = []
    for s in range(2):
        rows = jnp.where(core == s, whole, other)
        table = rows[:, 1344:1352].T.astype(F32)
        out.append((rows[:, 768:1344], rows[:, :768].reshape(N_SEQ, 192, D), rows[:, 1344:], table))
    return out


def expert_weights(w_in, w_out):
    core = lax.axis_index("section")
    first = w_in.reshape(48, N_SHARD, 4, 48).transpose(2, 0, 1, 3).reshape(4, 48, 768)
    second = w_out.reshape(4, 48, 768)
    quarters = jnp.stack([first, second], axis=1).reshape(2, 4, 48, 768)
    mine = pick(quarters, core)
    arrived = swap(pick(quarters, 1 - core))
    out = []
    for s in range(2):
        own = jnp.where(core == s, mine, arrived)
        if s == 1:
            own = tie(own, out[0][0])
        whole = lax.all_gather(own, "shard", axis=0, tiled=False)
        out.append((whole, swap(whole)))
    return out


def join_experts(own, other):
    return (own.astype(F32) + swap(other).astype(F32)).astype(BF16)


def scatter_beside(v):
    return lax.psum_scatter(v, "shard", scatter_dimension=0, tiled=True)[0]


def join_attention(mix, back):
    core = lax.axis_index("section")
    keep = jnp.where(core == 0, mix, back)
    give = jnp.where(core == 0, back, mix)
    return (keep.astype(F32) + swap(give).astype(F32)).astype(BF16)


def shards(images_in, out_grad, routes, w_qkv, w_proj, w_route, gain_attn, gain_ffn, w_in, w_out):
    core = lax.axis_index("section")
    me = lax.axis_index("seq").astype(jnp.int32).reshape(1)
    own_routes = routes[0, :, 0]
    mine = pick(own_routes, core)
    arrived = swap(pick(own_routes, 1 - core))
    route_of = (jnp.where(core == 0, mine, arrived), jnp.where(core == 0, arrived, mine))
    x0 = pick(images_in, core)[0]
    d_last = pick(out_grad, core)[0]
    attn = attention_weights(w_qkv[0], w_proj[0], w_route[0], gain_attn[0], gain_ffn[0])
    experts = expert_weights(w_in[0, 0], w_out[0, 0])

    saved = []
    x = x0
    layer_outs = []
    for s in range(2):
        w_mix, w_back, router, table = attn[s]
        x_all = gather_tokens(x)
        mixture, packed, logs = attend(x_all, w_mix, table)
        gathered = send_out(mixture)
        d_out = d_last if s == 1 else None
        residual, normed, gates, chosen, high, low, buffer = middle(
            me, x, gathered, w_back, router, table, route_of[s], d_out
        )
        blocks = send_out(buffer)
        kept = (x, x_all, packed, logs, gathered, residual, normed, gates, chosen, high, low, blocks)
        if s == 0:
            returned = send_back(expert_run(blocks, experts[s]))
            x = combine(residual, high, low, returned)
            layer_outs.append(x)
            saved.append((kept, returned))
        else:
            saved.append((kept, None))

    d_out = d_last
    in_grads = [None, None]
    expert_sums = [None, None]
    joined = [None, None]
    for s in (1, 0):
        w_mix, w_back, router, table = attn[s]
        kept, returned = saved[s]
        x, x_all, packed, logs, gathered, residual, normed, gates, chosen, high, low, blocks = kept
        if s == 1:
            sent, *states = expert_back(blocks, experts[s], True)
            arrived = send_back(sent)
            layer_outs.append(combine(residual, high, low, [v[0] for v in arrived]))
        else:
            d_blocks = send_out(send_grad(d_out, high, low))
            sent, *states = expert_back([*blocks, *d_blocks], experts[s], False)
            arrived = [*returned, *send_back(sent)]
        rows, d_result, act_own, act_other, dh_own, dh_other = states
        other = expert_grad(rows, d_result, act_other, dh_other)
        own = expert_grad(rows, d_result, act_own, dh_own)
        expert_sums[s] = scatter_beside(join_experts(own, other))
        d_residual, small, grad_back, d_mixture = middle_back(
            me, d_out, arrived, gathered, chosen, gates, residual, normed, table, w_back, s == 1
        )
        d_heads = send_back(d_mixture)
        d_normed, grad_mix = attend_back(x_all, w_mix, table, packed, logs, d_heads, small)
        d_parts = send_out(d_normed)
        joined[s] = join_attention(grad_mix, grad_back.reshape(D, D))
        d_out = finish(d_residual, x, table, d_parts)
        in_grads[s] = d_out

    pair = jnp.concatenate([joined[0], joined[1]], axis=1).reshape(N_SEQ * N_SHARD, 12, 2 * D)
    arrived = lax.all_to_all(pair, ("seq", "shard"), 0, 0, tiled=True)
    attn_sum = jnp.sum(arrived.reshape(N_SEQ, N_SHARD, 12, 2 * D).astype(F32), axis=1)
    attn_sums = [attn_sum[:, :, :D], attn_sum[:, :, D:]]

    def settle(pair):
        keep = jnp.where(core == 0, pair[0], pair[1])
        give = jnp.where(core == 0, pair[1], pair[0])
        return keep, swap(give)

    def in_order(keep, got):
        return jnp.where(core == 0, jnp.stack([keep, got]), jnp.stack([got, keep]))

    layer_out = in_order(*settle(layer_outs))
    in_grad = in_order(*settle(in_grads))
    expert_sum = in_order(*settle(expert_sums)).astype(F32)
    attn_sum = in_order(*settle(attn_sums))
    quarters = expert_sum.reshape(4, 2, 48, 768)
    grad_in = quarters[:, 0].reshape(4, 48, N_SHARD, 48).transpose(1, 2, 0, 3).reshape(48, FF)
    grad_out = quarters[:, 1].reshape(192, D)
    mix = attn_sum[0]
    back = jnp.sum(attn_sum[1], axis=0)
    grad_qkv = mix[:, :, :576].reshape(N_SEQ, 12, 3, 192).transpose(1, 2, 0, 3).reshape(12, 3 * D)
    small = jnp.sum(mix[:, :, 576:640], axis=0)
    return (
        layer_out[None, :, None],
        in_grad[None, :, None],
        grad_qkv[None],
        back[None],
        small[None, :, 0:4],
        small[None, :, 4],
        small[None, :, 5],
        grad_in[None],
        grad_out[None],
    )


def solution(mesh):
    def run(*args):
        outs = shards(*args)
        outs = list(outs)
        outs[7] = outs[7][:, None]
        outs[8] = outs[8][:, None]
        return tuple(outs)

    return jax.shard_map(
        run,
        mesh=mesh,
        in_specs=(
            P(None, "shard", "seq", None),
            P(None, "shard", "seq", None),
            P("section", None, "shard", "seq", None),
            P("section", ("seq", "shard"), None),
            P("section", ("seq", "shard"), None),
            P("section", ("seq", "shard"), None),
            P("section", ("seq", "shard")),
            P("section", ("seq", "shard")),
            P("section", "seq", "shard", None),
            P("section", "seq", "shard", None),
        ),
        out_specs=(
            P("section", None, "shard", "seq", None),
            P("section", None, "shard", "seq", None),
            P("section", ("seq", "shard"), None),
            P("section", ("seq", "shard"), None),
            P("section", ("seq", "shard"), None),
            P("section", ("seq", "shard")),
            P("section", ("seq", "shard")),
            P("section", "seq", "shard", None),
            P("section", "seq", "shard", None),
        ),
        check_vma=False,
    )
```

```python
import math
from functools import partial

import jax
import jax.numpy as jnp
from jax import lax
from jax.experimental import pallas as pl
from jax.experimental.pallas import tpu as pltpu
from jax.sharding import PartitionSpec as P

D = 768
FF = 3072
HEAD_DIM = 64
CAP = 80
N_SEQ = 4
N_SHARD = 16
GROUP = 3
ROWS = 144
SEQ = 576
WIDE = 1472
LIMIT = 56 * 1024 * 1024
EPSILON = 1e-06
F32 = jnp.float32
BF16 = jnp.bfloat16


def dot(a, b, ca, cb):
    return lax.dot_general(a, b, (((ca,), (cb,)), ((), ())), preferred_element_type=F32)


def swap(v):
    return lax.ppermute(v, "section", [(0, 1), (1, 0)])


def turn(v, d):
    return lax.ppermute(v, "seq", [(i, (i + d) % N_SEQ) for i in range(N_SEQ)])


def hop(v, axis, d):
    route = []
    for z in range(4):
        for x in range(4):
            to = ((z + d) % 4) * 4 + x if axis == "z" else z * 4 + (x + d) % 4
            route.append((z * 4 + x, to))
    return lax.ppermute(v, "shard", route)


def place(axis):
    i = lax.axis_index("shard")
    return i // 4 if axis == "z" else lax.rem(i, 4)


def hop(v, axis, d):
    route = []
    for z in range(4):
        for x in range(4):
            to = ((z + d) % 4) * 4 + x if axis == "z" else z * 4 + (x + d) % 4
            route.append((z * 4 + x, to))
    return lax.ppermute(v, "shard", route)


def from_ring(v, axis):
    return [v] + [hop(v, axis, -d) for d in (1, 2, 3)]


def along_ring(blocks, axis):
    return [blocks[0]] + [hop(blocks[d], axis, d) for d in (1, 2, 3)]


def where_shard():
    i = lax.axis_index("shard").astype(jnp.int32)
    return jnp.stack([i // 4, lax.rem(i, 4)])


def pick(v, i):
    return lax.dynamic_index_in_dim(v, i, 0, keepdims=False)


def tie(value, other):
    return lax.optimization_barrier((value, other))[0]


def norm_parts(values):
    centred = values - jnp.mean(values, axis=-1, keepdims=True)
    inverse = lax.rsqrt(jnp.mean(centred * centred, axis=-1, keepdims=True) + EPSILON)
    return centred * inverse, inverse


def norm_back(n, inverse, gain, dy):
    gdy = dy * gain
    return (
        gdy
        - jnp.mean(gdy, axis=-1, keepdims=True)
        - n * jnp.mean(gdy * n, axis=-1, keepdims=True)
    ) * inverse


def two_parts(v):
    high = v.astype(BF16)
    return high, (v - high.astype(F32)).astype(BF16)


def gather_tokens(x):
    return jnp.concatenate([x] + [turn(x, -d) for d in (1, 2, 3)], axis=0)


def send_out(blocks):
    return [blocks[0]] + [turn(blocks[d], d) for d in (1, 2, 3)]


def send_back(blocks):
    return [blocks[0]] + [turn(blocks[d], -d) for d in (1, 2, 3)]


def vmem():
    return pl.BlockSpec(memory_space=pltpu.VMEM)


def smem():
    return pl.BlockSpec(memory_space=pltpu.SMEM)


def shape(dims, kind):
    return jax.ShapeDtypeStruct(dims, kind)


def call(body, outs, ins, name, flops, scalars=0, scratch=()):
    specs = [smem()] * scalars + [vmem()] * (len(ins) - scalars)
    moved = sum(math.prod(v.shape) * v.dtype.itemsize for v in list(ins) + list(outs))
    return pl.pallas_call(
        body,
        out_shape=outs,
        in_specs=specs,
        out_specs=[vmem()] * len(outs),
        scratch_shapes=list(scratch),
        name=name,
        cost_estimate=pl.CostEstimate(flops=int(flops), bytes_accessed=moved, transcendentals=0),
        compiler_params=pltpu.CompilerParams(vmem_limit_bytes=LIMIT),
    )(*ins)


def attend_kernel(x0, x1, x2, x3, w_ref, gain_ref, m0, m1, m2, m3, x_ref, packed_ref, log_ref):
    for d, ref in enumerate((x0, x1, x2, x3)):
        x_ref[ROWS * d : ROWS * (d + 1)] = ref[...]
    n, _ = norm_parts(x_ref[...].astype(F32))
    normed = (n * gain_ref[4:5, :]).astype(BF16)
    packed_ref[...] = dot(normed, w_ref[...], 1, 0).astype(BF16)
    lane = lax.broadcasted_iota(jnp.int32, (SEQ, 128), 1)
    logs = jnp.zeros((SEQ, 128), F32)
    outs = []
    for h in range(GROUP):
        query = packed_ref[:, 64 * h : 64 * h + 64]
        key = packed_ref[:, 192 + 64 * h : 256 + 64 * h]
        value = packed_ref[:, 384 + 64 * h : 448 + 64 * h]
        scores = dot(query, key, 1, 1) * HEAD_DIM ** (-0.5)
        top = jnp.max(scores, axis=1, keepdims=True)
        exponent = jnp.exp(scores - top)
        total = jnp.sum(exponent, axis=1, keepdims=True)
        outs.append((dot(exponent.astype(BF16), value, 1, 0) / total).astype(BF16))
        logs = jnp.where(lane == h, top + jnp.log(total), logs)
    log_ref[...] = logs
    mixture = jnp.concatenate(outs, axis=1)
    for d, ref in enumerate((m0, m1, m2, m3)):
        ref[...] = mixture[ROWS * d : ROWS * (d + 1)]


def attend(x_blocks, w_mix, gains):
    outs = call(
        attend_kernel,
        [shape((ROWS, 192), BF16)] * 4
        + [shape((SEQ, D), BF16), shape((SEQ, 576), BF16), shape((SEQ, 128), F32)],
        [*x_blocks, w_mix, gains],
        "attention",
        2 * SEQ * D * 576 + 3 * 4 * SEQ * SEQ * 64,
    )
    return outs[:4], *outs[4:]


def attend_back_kernel(
    x_ref, w_ref, gain_ref, packed_ref, log_ref, d0, d1, d2, d3, small_ref,
    n0, n1, n2, n3, grad_ref, d_packed_ref, d_mix_ref,
):
    for d, ref in enumerate((d0, d1, d2, d3)):
        d_mix_ref[ROWS * d : ROWS * (d + 1)] = ref[...]
    scaling = HEAD_DIM ** (-0.5)
    parts = [[], [], []]
    for h in range(GROUP):
        query = packed_ref[:, 64 * h : 64 * h + 64]
        key = packed_ref[:, 192 + 64 * h : 256 + 64 * h]
        value = packed_ref[:, 384 + 64 * h : 448 + 64 * h]
        d_out = d_mix_ref[:, 64 * h : 64 * h + 64]
        attention = jnp.exp(dot(query, key, 1, 1) * scaling - log_ref[:, h : h + 1])
        parts[2].append(dot(attention.astype(BF16), d_out, 0, 0).astype(BF16))
        d_att = dot(d_out, value, 1, 1)
        centre = jnp.sum(attention * d_att, axis=1, keepdims=True)
        d_scores = (attention * (d_att - centre) * scaling).astype(BF16)
        parts[0].append(dot(d_scores, key, 1, 0).astype(BF16))
        parts[1].append(dot(d_scores, query, 0, 0).astype(BF16))
    d_packed_ref[...] = jnp.concatenate(parts[0] + parts[1] + parts[2], axis=1)
    n, _ = norm_parts(x_ref[...].astype(F32))
    normed = (n * gain_ref[4:5, :]).astype(BF16)
    d_packed = d_packed_ref[...]
    d_normed = dot(d_packed, w_ref[...], 1, 1)
    for d, ref in enumerate((n0, n1, n2, n3)):
        ref[...] = d_normed[ROWS * d : ROWS * (d + 1)].astype(BF16)
    column = (lax.broadcasted_iota(jnp.int32, (SEQ, 64), 1) == 4).astype(BF16)
    high, low = two_parts(d_normed * n)
    small = small_ref[...] + dot(high, column, 0, 0) + dot(low, column, 0, 0)
    grad = dot(normed, d_packed, 0, 0)
    grad = jnp.concatenate([grad, small, jnp.zeros((D, 128), F32)], axis=1)
    grad_ref[...] = by_shard(grad.astype(BF16))


def attend_back(x_all, w_mix, gains, packed, logs, d_heads, small):
    outs = call(
        attend_back_kernel,
        [shape((ROWS, D), BF16)] * 4 + [shape((D, D), BF16)],
        [x_all, w_mix, gains, packed, logs, *d_heads, small],
        "attention_back",
        4 * SEQ * D * 576 + 3 * 10 * SEQ * SEQ * 64,
        scratch=[pltpu.VMEM((SEQ, 576), BF16), pltpu.VMEM((SEQ, 192), BF16)],
    )
    return outs[:4], outs[4]


def order_rows(first, second):
    i = lax.broadcasted_iota(jnp.int32, (D, 1), 0)
    outer = lax.div(i, 12 * first)
    left = i - 12 * first * outer
    inner = lax.div(left, 12)
    source = inner * (12 * second) + outer * 12 + left - 12 * inner
    return (lax.broadcasted_iota(jnp.int32, (D, D), 1) == source).astype(BF16)


def by_shard(v):
    return dot(order_rows(N_SEQ, N_SHARD), v, 1, 0).astype(BF16)


def unpack_kernel(where_ref, b0, b1, b2, b3, rows_ref, back_ref, all_ref):
    z, x = where_ref[0], where_ref[1]
    for dz, ref in enumerate((b0, b1, b2, b3)):
        for dx in range(4):
            all_ref[lax.rem(z + dz, 4) * 4 + lax.rem(x + dx, 4)] = ref[dx]
    order = order_rows(N_SHARD, N_SEQ)
    whole = all_ref[...].reshape(D, 832)
    ordered = dot(order, whole, 1, 0).astype(BF16)
    rows_ref[...] = ordered[:, :640]
    for chunk in range(N_SEQ):
        back_ref[:, 192 * chunk : 192 * (chunk + 1)] = ordered[192 * chunk : 192 * (chunk + 1), 640:]


def unpack(where, blocks):
    return call(
        unpack_kernel,
        [shape((D, 640), BF16), shape((192, D), BF16)],
        [where, *blocks],
        "unpack",
        2 * D * D * 832,
        scalars=1,
        scratch=[pltpu.VMEM((N_SHARD, 48, 832), BF16)],
    )


def order_kernel(where_ref, a0, a1, a2, a3, b0, b1, b2, b3, out_ref):
    z, x = where_ref[0], where_ref[1]
    firsts, seconds = (a0, a1, a2, a3), (b0, b1, b2, b3)
    for dz in range(4):
        for dx in range(4):
            place = lax.rem(z + dz, 4) * 4 + lax.rem(x + dx, 4)
            out_ref[place, 0:2] = firsts[dz][dx]
            out_ref[place, 2:4] = seconds[dx][dz]


def order(where, firsts, seconds):
    return call(
        order_kernel,
        [shape((N_SHARD, 4, 48, D), BF16)],
        [where, *firsts, *seconds],
        "order",
        0,
        scalars=1,
    )[0]


def arrange_kernel(cut, where_ref, *refs):
    z, x = where_ref[0], where_ref[1]
    if cut:
        ka, ga, *outs = refs
        firsts, seconds = [(v, slice(0, 2)) for v in (ka, ga)], [(v, slice(2, 4)) for v in (ka, ga)]
    else:
        ka, ga, kb, gb, *outs = refs
        firsts, seconds = [(v, slice(None)) for v in (ka, ga)], [(v, slice(None)) for v in (kb, gb)]
    for d in range(4):
        for o in range(4):
            there = o * 4 + lax.rem(x + d, 4)
            (keep, part), (got, _) = firsts
            outs[d][o] = (keep[there, part].astype(F32) + got[there, part].astype(F32)).astype(BF16)
            there = lax.rem(z + d, 4) * 4 + o
            (keep, part), (got, _) = seconds
            outs[4 + d][o] = (keep[there, part].astype(F32) + got[there, part].astype(F32)).astype(BF16)


def arrange(where, pairs):
    cut = len(pairs) == 2
    dims = (4, 2, 48, D) if cut else (4, 48, D)
    outs = call(
        partial(arrange_kernel, cut), [shape(dims, BF16)] * 8, [where, *pairs], "arrange", 0, scalars=1
    )
    return outs[:4], outs[4:]


def add_up_kernel(where_ref, *refs):
    z, x = where_ref[0], where_ref[1]
    for half, here in ((0, z), (1, x)):
        blocks, outs = refs[4 * half : 4 * half + 4], refs[8 + 4 * half : 12 + 4 * half]
        for d in range(4):
            there = lax.rem(here + d, 4)
            total = blocks[0][there].astype(F32)
            for other in blocks[1:]:
                total = total + other[there].astype(F32)
            outs[d][...] = total.astype(BF16)


def add_up(where, firsts, seconds):
    dims = firsts[0].shape[1:]
    outs = call(
        add_up_kernel, [shape(dims, BF16)] * 8, [where, *firsts, *seconds], "add_up", 0, scalars=1
    )
    return outs[:4], outs[4:]


def last_kernel(*refs):
    for half in range(2):
        total = refs[4 * half][...].astype(F32)
        for d in (1, 2, 3):
            total = total + refs[4 * half + d][...].astype(F32)
        refs[8][half] = total.astype(BF16)


def last(firsts, seconds):
    dims = firsts[0].shape
    return call(last_kernel, [shape((2,) + dims, BF16)], [*firsts, *seconds], "last", 0)[0]


def scatter_pair(where, *pairs):
    firsts, seconds = arrange(where, pairs)
    firsts, seconds = add_up(where, along_ring(firsts, "x"), along_ring(seconds, "z"))
    return last(along_ring(firsts, "z"), along_ring(seconds, "x"))


def middle_kernel(
    extra, me_ref, x_ref, g0, g1, g2, g3, w_ref, router_ref, gain_ref, route_ref, *refs
):
    me = me_ref[0]
    if extra:
        d_out_ref, *refs = refs
    residual_ref, normed_ref, gates_ref, chosen_ref, high_ref, low_ref, *sent = refs
    residual = x_ref[...].astype(F32)
    for d, ref in enumerate((g0, g1, g2, g3)):
        residual = residual + dot(ref[...], w_ref[d], 1, 0)
    residual_ref[...] = residual
    n, _ = norm_parts(residual)
    normed = (n * gain_ref[5:6, :]).astype(BF16)
    normed_ref[...] = normed
    lane = lax.broadcasted_iota(jnp.int32, (ROWS, 128), 1)
    logits = jnp.where(lane < 4, dot(normed, router_ref[...], 1, 0), -1e30)
    logits = logits - jnp.max(logits, axis=1, keepdims=True)
    gates = jnp.exp(logits)
    gates = gates / jnp.sum(gates, axis=1, keepdims=True)
    gates_ref[...] = gates
    routes = route_ref[...]
    relative = lax.rem(routes - me + N_SEQ, N_SEQ)
    named = (lane == relative[:, 0:1]) | (lane == relative[:, 1:2])
    row = lax.broadcasted_iota(jnp.int32, (ROWS, ROWS), 0)
    column = lax.broadcasted_iota(jnp.int32, (ROWS, ROWS), 1)
    before = (row > column).astype(BF16)
    rank = dot(before, named.astype(BF16), 1, 0)
    slot = lax.broadcasted_iota(jnp.int32, (ROWS, 320), 1)
    own = jnp.where(slot >= 160, jnp.where(slot >= 240, 3, 2), jnp.where(slot >= 80, 1, 0))
    place = (slot - CAP * own).astype(F32)
    wanted = jnp.full((ROWS, 320), -1.0, F32)
    spread = jnp.zeros((ROWS, 320), F32)
    position = jnp.where(named, rank, -1.0)
    for e in range(N_SEQ):
        wanted = jnp.where(own == e, position[:, e : e + 1], wanted)
        spread = jnp.where(lax.rem(own + me, N_SEQ) == e, gates[:, e : e + 1], spread)
    taken = wanted == place
    chosen = taken.astype(BF16)
    high, low = two_parts(jnp.where(taken, spread, 0.0))
    chosen_ref[...] = chosen
    high_ref[...] = high
    low_ref[...] = low
    buffer = dot(chosen, normed, 0, 0).astype(BF16)
    if not extra:
        for d in range(N_SEQ):
            sent[d][...] = buffer[CAP * d : CAP * (d + 1)]
    else:
        d_out = d_out_ref[...]
        d_buffer = (dot(high, d_out, 0, 0) + dot(low, d_out, 0, 0)).astype(BF16)
        for d in range(N_SEQ):
            sent[d][0] = buffer[CAP * d : CAP * (d + 1)]
            sent[d][1] = d_buffer[CAP * d : CAP * (d + 1)]


def middle(me, x, gathered, w_back, router, gains, route_ids, d_out):
    extra = d_out is not None
    sent = (2, CAP, D) if extra else (CAP, D)
    outs = call(
        partial(middle_kernel, extra),
        [
            shape((ROWS, D), F32),
            shape((ROWS, D), BF16),
            shape((ROWS, 128), F32),
            shape((ROWS, 320), BF16),
            shape((ROWS, 320), BF16),
            shape((ROWS, 320), BF16),
        ]
        + [shape(sent, BF16)] * 4,
        [me, x, *gathered, w_back, router, gains, route_ids] + ([d_out] if extra else []),
        "middle",
        2 * ROWS * D * (D + 320),
        scalars=1,
    )
    return *outs[:6], outs[6:]


def gelu_of(hidden):
    cdf = 0.5 + 0.5 * lax.erf(hidden * 0.7071067811865476)
    return hidden * cdf, cdf


def quarter(ref, i):
    return ref[:, i].reshape(768, D)


def expert_kernel(r0, r1, r2, r3, own_ref, other_ref, o0, o1, o2, o3, rows_ref, total):
    @pl.when(pl.program_id(0) == 0)
    def _():
        for d, ref in enumerate((r0, r1, r2, r3)):
            rows_ref[CAP * d : CAP * (d + 1)] = ref[...]
        total[...] = jnp.zeros_like(total)

    rows = rows_ref[...]
    for pack in (own_ref, other_ref):
        hidden = dot(rows, quarter(pack, 0), 1, 0)
        active = gelu_of(hidden)[0].astype(BF16)
        total[...] += dot(active, quarter(pack, 1), 1, 0)

    @pl.when(pl.program_id(0) == 1)
    def _():
        for d, ref in enumerate((o0, o1, o2, o3)):
            ref[...] = total[CAP * d : CAP * (d + 1)].astype(BF16)


def whole_block(dims):
    return pl.BlockSpec(dims, lambda i: (0,) * len(dims))


def pack_block():
    return pl.BlockSpec((N_SHARD, 2, 48, 768), lambda i: (0, i, 0, 0))


def grid_call(body, outs, out_specs, ins, in_specs, name, flops, scratch):
    moved = sum(math.prod(v.shape) * v.dtype.itemsize for v in list(ins) + outs)
    return pl.pallas_call(
        body,
        grid=(2,),
        out_shape=outs,
        in_specs=in_specs,
        out_specs=out_specs,
        scratch_shapes=scratch,
        name=name,
        cost_estimate=pl.CostEstimate(flops=flops, bytes_accessed=moved, transcendentals=0),
        compiler_params=pltpu.CompilerParams(
            vmem_limit_bytes=LIMIT, dimension_semantics=("arbitrary",)
        ),
    )(*ins)


def expert_run(blocks, packs):
    return grid_call(
        expert_kernel,
        [shape((CAP, D), BF16)] * 4,
        [whole_block((CAP, D))] * 4,
        [*blocks, *packs],
        [whole_block((CAP, D))] * 4 + [pack_block()] * 2,
        "expert",
        4 * 320 * D * FF,
        [pltpu.VMEM((320, D), BF16), pltpu.VMEM((320, D), F32)],
    )


def expert_back_kernel(forward, *refs):
    ins, (own_ref, other_ref), refs = refs[: 4 if forward else 8], refs[4 if forward else 8 :][:2], refs[6 if forward else 10 :]
    sent, refs = refs[:4], refs[4:]
    rows_out, d_result_out, act_own, act_other, dh_own, dh_other, d_total, total = refs
    step = pl.program_id(0)

    @pl.when(step == 0)
    def _():
        for d in range(N_SEQ):
            there = pl.ds(CAP * d, CAP)
            rows_out[there] = ins[d][0] if forward else ins[d][...]
            d_result_out[there] = ins[d][1] if forward else ins[4 + d][...]
        d_total[...] = jnp.zeros_like(d_total)
        if forward:
            total[...] = jnp.zeros_like(total)

    rows = rows_out[...]
    d_result = d_result_out[...]
    for pack, act_ref, dh_ref in ((own_ref, act_own, dh_own), (other_ref, act_other, dh_other)):
        hidden = dot(rows, quarter(pack, 0), 1, 0)
        value, cdf = gelu_of(hidden)
        active = value.astype(BF16)
        act_ref[...] = active
        slope = cdf + hidden * jnp.exp(-0.5 * hidden * hidden) * 0.3989422804014327
        d_hidden = (dot(d_result, quarter(pack, 1), 1, 1) * slope).astype(BF16)
        dh_ref[...] = d_hidden
        d_total[...] += dot(d_hidden, quarter(pack, 0), 1, 1)
        if forward:
            total[...] += dot(active, quarter(pack, 1), 1, 0)

    @pl.when(step == 1)
    def _():
        for d in range(N_SEQ):
            there = pl.ds(CAP * d, CAP)
            if forward:
                sent[d][0] = total[there].astype(BF16)
                sent[d][1] = d_total[there].astype(BF16)
            else:
                sent[d][...] = d_total[there].astype(BF16)


def expert_back(blocks, packs, forward):
    half = pl.BlockSpec((320, 768), lambda i: (0, i))
    block = whole_block((2, CAP, D)) if forward else whole_block((CAP, D))
    sent = (2, CAP, D) if forward else (CAP, D)
    outs = grid_call(
        partial(expert_back_kernel, forward),
        [shape(sent, BF16)] * 4 + [shape((320, D), BF16)] * 2 + [shape((320, 1536), BF16)] * 4,
        [whole_block(sent)] * 4 + [whole_block((320, D))] * 2 + [half] * 4,
        [*blocks, *packs],
        [block] * len(blocks) + [pack_block()] * 2,
        "expert_back",
        8 * 320 * D * FF,
        [pltpu.VMEM((320, D), F32)] * 2,
    )
    return outs[:4], *outs[4:]


def expert_grad_kernel(rows_ref, d_result_ref, act_ref, dh_ref, out_ref):
    grad = dot(rows_ref[...], dh_ref[...], 0, 0).astype(BF16)
    out_ref[:, 0] = grad.reshape(N_SHARD, 48, 768)
    grad = dot(act_ref[...], d_result_ref[...], 0, 0).astype(BF16)
    out_ref[:, 1] = grad.reshape(N_SHARD, 48, 768)


def expert_grad(rows, d_result, active, d_hidden):
    half = pl.BlockSpec((320, 768), lambda i: (0, i))
    return grid_call(
        expert_grad_kernel,
        [shape((N_SHARD, 4, 48, 768), BF16)],
        [pack_block()],
        [rows, d_result, active, d_hidden],
        [whole_block((320, D))] * 2 + [half] * 2,
        "expert_grad",
        2 * 320 * D * FF,
        [],
    )[0]


def combine_kernel(residual_ref, high_ref, low_ref, r0, r1, r2, r3, out_ref, rows_ref):
    for d, ref in enumerate((r0, r1, r2, r3)):
        rows_ref[CAP * d : CAP * (d + 1)] = ref[...]
    rows = rows_ref[...]
    total = residual_ref[...] + dot(high_ref[...], rows, 1, 0) + dot(low_ref[...], rows, 1, 0)
    out_ref[...] = total.astype(BF16)


def combine(residual, high, low, blocks):
    return call(
        combine_kernel,
        [shape((ROWS, D), BF16)],
        [residual, high, low, *blocks],
        "combine",
        4 * ROWS * D * 320,
        scratch=[pltpu.VMEM((320, D), BF16)],
    )[0]


def middle_back_kernel(paired, me_ref, d_out_ref, *refs):
    me = me_ref[0]
    count = 4 if paired else 8
    blocks, refs = refs[:count], refs[count:]
    gathered, refs = refs[:4], refs[4:]
    (
        chosen_ref, gates_ref, residual_ref, normed_ref, gain_ref, w_ref,
        d_residual_ref, small_ref, grad_ref, m0, m1, m2, m3, rows_ref, d_rows_ref, back_ref,
    ) = refs
    for d in range(N_SEQ):
        there = pl.ds(CAP * d, CAP)
        rows_ref[there] = blocks[d][0] if paired else blocks[d][...]
        d_rows_ref[there] = blocks[d][1] if paired else blocks[4 + d][...]
    d_out = d_out_ref[...]
    chosen = chosen_ref[...]
    gates = gates_ref[...]
    products = dot(d_out, rows_ref[...], 1, 1) * chosen.astype(F32)
    slot = lax.broadcasted_iota(jnp.int32, (ROWS, 320), 1)
    own = jnp.where(slot >= 160, jnp.where(slot >= 240, 3, 2), jnp.where(slot >= 80, 1, 0))
    own = lax.rem(own + me, N_SEQ)
    lane = lax.broadcasted_iota(jnp.int32, (ROWS, 128), 1)
    d_gates = jnp.zeros((ROWS, 128), F32)
    for e in range(N_SEQ):
        part = jnp.sum(jnp.where(own == e, products, 0.0), axis=1, keepdims=True)
        d_gates = jnp.where(lane == e, part, d_gates)
    d_logits = gates * (d_gates - jnp.sum(gates * d_gates, axis=1, keepdims=True))
    d_normed = dot(chosen, d_rows_ref[...], 1, 0)
    for e in range(N_SEQ):
        d_normed = d_normed + d_logits[:, e : e + 1] * gain_ref[e : e + 1, :]
    n, inverse = norm_parts(residual_ref[...])
    d_residual = d_out.astype(F32) + norm_back(n, inverse, gain_ref[5:6, :], d_normed)
    d_residual_ref[...] = d_residual
    d_branch = d_residual.astype(BF16)
    for d, ref in enumerate((m0, m1, m2, m3)):
        group = lax.rem(me - d + N_SEQ, N_SEQ)
        ref[...] = dot(d_branch, w_ref[d], 1, 1).astype(BF16)
        back_ref[group] = dot(gathered[d][...], d_branch, 0, 0).astype(BF16)
    grad_ref[...] = by_shard(back_ref[...].reshape(D, D))
    high, low = two_parts(d_logits)
    small = dot(normed_ref[...], high, 0, 0) + dot(normed_ref[...], low, 0, 0)
    column = (lax.broadcasted_iota(jnp.int32, (ROWS, 128), 1) == 5).astype(BF16)
    high, low = two_parts(d_normed * n)
    small = small + dot(high, column, 0, 0) + dot(low, column, 0, 0)
    small_ref[...] = small[:, 0:64]


def middle_back(me, d_out, blocks, gathered, chosen, gates, residual, normed, gains, w_back, paired):
    outs = call(
        partial(middle_back_kernel, paired),
        [
            shape((ROWS, D), F32),
            shape((D, 64), F32),
            shape((D, D), BF16),
        ]
        + [shape((ROWS, 192), BF16)] * 4,
        [me, d_out, *blocks, *gathered, chosen, gates, residual, normed, gains, w_back],
        "middle_back",
        2 * ROWS * D * (2 * D + 640),
        scalars=1,
        scratch=[pltpu.VMEM((320, D), BF16)] * 2 + [pltpu.VMEM((N_SEQ, 192, D), BF16)],
    )
    return *outs[:3], outs[3:]


def finish_kernel(further, d_residual_ref, x_ref, gain_ref, b0, b1, b2, b3, *refs):
    d_normed = b0[...].astype(F32) + b1[...].astype(F32) + b2[...].astype(F32) + b3[...].astype(F32)
    n, inverse = norm_parts(x_ref[...].astype(F32))
    total = d_residual_ref[...] + norm_back(n, inverse, gain_ref[4:5, :], d_normed)
    if not further:
        refs[0][...] = total.astype(BF16)
        return
    high_ref, low_ref, out_ref, *sent = refs
    d_out = total.astype(BF16)
    out_ref[...] = d_out
    rows = dot(high_ref[...], d_out, 0, 0) + dot(low_ref[...], d_out, 0, 0)
    for d in range(N_SEQ):
        sent[d][...] = rows[CAP * d : CAP * (d + 1)].astype(BF16)


def finish(d_residual, x, gains, blocks, weights):
    further = weights is not None
    outs = call(
        partial(finish_kernel, further),
        [shape((ROWS, D), BF16)] + [shape((CAP, D), BF16)] * (4 if further else 0),
        [d_residual, x, gains, *blocks] + (list(weights) if further else []),
        "finish",
        4 * ROWS * D * 320,
    )
    return outs[0], outs[1:]


def attention_weights(where, w_qkv, w_proj, w_route, gain_attn, gain_ffn):
    mine = w_qkv.reshape(12, 3, N_SEQ, 192).transpose(2, 0, 1, 3).reshape(N_SEQ, 12, 576)
    small = jnp.concatenate(
        [w_route, gain_attn[:, None], gain_ffn[:, None], jnp.zeros((12, 58), BF16)], axis=1
    )
    mine = jnp.concatenate([mine, jnp.broadcast_to(small, (N_SEQ, 12, 64))], axis=2)
    arrived = lax.all_to_all(mine, "seq", 0, 0, tiled=True).reshape(48, 640)
    back = w_proj.reshape(12, N_SEQ, 192).transpose(1, 0, 2).reshape(48, 192)
    pack = jnp.concatenate([arrived, back], axis=1)
    near = jnp.stack(from_ring(pack, "x"))
    return unpack(where, from_ring(near, "z"))


def both_layers(mine):
    core = lax.axis_index("section")
    other = swap(mine)
    return [jnp.where(core == s, mine, other) for s in range(2)]


def half_packs(w_in, w_out):
    core = lax.axis_index("section")
    first = w_in.reshape(48, N_SHARD, 4, 48).transpose(2, 0, 1, 3).reshape(4, 48, 768)
    second = w_out.reshape(4, 48, 768)
    quarters = jnp.stack([first, second], axis=1).reshape(2, 4, 48, 768)
    mine = pick(quarters, core)
    arrived = swap(pick(quarters, 1 - core))
    return [jnp.where(core == s, mine, arrived) for s in range(2)]


def join_experts(own, other):
    return (own.astype(F32) + swap(other).astype(F32)).astype(BF16)


def scatter_beside(v):
    return lax.psum_scatter(v, "shard", scatter_dimension=0, tiled=True)[0]


def shards(images_in, out_grad, routes, w_qkv, w_proj, w_route, gain_attn, gain_ffn, w_in, w_out):
    core = lax.axis_index("section")
    me = lax.axis_index("seq").astype(jnp.int32).reshape(1)
    own_routes = routes[0, :, 0]
    mine = pick(own_routes, core)
    arrived = swap(pick(own_routes, 1 - core))
    route_of = (jnp.where(core == 0, mine, arrived), jnp.where(core == 0, arrived, mine))
    x0 = pick(images_in, core)[0]
    d_last = pick(out_grad, core)[0]
    where = where_shard()
    halves = half_packs(w_in[0, 0], w_out[0, 0])
    near_a = jnp.stack(from_ring(halves[0][0:2], "x"))
    near_b = jnp.stack(from_ring(halves[0][2:4], "z"))
    rows, back_rows = attention_weights(
        where, w_qkv[0], w_proj[0], w_route[0], gain_attn[0], gain_ffn[0]
    )
    near_a, near_b, rows = lax.optimization_barrier((near_a, near_b, rows))
    own = order(where, from_ring(near_a, "z"), from_ring(near_b, "x"))
    experts = [(own, swap(own)), None]
    attn_rows = both_layers(rows)
    w_mix = [v[:, :576] for v in attn_rows]
    routers = [jnp.pad(v[:, 576:], ((0, 0), (0, 64))) for v in attn_rows]
    tables = [v[:, 576:584].T.astype(F32) for v in attn_rows]
    w_back = both_layers(jnp.stack([back_rows] + [turn(back_rows, d) for d in (1, 2, 3)]))

    saved = []
    x = x0
    layer_outs = []
    for s in range(2):
        mixture, x_all, packed, logs = attend([x] + [turn(x, -d) for d in (1, 2, 3)], w_mix[s], tables[s])
        if s == 0:
            later = tie(halves[1], (mixture[0], own))
            later = lax.all_gather(later, "shard", axis=0, tiled=False)
        else:
            later = tie(later, mixture[0])
            experts[1] = (later, swap(later))
        gathered = send_out(mixture)
        d_out = d_last if s == 1 else None
        residual, normed, gates, chosen, high, low, buffer = middle(
            me, x, gathered, w_back[s], routers[s], tables[s], route_of[s], d_out
        )
        blocks = send_out(buffer)
        kept = (x, x_all, packed, logs, gathered, residual, normed, gates, chosen, high, low, blocks)
        if s == 0:
            returned = send_back(expert_run(blocks, experts[s]))
            x = combine(residual, high, low, returned)
            layer_outs.append(x)
            saved.append((kept, returned))
        else:
            saved.append((kept, None))

    d_out = d_last
    d_buffer = None
    in_grads = [None, None]
    expert_sums = [None, None]
    attn_grads = [None, None]
    for s in (1, 0):
        kept, returned = saved[s]
        x, x_all, packed, logs, gathered, residual, normed, gates, chosen, high, low, blocks = kept
        if s == 1:
            sent, *states = expert_back(blocks, experts[s], True)
            arrived = send_back(sent)
            first_arrival = arrived[1]
            layer_outs.append(combine(residual, high, low, [v[0] for v in arrived]))
        else:
            sent, *states = expert_back([*blocks, *send_out(d_buffer)], experts[s], False)
            back = send_back(sent)
            first_arrival = back[1]
            arrived = [*returned, *back]
        rows, d_result, act_own, act_other, dh_own, dh_other = states
        if s == 1:
            rows = tie(rows, first_arrival)
        other = swap(expert_grad(rows, d_result, act_other, dh_other))
        d_residual, small, grad_back, d_mixture = middle_back(
            me, d_out, arrived, gathered, chosen, gates, residual, normed, tables[s], w_back[s], s == 1
        )
        d_heads = send_back(d_mixture)
        if s == 1:
            rows = tie(rows, d_heads[1])
        own = expert_grad(rows, d_result, act_own, dh_own)
        if s == 1:
            expert_sums[s] = scatter_beside((own.astype(F32) + other.astype(F32)).astype(BF16))
        else:
            expert_sums[s] = scatter_pair(where, own, other)
            expert_sums[s] = expert_sums[s].reshape(4, 48, D)
        d_normed, grad_mix = attend_back(x_all, w_mix[s], tables[s], packed, logs, d_heads, small)
        d_parts = send_out(d_normed)
        keep = jnp.where(core == 0, grad_mix, grad_back)
        give = jnp.where(core == 0, grad_back, grad_mix)
        attn_grads[s] = (keep.reshape(N_SHARD, 48, D), swap(give).reshape(N_SHARD, 48, D))
        weights = saved[0][0][9:11] if s == 1 else None
        d_out, d_buffer = finish(d_residual, x, tables[s], d_parts, weights)
        in_grads[s] = d_out

    attn_sum = scatter_pair(where, *attn_grads[0], *attn_grads[1])
    attn_sum = attn_sum.reshape(2, N_SEQ, 12, D).transpose(1, 2, 0, 3).reshape(N_SEQ, 12, 2 * D)
    attn_sum = lax.all_to_all(attn_sum, "seq", 0, 0, tiled=True).astype(F32)
    attn_sums = [attn_sum[:, :, :D], attn_sum[:, :, D:]]

    def settle(pair):
        keep = jnp.where(core == 0, pair[0], pair[1])
        give = jnp.where(core == 0, pair[1], pair[0])
        return keep, swap(give)

    def in_order(keep, got):
        return jnp.where(core == 0, jnp.stack([keep, got]), jnp.stack([got, keep]))

    layer_out = in_order(*settle(layer_outs))
    in_grad = in_order(*settle(in_grads))
    expert_sum = in_order(*settle(expert_sums)).astype(F32)
    attn_sum = in_order(*settle(attn_sums))
    quarters = expert_sum.reshape(4, 2, 48, 768)
    grad_in = quarters[:, 0].reshape(4, 48, N_SHARD, 48).transpose(1, 2, 0, 3).reshape(48, FF)
    grad_out = quarters[:, 1].reshape(192, D)
    mix = attn_sum[0]
    back = jnp.sum(attn_sum[1], axis=0)
    grad_qkv = mix[:, :, :576].reshape(N_SEQ, 12, 3, 192).transpose(1, 2, 0, 3).reshape(12, 3 * D)
    small = jnp.sum(mix[:, :, 576:640], axis=0)
    return (
        layer_out[None, :, None],
        in_grad[None, :, None],
        grad_qkv[None],
        back[None],
        small[None, :, 0:4],
        small[None, :, 4],
        small[None, :, 5],
        grad_in[None],
        grad_out[None],
    )


def solution(mesh):
    def run(*args):
        outs = shards(*args)
        outs = list(outs)
        outs[7] = outs[7][:, None]
        outs[8] = outs[8][:, None]
        return tuple(outs)

    return jax.shard_map(
        run,
        mesh=mesh,
        in_specs=(
            P(None, "shard", "seq", None),
            P(None, "shard", "seq", None),
            P("section", None, "shard", "seq", None),
            P("section", ("seq", "shard"), None),
            P("section", ("seq", "shard"), None),
            P("section", ("seq", "shard"), None),
            P("section", ("seq", "shard")),
            P("section", ("seq", "shard")),
            P("section", "seq", "shard", None),
            P("section", "seq", "shard", None),
        ),
        out_specs=(
            P("section", None, "shard", "seq", None),
            P("section", None, "shard", "seq", None),
            P("section", ("seq", "shard"), None),
            P("section", ("seq", "shard"), None),
            P("section", ("seq", "shard"), None),
            P("section", ("seq", "shard")),
            P("section", ("seq", "shard")),
            P("section", "seq", "shard", None),
            P("section", "seq", "shard", None),
        ),
        check_vma=False,
    )
```

```python
from functools import partial

import jax
import jax.numpy as jnp
from jax import lax
from jax.experimental import pallas as pl
from jax.experimental.pallas import tpu as pltpu
from jax.sharding import PartitionSpec as P

D = 768
FF = 3072
HEAD_DIM = 64
CAP = 80
N_SEQ = 4
N_SHARD = 16
GROUP = 3
ROWS = 144
SEQ = 576
WIDE = 1472
LIMIT = 56 * 1024 * 1024
EPSILON = 1e-06
F32 = jnp.float32
BF16 = jnp.bfloat16


def dot(a, b, ca, cb):
    return lax.dot_general(a, b, (((ca,), (cb,)), ((), ())), preferred_element_type=F32)


def swap(v):
    return lax.ppermute(v, "section", [(0, 1), (1, 0)])


def turn(v, d):
    return lax.ppermute(v, "seq", [(i, (i + d) % N_SEQ) for i in range(N_SEQ)])


def pick(v, i):
    return lax.dynamic_index_in_dim(v, i, 0, keepdims=False)


def tie(value, other):
    return lax.optimization_barrier((value, other))[0]


def norm_parts(values):
    centred = values - jnp.mean(values, axis=-1, keepdims=True)
    inverse = lax.rsqrt(jnp.mean(centred * centred, axis=-1, keepdims=True) + EPSILON)
    return centred * inverse, inverse


def norm_back(n, inverse, gain, dy):
    gdy = dy * gain
    return (
        gdy
        - jnp.mean(gdy, axis=-1, keepdims=True)
        - n * jnp.mean(gdy * n, axis=-1, keepdims=True)
    ) * inverse


def two_parts(v):
    high = v.astype(BF16)
    return high, (v - high.astype(F32)).astype(BF16)


def gather_tokens(x):
    return jnp.concatenate([x] + [turn(x, -d) for d in (1, 2, 3)], axis=0)


def send_out(blocks):
    return [blocks[0]] + [turn(blocks[d], d) for d in (1, 2, 3)]


def send_back(blocks):
    return [blocks[0]] + [turn(blocks[d], -d) for d in (1, 2, 3)]


def vmem():
    return pl.BlockSpec(memory_space=pltpu.VMEM)


def smem():
    return pl.BlockSpec(memory_space=pltpu.SMEM)


def shape(dims, kind):
    return jax.ShapeDtypeStruct(dims, kind)


def call(body, outs, ins, name, scalars=0, scratch=()):
    specs = [smem()] * scalars + [vmem()] * (len(ins) - scalars)
    return pl.pallas_call(
        body,
        out_shape=outs,
        in_specs=specs,
        out_specs=[vmem()] * len(outs),
        scratch_shapes=list(scratch),
        name=name,
        compiler_params=pltpu.CompilerParams(vmem_limit_bytes=LIMIT),
    )(*ins)


def attend_kernel(x0, x1, x2, x3, w_ref, gain_ref, m0, m1, m2, m3, x_ref, packed_ref, log_ref):
    for d, ref in enumerate((x0, x1, x2, x3)):
        x_ref[ROWS * d : ROWS * (d + 1)] = ref[...]
    n, _ = norm_parts(x_ref[...].astype(F32))
    normed = (n * gain_ref[4:5, :]).astype(BF16)
    packed_ref[...] = dot(normed, w_ref[...], 1, 0).astype(BF16)
    lane = lax.broadcasted_iota(jnp.int32, (SEQ, 128), 1)
    logs = jnp.zeros((SEQ, 128), F32)
    outs = []
    for h in range(GROUP):
        query = packed_ref[:, 64 * h : 64 * h + 64]
        key = packed_ref[:, 192 + 64 * h : 256 + 64 * h]
        value = packed_ref[:, 384 + 64 * h : 448 + 64 * h]
        scores = dot(query, key, 1, 1) * HEAD_DIM ** (-0.5)
        top = jnp.max(scores, axis=1, keepdims=True)
        exponent = jnp.exp(scores - top)
        total = jnp.sum(exponent, axis=1, keepdims=True)
        outs.append((dot(exponent.astype(BF16), value, 1, 0) / total).astype(BF16))
        logs = jnp.where(lane == h, top + jnp.log(total), logs)
    log_ref[...] = logs
    mixture = jnp.concatenate(outs, axis=1)
    for d, ref in enumerate((m0, m1, m2, m3)):
        ref[...] = mixture[ROWS * d : ROWS * (d + 1)]


def attend(x_blocks, w_mix, gains):
    outs = call(
        attend_kernel,
        [shape((ROWS, 192), BF16)] * 4
        + [shape((SEQ, D), BF16), shape((SEQ, 576), BF16), shape((SEQ, 128), F32)],
        [*x_blocks, w_mix, gains],
        "attention",
    )
    return list(outs[:4]), *outs[4:]


def attend_back_kernel(
    x_ref, w_ref, gain_ref, packed_ref, log_ref, d0, d1, d2, d3, small_ref,
    n0, n1, n2, n3, grad_ref, d_packed_ref, d_mix_ref,
):
    for d, ref in enumerate((d0, d1, d2, d3)):
        d_mix_ref[ROWS * d : ROWS * (d + 1)] = ref[...]
    scaling = HEAD_DIM ** (-0.5)
    parts = [[], [], []]
    for h in range(GROUP):
        query = packed_ref[:, 64 * h : 64 * h + 64]
        key = packed_ref[:, 192 + 64 * h : 256 + 64 * h]
        value = packed_ref[:, 384 + 64 * h : 448 + 64 * h]
        d_out = d_mix_ref[:, 64 * h : 64 * h + 64]
        attention = jnp.exp(dot(query, key, 1, 1) * scaling - log_ref[:, h : h + 1])
        parts[2].append(dot(attention.astype(BF16), d_out, 0, 0).astype(BF16))
        d_att = dot(d_out, value, 1, 1)
        centre = jnp.sum(attention * d_att, axis=1, keepdims=True)
        d_scores = (attention * (d_att - centre) * scaling).astype(BF16)
        parts[0].append(dot(d_scores, key, 1, 0).astype(BF16))
        parts[1].append(dot(d_scores, query, 0, 0).astype(BF16))
    d_packed_ref[...] = jnp.concatenate(parts[0] + parts[1] + parts[2], axis=1)
    n, _ = norm_parts(x_ref[...].astype(F32))
    normed = (n * gain_ref[4:5, :]).astype(BF16)
    d_packed = d_packed_ref[...]
    d_normed = dot(d_packed, w_ref[...], 1, 1)
    for d, ref in enumerate((n0, n1, n2, n3)):
        ref[...] = d_normed[ROWS * d : ROWS * (d + 1)].astype(BF16)
    column = (lax.broadcasted_iota(jnp.int32, (SEQ, 64), 1) == 4).astype(BF16)
    high, low = two_parts(d_normed * n)
    small = small_ref[...] + dot(high, column, 0, 0) + dot(low, column, 0, 0)
    grad = dot(normed, d_packed, 0, 0)
    grad = jnp.concatenate([grad, small, jnp.zeros((D, 128), F32)], axis=1)
    grad_ref[...] = grad.astype(BF16)


def attend_back(x_all, w_mix, gains, packed, logs, d_heads, small):
    outs = call(
        attend_back_kernel,
        [shape((ROWS, D), BF16)] * 4 + [shape((D, D), BF16)],
        [x_all, w_mix, gains, packed, logs, *d_heads, small],
        "attention_back",
        scratch=[pltpu.VMEM((SEQ, 576), BF16), pltpu.VMEM((SEQ, 192), BF16)],
    )
    return outs[:4], outs[4]


def order_rows(first, second):
    i = lax.broadcasted_iota(jnp.int32, (D, 1), 0)
    outer = lax.div(i, 12 * first)
    left = i - 12 * first * outer
    inner = lax.div(left, 12)
    source = inner * (12 * second) + outer * 12 + left - 12 * inner
    return (lax.broadcasted_iota(jnp.int32, (D, D), 1) == source).astype(BF16)


def unpack_kernel(all_ref, rows_ref, back_ref):
    whole = all_ref[...].reshape(D, 832)
    ordered = dot(order_rows(N_SHARD, N_SEQ), whole, 1, 0).astype(BF16)
    rows_ref[...] = ordered[:, :640]
    for chunk in range(N_SEQ):
        back_ref[:, 192 * chunk : 192 * (chunk + 1)] = ordered[192 * chunk : 192 * (chunk + 1), 640:]


def unpack(whole):
    return call(unpack_kernel, [shape((D, 640), BF16), shape((192, D), BF16)], [whole], "unpack")


def middle_kernel(
    extra, me_ref, x_ref, g0, g1, g2, g3, w0, w1, w2, w3, router_ref, gain_ref, route_ref, *refs
):
    me = me_ref[0]
    if extra:
        d_out_ref, *refs = refs
    residual_ref, normed_ref, gates_ref, chosen_ref, high_ref, low_ref, *sent = refs
    residual = x_ref[...].astype(F32)
    for ref, w_ref in zip((g0, g1, g2, g3), (w0, w1, w2, w3)):
        residual = residual + dot(ref[...], w_ref[...], 1, 0)
    residual_ref[...] = residual
    n, _ = norm_parts(residual)
    normed = (n * gain_ref[5:6, :]).astype(BF16)
    normed_ref[...] = normed
    lane = lax.broadcasted_iota(jnp.int32, (ROWS, 128), 1)
    logits = jnp.where(lane < 4, dot(normed, router_ref[...], 1, 0), -1e30)
    logits = logits - jnp.max(logits, axis=1, keepdims=True)
    gates = jnp.exp(logits)
    gates = gates / jnp.sum(gates, axis=1, keepdims=True)
    gates_ref[...] = gates
    routes = route_ref[...]
    relative = lax.rem(routes - me + N_SEQ, N_SEQ)
    named = (lane == relative[:, 0:1]) | (lane == relative[:, 1:2])
    row = lax.broadcasted_iota(jnp.int32, (ROWS, ROWS), 0)
    column = lax.broadcasted_iota(jnp.int32, (ROWS, ROWS), 1)
    before = (row > column).astype(BF16)
    rank = dot(before, named.astype(BF16), 1, 0)
    slot = lax.broadcasted_iota(jnp.int32, (ROWS, 320), 1)
    own = jnp.where(slot >= 160, jnp.where(slot >= 240, 3, 2), jnp.where(slot >= 80, 1, 0))
    place = (slot - CAP * own).astype(F32)
    wanted = jnp.full((ROWS, 320), -1.0, F32)
    spread = jnp.zeros((ROWS, 320), F32)
    position = jnp.where(named, rank, -1.0)
    for e in range(N_SEQ):
        wanted = jnp.where(own == e, position[:, e : e + 1], wanted)
        spread = jnp.where(lax.rem(own + me, N_SEQ) == e, gates[:, e : e + 1], spread)
    taken = wanted == place
    chosen = taken.astype(BF16)
    high, low = two_parts(jnp.where(taken, spread, 0.0))
    chosen_ref[...] = chosen
    high_ref[...] = high
    low_ref[...] = low
    buffer = dot(chosen, normed, 0, 0).astype(BF16)
    if not extra:
        for d in range(N_SEQ):
            sent[d][...] = buffer[CAP * d : CAP * (d + 1)]
    else:
        d_out = d_out_ref[...]
        d_buffer = (dot(high, d_out, 0, 0) + dot(low, d_out, 0, 0)).astype(BF16)
        for d in range(N_SEQ):
            sent[d][0] = buffer[CAP * d : CAP * (d + 1)]
            sent[d][1] = d_buffer[CAP * d : CAP * (d + 1)]


def middle(me, x, gathered, w_back, router, gains, route_ids, d_out):
    extra = d_out is not None
    sent = (2, CAP, D) if extra else (CAP, D)
    outs = call(
        partial(middle_kernel, extra),
        [
            shape((ROWS, D), F32),
            shape((ROWS, D), BF16),
            shape((ROWS, 128), F32),
            shape((ROWS, 320), BF16),
            shape((ROWS, 320), BF16),
            shape((ROWS, 320), BF16),
        ]
        + [shape(sent, BF16)] * 4,
        [me, x, *gathered, *w_back, router, gains, route_ids] + ([d_out] if extra else []),
        "middle",
        scalars=1,
    )
    return *outs[:6], outs[6:]


def gelu_of(hidden):
    cdf = 0.5 + 0.5 * lax.erf(hidden * 0.7071067811865476)
    return hidden * cdf, cdf


def quarter(ref, i):
    return ref[:, i].reshape(768, D)


def expert_kernel(r0, r1, r2, r3, own_ref, other_ref, o0, o1, o2, o3, rows_ref, total):
    @pl.when(pl.program_id(0) == 0)
    def _():
        for d, ref in enumerate((r0, r1, r2, r3)):
            rows_ref[CAP * d : CAP * (d + 1)] = ref[...]
        total[...] = jnp.zeros_like(total)

    rows = rows_ref[...]
    for pack in (own_ref, other_ref):
        hidden = dot(rows, quarter(pack, 0), 1, 0)
        active = gelu_of(hidden)[0].astype(BF16)
        total[...] += dot(active, quarter(pack, 1), 1, 0)

    @pl.when(pl.program_id(0) == 1)
    def _():
        for d, ref in enumerate((o0, o1, o2, o3)):
            ref[...] = total[CAP * d : CAP * (d + 1)].astype(BF16)


def whole_block(dims):
    return pl.BlockSpec(dims, lambda i: (0,) * len(dims))


def pack_block():
    return pl.BlockSpec((N_SHARD, 2, 48, 768), lambda i: (0, i, 0, 0))


def grid_call(body, outs, out_specs, ins, in_specs, name, scratch):
    return pl.pallas_call(
        body,
        grid=(2,),
        out_shape=outs,
        in_specs=in_specs,
        out_specs=out_specs,
        scratch_shapes=scratch,
        name=name,
        compiler_params=pltpu.CompilerParams(
            vmem_limit_bytes=LIMIT, dimension_semantics=("arbitrary",)
        ),
    )(*ins)


def expert_run(blocks, packs):
    return grid_call(
        expert_kernel,
        [shape((CAP, D), BF16)] * 4,
        [whole_block((CAP, D))] * 4,
        [*blocks, *packs],
        [whole_block((CAP, D))] * 4 + [pack_block()] * 2,
        "expert",
        [pltpu.VMEM((320, D), BF16), pltpu.VMEM((320, D), F32)],
    )


def expert_back_kernel(forward, *refs):
    ins, (own_ref, other_ref), refs = refs[: 4 if forward else 8], refs[4 if forward else 8 :][:2], refs[6 if forward else 10 :]
    sent, refs = refs[:4], refs[4:]
    rows_out, d_result_out, act_own, act_other, dh_own, dh_other, d_total, total = refs
    step = pl.program_id(0)

    @pl.when(step == 0)
    def _():
        for d in range(N_SEQ):
            there = pl.ds(CAP * d, CAP)
            rows_out[there] = ins[d][0] if forward else ins[d][...]
            d_result_out[there] = ins[d][1] if forward else ins[4 + d][...]
        d_total[...] = jnp.zeros_like(d_total)
        if forward:
            total[...] = jnp.zeros_like(total)

    rows = rows_out[...]
    d_result = d_result_out[...]
    for pack, act_ref, dh_ref in ((own_ref, act_own, dh_own), (other_ref, act_other, dh_other)):
        hidden = dot(rows, quarter(pack, 0), 1, 0)
        value, cdf = gelu_of(hidden)
        active = value.astype(BF16)
        act_ref[...] = active
        slope = cdf + hidden * jnp.exp(-0.5 * hidden * hidden) * 0.3989422804014327
        d_hidden = (dot(d_result, quarter(pack, 1), 1, 1) * slope).astype(BF16)
        dh_ref[...] = d_hidden
        d_total[...] += dot(d_hidden, quarter(pack, 0), 1, 1)
        if forward:
            total[...] += dot(active, quarter(pack, 1), 1, 0)

    @pl.when(step == 1)
    def _():
        for d in range(N_SEQ):
            there = pl.ds(CAP * d, CAP)
            if forward:
                sent[d][0] = total[there].astype(BF16)
                sent[d][1] = d_total[there].astype(BF16)
            else:
                sent[d][...] = d_total[there].astype(BF16)


def expert_back(blocks, packs, forward):
    half = pl.BlockSpec((320, 768), lambda i: (0, i))
    block = whole_block((2, CAP, D)) if forward else whole_block((CAP, D))
    sent = (2, CAP, D) if forward else (CAP, D)
    outs = grid_call(
        partial(expert_back_kernel, forward),
        [shape(sent, BF16)] * 4 + [shape((320, D), BF16)] * 2 + [shape((320, 1536), BF16)] * 4,
        [whole_block(sent)] * 4 + [whole_block((320, D))] * 2 + [half] * 4,
        [*blocks, *packs],
        [block] * len(blocks) + [pack_block()] * 2,
        "expert_back",
        [pltpu.VMEM((320, D), F32)] * 2,
    )
    return outs[:4], *outs[4:]


def expert_grads_kernel(core_ref, rows_ref, d_result_ref, act_own, dh_own, act_other, dh_other, out_ref):
    for place, act_ref, dh_ref in ((0, act_own, dh_own), (1, act_other, dh_other)):
        @pl.when(pl.program_id(0) == place)
        def _():
            grad = dot(rows_ref[...], dh_ref[...], 0, 0).astype(BF16)
            out_ref[0, :, 0] = grad.reshape(N_SHARD, 48, 768)
            grad = dot(act_ref[...], d_result_ref[...], 0, 0).astype(BF16)
            out_ref[0, :, 1] = grad.reshape(N_SHARD, 48, 768)


def expert_grads(core, rows, d_result, act_own, dh_own, act_other, dh_other):
    whole = pl.BlockSpec((320, D), lambda h, i, c: (0, 0))
    mine = pl.BlockSpec((320, 768), lambda h, i, c: (0, jnp.where(h == 0, i, 1)))
    theirs = pl.BlockSpec((320, 768), lambda h, i, c: (0, jnp.where(h == 0, 0, i)))
    return pl.pallas_call(
        expert_grads_kernel,
        out_shape=shape((2, N_SHARD, 4, 48, D), BF16),
        grid_spec=pltpu.PrefetchScalarGridSpec(
            num_scalar_prefetch=1,
            grid=(2, 2),
            in_specs=[whole, whole, mine, mine, theirs, theirs],
            out_specs=pl.BlockSpec(
                (1, N_SHARD, 2, 48, D), lambda h, i, c: (jnp.where(h == 0, c[0], 1 - c[0]), 0, i, 0, 0)
            ),
        ),
        name="expert_grads",
        compiler_params=pltpu.CompilerParams(
            vmem_limit_bytes=LIMIT, dimension_semantics=("arbitrary", "arbitrary")
        ),
    )(core, rows, d_result, act_own, dh_own, act_other, dh_other)


def combine_kernel(residual_ref, high_ref, low_ref, r0, r1, r2, r3, out_ref, rows_ref):
    for d, ref in enumerate((r0, r1, r2, r3)):
        rows_ref[CAP * d : CAP * (d + 1)] = ref[...]
    rows = rows_ref[...]
    total = residual_ref[...] + dot(high_ref[...], rows, 1, 0) + dot(low_ref[...], rows, 1, 0)
    out_ref[...] = total.astype(BF16)


def combine(residual, high, low, blocks):
    return call(
        combine_kernel,
        [shape((ROWS, D), BF16)],
        [residual, high, low, *blocks],
        "combine",
        scratch=[pltpu.VMEM((320, D), BF16)],
    )[0]


def middle_back_kernel(paired, me_ref, d_out_ref, *refs):
    me = me_ref[0]
    count = 4 if paired else 8
    blocks, refs = refs[:count], refs[count:]
    gathered, refs = refs[:4], refs[4:]
    (
        chosen_ref, gates_ref, residual_ref, normed_ref, gain_ref, w0, w1, w2, w3,
        d_residual_ref, small_ref, grad_ref, m0, m1, m2, m3, rows_ref, d_rows_ref, back_ref,
    ) = refs
    for d in range(N_SEQ):
        there = pl.ds(CAP * d, CAP)
        rows_ref[there] = blocks[d][0] if paired else blocks[d][...]
        d_rows_ref[there] = blocks[d][1] if paired else blocks[4 + d][...]
    d_out = d_out_ref[...]
    chosen = chosen_ref[...]
    gates = gates_ref[...]
    products = dot(d_out, rows_ref[...], 1, 1) * chosen.astype(F32)
    slot = lax.broadcasted_iota(jnp.int32, (ROWS, 320), 1)
    own = jnp.where(slot >= 160, jnp.where(slot >= 240, 3, 2), jnp.where(slot >= 80, 1, 0))
    own = lax.rem(own + me, N_SEQ)
    lane = lax.broadcasted_iota(jnp.int32, (ROWS, 128), 1)
    d_gates = jnp.zeros((ROWS, 128), F32)
    for e in range(N_SEQ):
        part = jnp.sum(jnp.where(own == e, products, 0.0), axis=1, keepdims=True)
        d_gates = jnp.where(lane == e, part, d_gates)
    d_logits = gates * (d_gates - jnp.sum(gates * d_gates, axis=1, keepdims=True))
    d_normed = dot(chosen, d_rows_ref[...], 1, 0)
    for e in range(N_SEQ):
        d_normed = d_normed + d_logits[:, e : e + 1] * gain_ref[e : e + 1, :]
    n, inverse = norm_parts(residual_ref[...])
    d_residual = d_out.astype(F32) + norm_back(n, inverse, gain_ref[5:6, :], d_normed)
    d_residual_ref[...] = d_residual
    d_branch = d_residual.astype(BF16)
    for d, (ref, w_ref) in enumerate(zip((m0, m1, m2, m3), (w0, w1, w2, w3))):
        group = lax.rem(me - d + N_SEQ, N_SEQ)
        ref[...] = dot(d_branch, w_ref[...], 1, 1).astype(BF16)
        back_ref[group] = dot(gathered[d][...], d_branch, 0, 0).astype(BF16)
    grad_ref[...] = back_ref[...].reshape(D, D)
    high, low = two_parts(d_logits)
    small = dot(normed_ref[...], high, 0, 0) + dot(normed_ref[...], low, 0, 0)
    column = (lax.broadcasted_iota(jnp.int32, (ROWS, 128), 1) == 5).astype(BF16)
    high, low = two_parts(d_normed * n)
    small = small + dot(high, column, 0, 0) + dot(low, column, 0, 0)
    small_ref[...] = small[:, 0:64]


def middle_back(me, d_out, blocks, gathered, chosen, gates, residual, normed, gains, w_back, paired):
    outs = call(
        partial(middle_back_kernel, paired),
        [
            shape((ROWS, D), F32),
            shape((D, 64), F32),
            shape((D, D), BF16),
        ]
        + [shape((ROWS, 192), BF16)] * 4,
        [me, d_out, *blocks, *gathered, chosen, gates, residual, normed, gains, *w_back],
        "middle_back",
        scalars=1,
        scratch=[pltpu.VMEM((320, D), BF16)] * 2 + [pltpu.VMEM((N_SEQ, 192, D), BF16)],
    )
    return *outs[:3], outs[3:]


def finish_kernel(further, d_residual_ref, x_ref, gain_ref, b0, b1, b2, b3, *refs):
    d_normed = b0[...].astype(F32) + b1[...].astype(F32) + b2[...].astype(F32) + b3[...].astype(F32)
    n, inverse = norm_parts(x_ref[...].astype(F32))
    total = d_residual_ref[...] + norm_back(n, inverse, gain_ref[4:5, :], d_normed)
    if not further:
        refs[0][...] = total.astype(BF16)
        return
    high_ref, low_ref, out_ref, *sent = refs
    d_out = total.astype(BF16)
    out_ref[...] = d_out
    rows = dot(high_ref[...], d_out, 0, 0) + dot(low_ref[...], d_out, 0, 0)
    for d in range(N_SEQ):
        sent[d][...] = rows[CAP * d : CAP * (d + 1)].astype(BF16)


def finish(d_residual, x, gains, blocks, weights):
    further = weights is not None
    outs = call(
        partial(finish_kernel, further),
        [shape((ROWS, D), BF16)] + [shape((CAP, D), BF16)] * (4 if further else 0),
        [d_residual, x, gains, *blocks] + (list(weights) if further else []),
        "finish",
    )
    return outs[0], outs[1:]


def attention_weights(w_qkv, w_proj, w_route, gain_attn, gain_ffn):
    mine = w_qkv.reshape(12, 3, N_SEQ, 192).transpose(2, 0, 1, 3).reshape(N_SEQ, 12, 576)
    small = jnp.concatenate(
        [w_route, gain_attn[:, None], gain_ffn[:, None], jnp.zeros((12, 58), BF16)], axis=1
    )
    mine = jnp.concatenate([mine, jnp.broadcast_to(small, (N_SEQ, 12, 64))], axis=2)
    arrived = lax.all_to_all(mine, "seq", 0, 0, tiled=True).reshape(48, 640)
    back = w_proj.reshape(12, N_SEQ, 192).transpose(1, 0, 2).reshape(48, 192)
    pack = jnp.concatenate([arrived, back], axis=1)
    whole = lax.all_gather(pack, "shard", axis=0, tiled=False)
    return whole, *unpack(whole)


def both_layers(mine):
    core = lax.axis_index("section")
    other = swap(mine)
    return [jnp.where(core == s, mine, other) for s in range(2)]


def half_packs(w_in, w_out):
    core = lax.axis_index("section")
    first = w_in.reshape(48, N_SHARD, 4, 48).transpose(2, 0, 1, 3).reshape(4, 48, 768)
    second = w_out.reshape(4, 48, 768)
    quarters = jnp.stack([first, second], axis=1).reshape(2, 4, 48, 768)
    mine = pick(quarters, core)
    arrived = swap(pick(quarters, 1 - core))
    return [jnp.where(core == s, mine, arrived) for s in range(2)]


def shards(images_in, out_grad, routes, w_qkv, w_proj, w_route, gain_attn, gain_ffn, w_in, w_out):
    core = lax.axis_index("section")
    me = lax.axis_index("seq").astype(jnp.int32).reshape(1)
    core_index = core.astype(jnp.int32).reshape(1)
    own_routes = routes[0, :, 0]
    mine = pick(own_routes, core)
    arrived = swap(pick(own_routes, 1 - core))
    route_of = (jnp.where(core == 0, mine, arrived), jnp.where(core == 0, arrived, mine))
    x0 = pick(images_in, core)[0]
    d_last = pick(out_grad, core)[0]
    halves = half_packs(w_in[0, 0], w_out[0, 0])
    whole, rows, back_rows = attention_weights(
        w_qkv[0], w_proj[0], w_route[0], gain_attn[0], gain_ffn[0]
    )
    own = lax.all_gather(tie(halves[0], whole), "shard", axis=0, tiled=False)
    x_blocks = [x0] + [turn(x0, -d) for d in (1, 2, 3)]
    attn_rows = both_layers(rows)
    back_rows = both_layers(back_rows)
    attn_rows[0], attn_rows[1], back_rows[0], back_rows[1] = lax.optimization_barrier(
        (attn_rows[0], attn_rows[1], back_rows[0], back_rows[1])
    )
    w_mix = [v[:, :576] for v in attn_rows]
    routers = [jnp.pad(v[:, 576:], ((0, 0), (0, 64))) for v in attn_rows]
    tables = [v[:, 576:584].T.astype(F32) for v in attn_rows]
    w_back = [[back_rows[0]] + [turn(back_rows[0], d) for d in (1, 2, 3)], None]
    experts = [None, None]

    saved = []
    x = x0
    layer_outs = []
    for s in range(2):
        if s == 1:
            x_blocks = [x] + [turn(x, -d) for d in (1, 2, 3)]
        mixture, x_all, packed, logs = attend(x_blocks, w_mix[s], tables[s])
        if s == 0:
            w_back[0], mixture = lax.optimization_barrier((w_back[0], mixture))
        else:
            later, mixture[0] = lax.optimization_barrier((later, mixture[0]))
            experts[1] = (later, swap(later))
        gathered = send_out(mixture)
        d_out = d_last if s == 1 else None
        residual, normed, gates, chosen, high, low, buffer = middle(
            me, x, gathered, w_back[s], routers[s], tables[s], route_of[s], d_out
        )
        blocks = send_out(buffer)
        kept = (x, x_all, packed, logs, gathered, residual, normed, gates, chosen, high, low, blocks)
        if s == 0:
            own, blocks[1] = lax.optimization_barrier((own, blocks[1]))
            experts[0] = (own, swap(own))
            later = lax.all_gather(tie(halves[1], own), "shard", axis=0, tiled=False)
            later_back = tie(back_rows[1], blocks[1])
            w_back[1] = [later_back] + [turn(later_back, d) for d in (1, 2, 3)]
            result = expert_run(blocks, experts[s])
            w_back[1], result = lax.optimization_barrier((w_back[1], result))
            returned = send_back(result)
            x = combine(residual, high, low, returned)
            layer_outs.append(x)
            saved.append((kept, returned))
        else:
            saved.append((kept, None))

    d_out = d_last
    d_buffer = None
    in_grads = [None, None]
    expert_sums = [None, None]
    attn_grads = [None, None]
    for s in (1, 0):
        kept, returned = saved[s]
        x, x_all, packed, logs, gathered, residual, normed, gates, chosen, high, low, blocks = kept
        if s == 1:
            sent, *states = expert_back(blocks, experts[s], True)
            arrived = send_back(sent)
            layer_outs.append(combine(residual, high, low, [v[0] for v in arrived]))
        else:
            sent, *states = expert_back([*blocks, *send_out(d_buffer)], experts[s], False)
            arrived = [*returned, *send_back(sent)]
        d_residual, small, grad_back, d_mixture = middle_back(
            me, d_out, arrived, gathered, chosen, gates, residual, normed, tables[s], w_back[s], s == 1
        )
        d_heads = send_back(d_mixture)
        rows, d_result, act_own, act_other, dh_own, dh_other = states
        if s == 1:
            rows = tie(rows, d_residual)
        both = expert_grads(core_index, rows, d_result, act_own, dh_own, act_other, dh_other)
        both = both.reshape(2 * N_SHARD, 4, 48, D)
        expert_sums[s] = lax.psum_scatter(both, ("section", "shard"), scatter_dimension=0, tiled=True)[0]
        d_normed, grad_mix = attend_back(x_all, w_mix[s], tables[s], packed, logs, d_heads, small)
        d_parts = send_out(d_normed)
        keep = jnp.where(core == 0, grad_mix, grad_back)
        give = jnp.where(core == 0, grad_back, grad_mix)
        attn_grads[s] = (keep.astype(F32) + swap(give).astype(F32)).astype(BF16)
        weights = saved[0][0][9:11] if s == 1 else None
        d_out, d_buffer = finish(d_residual, x, tables[s], d_parts, weights)
        in_grads[s] = d_out

    pair = jnp.concatenate(attn_grads, axis=1).reshape(N_SEQ * N_SHARD, 12, 2 * D)
    pair = tie(pair, d_parts)
    arrived = lax.all_to_all(pair, ("seq", "shard"), 0, 0, tiled=True)
    attn_sum = jnp.sum(arrived.reshape(N_SEQ, N_SHARD, 12, 2 * D).astype(F32), axis=1)
    attn_sums = [attn_sum[:, :, :D], attn_sum[:, :, D:]]

    def settle(pair):
        keep = jnp.where(core == 0, pair[0], pair[1])
        give = jnp.where(core == 0, pair[1], pair[0])
        return keep, swap(give)

    def in_order(keep, got):
        return jnp.where(core == 0, jnp.stack([keep, got]), jnp.stack([got, keep]))

    layer_out = in_order(*settle(layer_outs))
    in_grad = in_order(*settle(in_grads))
    expert_sum = in_order(*settle(expert_sums)).astype(F32)
    attn_sum = in_order(*settle(attn_sums))
    quarters = expert_sum.reshape(4, 2, 48, 768)
    grad_in = quarters[:, 0].reshape(4, 48, N_SHARD, 48).transpose(1, 2, 0, 3).reshape(48, FF)
    grad_out = quarters[:, 1].reshape(192, D)
    mix = attn_sum[0]
    back = jnp.sum(attn_sum[1], axis=0)
    grad_qkv = mix[:, :, :576].reshape(N_SEQ, 12, 3, 192).transpose(1, 2, 0, 3).reshape(12, 3 * D)
    small = jnp.sum(mix[:, :, 576:640], axis=0)
    return (
        layer_out[None, :, None],
        in_grad[None, :, None],
        grad_qkv[None],
        back[None],
        small[None, :, 0:4],
        small[None, :, 4],
        small[None, :, 5],
        grad_in[None],
        grad_out[None],
    )


def solution(mesh):
    def run(*args):
        outs = shards(*args)
        outs = list(outs)
        outs[7] = outs[7][:, None]
        outs[8] = outs[8][:, None]
        return tuple(outs)

    return jax.shard_map(
        run,
        mesh=mesh,
        in_specs=(
            P(None, "shard", "seq", None),
            P(None, "shard", "seq", None),
            P("section", None, "shard", "seq", None),
            P("section", ("seq", "shard"), None),
            P("section", ("seq", "shard"), None),
            P("section", ("seq", "shard"), None),
            P("section", ("seq", "shard")),
            P("section", ("seq", "shard")),
            P("section", "seq", "shard", None),
            P("section", "seq", "shard", None),
        ),
        out_specs=(
            P("section", None, "shard", "seq", None),
            P("section", None, "shard", "seq", None),
            P("section", ("seq", "shard"), None),
            P("section", ("seq", "shard"), None),
            P("section", ("seq", "shard"), None),
            P("section", ("seq", "shard")),
            P("section", ("seq", "shard")),
            P("section", "seq", "shard", None),
            P("section", "seq", "shard", None),
        ),
        check_vma=False,
    )
```

```python
from functools import partial

import jax
import jax.numpy as jnp
from jax import lax
from jax.experimental import pallas as pl
from jax.experimental.pallas import tpu as pltpu
from jax.sharding import PartitionSpec as P

D = 768
FF = 3072
HEAD_DIM = 64
CAP = 80
N_SEQ = 4
N_SHARD = 16
GROUP = 3
ROWS = 144
SEQ = 576
WIDE = 1472
LIMIT = 56 * 1024 * 1024
EPSILON = 1e-06
F32 = jnp.float32
BF16 = jnp.bfloat16


def dot(a, b, ca, cb):
    return lax.dot_general(a, b, (((ca,), (cb,)), ((), ())), preferred_element_type=F32)


def swap(v):
    return lax.ppermute(v, "section", [(0, 1), (1, 0)])


def turn(v, d):
    return lax.ppermute(v, "seq", [(i, (i + d) % N_SEQ) for i in range(N_SEQ)])


def hop(v, axis, d):
    route = []
    for z in range(4):
        for x in range(4):
            to = ((z + d) % 4) * 4 + x if axis == "z" else z * 4 + (x + d) % 4
            route.append((z * 4 + x, to))
    return lax.ppermute(v, "shard", route)


def from_ring(v, axis):
    return [v] + [hop(v, axis, -d) for d in (1, 2, 3)]


def pick(v, i):
    return lax.dynamic_index_in_dim(v, i, 0, keepdims=False)


def tie(value, other):
    return lax.optimization_barrier((value, other))[0]


def norm_parts(values):
    centred = values - jnp.mean(values, axis=-1, keepdims=True)
    inverse = lax.rsqrt(jnp.mean(centred * centred, axis=-1, keepdims=True) + EPSILON)
    return centred * inverse, inverse


def norm_back(n, inverse, gain, dy):
    gdy = dy * gain
    return (
        gdy
        - jnp.mean(gdy, axis=-1, keepdims=True)
        - n * jnp.mean(gdy * n, axis=-1, keepdims=True)
    ) * inverse


def two_parts(v):
    high = v.astype(BF16)
    return high, (v - high.astype(F32)).astype(BF16)


def gather_tokens(x):
    return jnp.concatenate([x] + [turn(x, -d) for d in (1, 2, 3)], axis=0)


def send_out(blocks):
    return [blocks[0]] + [turn(blocks[d], d) for d in (1, 2, 3)]


def send_back(blocks):
    return [blocks[0]] + [turn(blocks[d], -d) for d in (1, 2, 3)]


def vmem():
    return pl.BlockSpec(memory_space=pltpu.VMEM)


def smem():
    return pl.BlockSpec(memory_space=pltpu.SMEM)


def shape(dims, kind):
    return jax.ShapeDtypeStruct(dims, kind)


def call(body, outs, ins, name, scalars=0, scratch=()):
    specs = [smem()] * scalars + [vmem()] * (len(ins) - scalars)
    return pl.pallas_call(
        body,
        out_shape=outs,
        in_specs=specs,
        out_specs=[vmem()] * len(outs),
        scratch_shapes=list(scratch),
        name=name,
        compiler_params=pltpu.CompilerParams(vmem_limit_bytes=LIMIT),
    )(*ins)


def attend_kernel(x0, x1, x2, x3, w_ref, gain_ref, m0, m1, m2, m3, x_ref, packed_ref, log_ref):
    for d, ref in enumerate((x0, x1, x2, x3)):
        x_ref[ROWS * d : ROWS * (d + 1)] = ref[...]
    n, _ = norm_parts(x_ref[...].astype(F32))
    normed = (n * gain_ref[4:5, :]).astype(BF16)
    packed_ref[...] = dot(normed, w_ref[...], 1, 0).astype(BF16)
    lane = lax.broadcasted_iota(jnp.int32, (SEQ, 128), 1)
    logs = jnp.zeros((SEQ, 128), F32)
    outs = []
    for h in range(GROUP):
        query = packed_ref[:, 64 * h : 64 * h + 64]
        key = packed_ref[:, 192 + 64 * h : 256 + 64 * h]
        value = packed_ref[:, 384 + 64 * h : 448 + 64 * h]
        scores = dot(query, key, 1, 1) * HEAD_DIM ** (-0.5)
        top = jnp.max(scores, axis=1, keepdims=True)
        exponent = jnp.exp(scores - top)
        total = jnp.sum(exponent, axis=1, keepdims=True)
        outs.append((dot(exponent.astype(BF16), value, 1, 0) / total).astype(BF16))
        logs = jnp.where(lane == h, top + jnp.log(total), logs)
    log_ref[...] = logs
    mixture = jnp.concatenate(outs, axis=1)
    for d, ref in enumerate((m0, m1, m2, m3)):
        ref[...] = mixture[ROWS * d : ROWS * (d + 1)]


def attend(x_blocks, w_mix, gains):
    outs = call(
        attend_kernel,
        [shape((ROWS, 192), BF16)] * 4
        + [shape((SEQ, D), BF16), shape((SEQ, 576), BF16), shape((SEQ, 128), F32)],
        [*x_blocks, w_mix, gains],
        "attention",
    )
    return list(outs[:4]), *outs[4:]


def attend_back_kernel(
    x_ref, w_ref, gain_ref, packed_ref, log_ref, d0, d1, d2, d3, small_ref,
    n0, n1, n2, n3, grad_ref, d_packed_ref, d_mix_ref,
):
    for d, ref in enumerate((d0, d1, d2, d3)):
        d_mix_ref[ROWS * d : ROWS * (d + 1)] = ref[...]
    scaling = HEAD_DIM ** (-0.5)
    parts = [[], [], []]
    for h in range(GROUP):
        query = packed_ref[:, 64 * h : 64 * h + 64]
        key = packed_ref[:, 192 + 64 * h : 256 + 64 * h]
        value = packed_ref[:, 384 + 64 * h : 448 + 64 * h]
        d_out = d_mix_ref[:, 64 * h : 64 * h + 64]
        attention = jnp.exp(dot(query, key, 1, 1) * scaling - log_ref[:, h : h + 1])
        parts[2].append(dot(attention.astype(BF16), d_out, 0, 0).astype(BF16))
        d_att = dot(d_out, value, 1, 1)
        centre = jnp.sum(attention * d_att, axis=1, keepdims=True)
        d_scores = (attention * (d_att - centre) * scaling).astype(BF16)
        parts[0].append(dot(d_scores, key, 1, 0).astype(BF16))
        parts[1].append(dot(d_scores, query, 0, 0).astype(BF16))
    d_packed_ref[...] = jnp.concatenate(parts[0] + parts[1] + parts[2], axis=1)
    n, _ = norm_parts(x_ref[...].astype(F32))
    normed = (n * gain_ref[4:5, :]).astype(BF16)
    d_packed = d_packed_ref[...]
    d_normed = dot(d_packed, w_ref[...], 1, 1)
    for d, ref in enumerate((n0, n1, n2, n3)):
        ref[...] = d_normed[ROWS * d : ROWS * (d + 1)].astype(BF16)
    column = (lax.broadcasted_iota(jnp.int32, (SEQ, 64), 1) == 4).astype(BF16)
    high, low = two_parts(d_normed * n)
    small = small_ref[...] + dot(high, column, 0, 0) + dot(low, column, 0, 0)
    grad = dot(normed, d_packed, 0, 0)
    grad = jnp.concatenate([grad, small, jnp.zeros((D, 128), F32)], axis=1)
    grad_ref[...] = grad.astype(BF16)


def attend_back(x_all, w_mix, gains, packed, logs, d_heads, small):
    outs = call(
        attend_back_kernel,
        [shape((ROWS, D), BF16)] * 4 + [shape((D, D), BF16)],
        [x_all, w_mix, gains, packed, logs, *d_heads, small],
        "attention_back",
        scratch=[pltpu.VMEM((SEQ, 576), BF16), pltpu.VMEM((SEQ, 192), BF16)],
    )
    return outs[:4], outs[4]


def order_rows(first, second):
    i = lax.broadcasted_iota(jnp.int32, (D, 1), 0)
    outer = lax.div(i, 12 * first)
    left = i - 12 * first * outer
    inner = lax.div(left, 12)
    source = inner * (12 * second) + outer * 12 + left - 12 * inner
    return (lax.broadcasted_iota(jnp.int32, (D, D), 1) == source).astype(BF16)


def unpack_kernel(where_ref, b0, b1, b2, b3, rows_ref, back_ref, all_ref):
    z, x = where_ref[0], where_ref[1]
    for dz, ref in enumerate((b0, b1, b2, b3)):
        for dx in range(4):
            all_ref[lax.rem(z + dz, 4) * 4 + lax.rem(x + dx, 4)] = ref[dx]
    whole = all_ref[...].reshape(D, 832)
    ordered = dot(order_rows(N_SHARD, N_SEQ), whole, 1, 0).astype(BF16)
    rows_ref[...] = ordered[:, :640]
    for chunk in range(N_SEQ):
        back_ref[:, 192 * chunk : 192 * (chunk + 1)] = ordered[192 * chunk : 192 * (chunk + 1), 640:]


def unpack(blocks):
    i = lax.axis_index("shard").astype(jnp.int32)
    return call(
        unpack_kernel,
        [shape((D, 640), BF16), shape((192, D), BF16)],
        [jnp.stack([i // 4, lax.rem(i, 4)]), *blocks],
        "unpack",
        scalars=1,
        scratch=[pltpu.VMEM((N_SHARD, 48, 832), BF16)],
    )


def reorder_kernel(core_ref, keep_ref, got_ref, in_ref, out_ref):
    def write(halves):
        columns = []
        for shard in range(N_SHARD):
            for p in range(4):
                block = halves[p // 2][2 * (p % 2)]
                columns.append(block[:, 48 * shard : 48 * (shard + 1)])
        in_ref[...] = jnp.concatenate(columns, axis=1).astype(F32)
        for p in range(4):
            out_ref[48 * p : 48 * (p + 1)] = halves[p // 2][2 * (p % 2) + 1].astype(F32)

    @pl.when(core_ref[0] == 0)
    def _():
        write((keep_ref, got_ref))

    @pl.when(core_ref[0] == 1)
    def _():
        write((got_ref, keep_ref))


def reorder(core, keep, got):
    return call(
        reorder_kernel,
        [shape((48, FF), F32), shape((192, D), F32)],
        [core, keep, got],
        "reorder",
        scalars=1,
    )


def middle_kernel(
    layer, me_ref, x_ref, g0, g1, g2, g3, w0, w1, w2, w3, router_ref, gain_ref, route_ref, *refs
):
    me = me_ref[0]
    extra = layer == 1
    if extra:
        d_out_ref, *refs = refs
    residual_ref, normed_ref, gates_ref, chosen_ref, high_ref, low_ref, *sent = refs
    residual = x_ref[...].astype(F32)
    for ref, w_ref in zip((g0, g1, g2, g3), (w0, w1, w2, w3)):
        residual = residual + dot(ref[...], w_ref[layer], 1, 0)
    residual_ref[...] = residual
    n, _ = norm_parts(residual)
    normed = (n * gain_ref[5:6, :]).astype(BF16)
    normed_ref[...] = normed
    lane = lax.broadcasted_iota(jnp.int32, (ROWS, 128), 1)
    logits = jnp.where(lane < 4, dot(normed, router_ref[...], 1, 0), -1e30)
    logits = logits - jnp.max(logits, axis=1, keepdims=True)
    gates = jnp.exp(logits)
    gates = gates / jnp.sum(gates, axis=1, keepdims=True)
    gates_ref[...] = gates
    routes = route_ref[...]
    relative = lax.rem(routes - me + N_SEQ, N_SEQ)
    named = (lane == relative[:, 0:1]) | (lane == relative[:, 1:2])
    row = lax.broadcasted_iota(jnp.int32, (ROWS, ROWS), 0)
    column = lax.broadcasted_iota(jnp.int32, (ROWS, ROWS), 1)
    before = (row > column).astype(BF16)
    rank = dot(before, named.astype(BF16), 1, 0)
    slot = lax.broadcasted_iota(jnp.int32, (ROWS, 320), 1)
    own = jnp.where(slot >= 160, jnp.where(slot >= 240, 3, 2), jnp.where(slot >= 80, 1, 0))
    place = (slot - CAP * own).astype(F32)
    wanted = jnp.full((ROWS, 320), -1.0, F32)
    spread = jnp.zeros((ROWS, 320), F32)
    position = jnp.where(named, rank, -1.0)
    for e in range(N_SEQ):
        wanted = jnp.where(own == e, position[:, e : e + 1], wanted)
        spread = jnp.where(lax.rem(own + me, N_SEQ) == e, gates[:, e : e + 1], spread)
    taken = wanted == place
    chosen = taken.astype(BF16)
    high, low = two_parts(jnp.where(taken, spread, 0.0))
    chosen_ref[...] = chosen
    high_ref[...] = high
    low_ref[...] = low
    buffer = dot(chosen, normed, 0, 0).astype(BF16)
    if not extra:
        for d in range(N_SEQ):
            sent[d][...] = buffer[CAP * d : CAP * (d + 1)]
    else:
        d_out = d_out_ref[...]
        d_buffer = (dot(high, d_out, 0, 0) + dot(low, d_out, 0, 0)).astype(BF16)
        for d in range(N_SEQ):
            sent[d][0] = buffer[CAP * d : CAP * (d + 1)]
            sent[d][1] = d_buffer[CAP * d : CAP * (d + 1)]


def middle(me, x, gathered, w_back, router, gains, route_ids, d_out):
    extra = d_out is not None
    sent = (2, CAP, D) if extra else (CAP, D)
    outs = call(
        partial(middle_kernel, int(extra)),
        [
            shape((ROWS, D), F32),
            shape((ROWS, D), BF16),
            shape((ROWS, 128), F32),
            shape((ROWS, 320), BF16),
            shape((ROWS, 320), BF16),
            shape((ROWS, 320), BF16),
        ]
        + [shape(sent, BF16)] * 4,
        [me, x, *gathered, *w_back, router, gains, route_ids] + ([d_out] if extra else []),
        "middle",
        scalars=1,
    )
    return *outs[:6], outs[6:]


def gelu_of(hidden):
    cdf = 0.5 + 0.5 * lax.erf(hidden * 0.7071067811865476)
    return hidden * cdf, cdf


def quarter(ref, i):
    return ref[:, i].reshape(768, D)


def expert_kernel(r0, r1, r2, r3, own_ref, other_ref, o0, o1, o2, o3, rows_ref, total):
    @pl.when(pl.program_id(0) == 0)
    def _():
        for d, ref in enumerate((r0, r1, r2, r3)):
            rows_ref[CAP * d : CAP * (d + 1)] = ref[...]
        total[...] = jnp.zeros_like(total)

    rows = rows_ref[...]
    for pack in (own_ref, other_ref):
        hidden = dot(rows, quarter(pack, 0), 1, 0)
        active = gelu_of(hidden)[0].astype(BF16)
        total[...] += dot(active, quarter(pack, 1), 1, 0)

    @pl.when(pl.program_id(0) == 1)
    def _():
        for d, ref in enumerate((o0, o1, o2, o3)):
            ref[...] = total[CAP * d : CAP * (d + 1)].astype(BF16)


def whole_block(dims):
    return pl.BlockSpec(dims, lambda i: (0,) * len(dims))


def pack_block():
    return pl.BlockSpec((N_SHARD, 2, 48, 768), lambda i: (0, i, 0, 0))


def grid_call(body, outs, out_specs, ins, in_specs, name, scratch):
    return pl.pallas_call(
        body,
        grid=(2,),
        out_shape=outs,
        in_specs=in_specs,
        out_specs=out_specs,
        scratch_shapes=scratch,
        name=name,
        compiler_params=pltpu.CompilerParams(
            vmem_limit_bytes=LIMIT, dimension_semantics=("arbitrary",)
        ),
    )(*ins)


def expert_run(blocks, packs):
    return grid_call(
        expert_kernel,
        [shape((CAP, D), BF16)] * 4,
        [whole_block((CAP, D))] * 4,
        [*blocks, *packs],
        [whole_block((CAP, D))] * 4 + [pack_block()] * 2,
        "expert",
        [pltpu.VMEM((320, D), BF16), pltpu.VMEM((320, D), F32)],
    )


def expert_back_kernel(forward, *refs):
    ins, (own_ref, other_ref), refs = refs[: 4 if forward else 8], refs[4 if forward else 8 :][:2], refs[6 if forward else 10 :]
    sent, refs = refs[:4], refs[4:]
    rows_out, d_result_out, act_own, act_other, dh_own, dh_other, d_total, total = refs
    step = pl.program_id(0)

    @pl.when(step == 0)
    def _():
        for d in range(N_SEQ):
            there = pl.ds(CAP * d, CAP)
            rows_out[there] = ins[d][0] if forward else ins[d][...]
            d_result_out[there] = ins[d][1] if forward else ins[4 + d][...]
        d_total[...] = jnp.zeros_like(d_total)
        if forward:
            total[...] = jnp.zeros_like(total)

    rows = rows_out[...]
    d_result = d_result_out[...]
    for pack, act_ref, dh_ref in ((own_ref, act_own, dh_own), (other_ref, act_other, dh_other)):
        hidden = dot(rows, quarter(pack, 0), 1, 0)
        value, cdf = gelu_of(hidden)
        active = value.astype(BF16)
        act_ref[...] = active
        slope = cdf + hidden * jnp.exp(-0.5 * hidden * hidden) * 0.3989422804014327
        d_hidden = (dot(d_result, quarter(pack, 1), 1, 1) * slope).astype(BF16)
        dh_ref[...] = d_hidden
        d_total[...] += dot(d_hidden, quarter(pack, 0), 1, 1)
        if forward:
            total[...] += dot(active, quarter(pack, 1), 1, 0)

    @pl.when(step == 1)
    def _():
        for d in range(N_SEQ):
            there = pl.ds(CAP * d, CAP)
            if forward:
                sent[d][0] = total[there].astype(BF16)
                sent[d][1] = d_total[there].astype(BF16)
            else:
                sent[d][...] = d_total[there].astype(BF16)


def expert_back(blocks, packs, forward):
    half = pl.BlockSpec((320, 768), lambda i: (0, i))
    block = whole_block((2, CAP, D)) if forward else whole_block((CAP, D))
    sent = (2, CAP, D) if forward else (CAP, D)
    outs = grid_call(
        partial(expert_back_kernel, forward),
        [shape(sent, BF16)] * 4 + [shape((320, D), BF16)] * 2 + [shape((320, 1536), BF16)] * 4,
        [whole_block(sent)] * 4 + [whole_block((320, D))] * 2 + [half] * 4,
        [*blocks, *packs],
        [block] * len(blocks) + [pack_block()] * 2,
        "expert_back",
        [pltpu.VMEM((320, D), F32)] * 2,
    )
    return outs[:4], *outs[4:]


def expert_grads_kernel(
    core_ref, rows_ref, d_result_ref, act_own, dh_own, act_other, dh_other, out_ref, turned_ref
):
    @pl.when((pl.program_id(0) == 0) & (pl.program_id(1) == 0))
    def _():
        turned_ref[...] = rows_ref[...].T

    for place, act_ref, dh_ref in ((0, act_own, dh_own), (1, act_other, dh_other)):
        @pl.when(pl.program_id(0) == place)
        def _():
            grad = dot(turned_ref[...], dh_ref[...], 1, 0).astype(BF16)
            out_ref[0, :, 0] = grad.reshape(N_SHARD, 48, 768)
            grad = dot(act_ref[...], d_result_ref[...], 0, 0).astype(BF16)
            out_ref[0, :, 1] = grad.reshape(N_SHARD, 48, 768)


def expert_grads(core, rows, d_result, act_own, dh_own, act_other, dh_other):
    whole = pl.BlockSpec((320, D), lambda h, i, c: (0, 0))
    mine = pl.BlockSpec((320, 768), lambda h, i, c: (0, jnp.where(h == 0, i, 1)))
    theirs = pl.BlockSpec((320, 768), lambda h, i, c: (0, jnp.where(h == 0, 0, i)))
    return pl.pallas_call(
        expert_grads_kernel,
        out_shape=shape((2, N_SHARD, 4, 48, D), BF16),
        grid_spec=pltpu.PrefetchScalarGridSpec(
            num_scalar_prefetch=1,
            grid=(2, 2),
            in_specs=[whole, whole, mine, mine, theirs, theirs],
            out_specs=pl.BlockSpec(
                (1, N_SHARD, 2, 48, D), lambda h, i, c: (jnp.where(h == 0, c[0], 1 - c[0]), 0, i, 0, 0)
            ),
            scratch_shapes=[pltpu.VMEM((D, 320), BF16)],
        ),
        name="expert_grads",
        compiler_params=pltpu.CompilerParams(
            vmem_limit_bytes=LIMIT, dimension_semantics=("arbitrary", "arbitrary")
        ),
    )(core, rows, d_result, act_own, dh_own, act_other, dh_other)


def combine_kernel(residual_ref, high_ref, low_ref, r0, r1, r2, r3, out_ref, rows_ref):
    for d, ref in enumerate((r0, r1, r2, r3)):
        rows_ref[CAP * d : CAP * (d + 1)] = ref[...]
    rows = rows_ref[...]
    total = residual_ref[...] + dot(high_ref[...], rows, 1, 0) + dot(low_ref[...], rows, 1, 0)
    out_ref[...] = total.astype(BF16)


def combine(residual, high, low, blocks):
    return call(
        combine_kernel,
        [shape((ROWS, D), BF16)],
        [residual, high, low, *blocks],
        "combine",
        scratch=[pltpu.VMEM((320, D), BF16)],
    )[0]


def middle_back_kernel(paired, me_ref, d_out_ref, *refs):
    me = me_ref[0]
    count = 4 if paired else 8
    blocks, refs = refs[:count], refs[count:]
    gathered, refs = refs[:4], refs[4:]
    (
        chosen_ref, gates_ref, residual_ref, normed_ref, gain_ref, w0, w1, w2, w3,
        d_residual_ref, small_ref, grad_ref, m0, m1, m2, m3, rows_ref, d_rows_ref, back_ref,
    ) = refs
    for d in range(N_SEQ):
        there = pl.ds(CAP * d, CAP)
        rows_ref[there] = blocks[d][0] if paired else blocks[d][...]
        d_rows_ref[there] = blocks[d][1] if paired else blocks[4 + d][...]
    d_out = d_out_ref[...]
    chosen = chosen_ref[...]
    gates = gates_ref[...]
    products = dot(d_out, rows_ref[...], 1, 1) * chosen.astype(F32)
    slot = lax.broadcasted_iota(jnp.int32, (ROWS, 320), 1)
    own = jnp.where(slot >= 160, jnp.where(slot >= 240, 3, 2), jnp.where(slot >= 80, 1, 0))
    own = lax.rem(own + me, N_SEQ)
    lane = lax.broadcasted_iota(jnp.int32, (ROWS, 128), 1)
    d_gates = jnp.zeros((ROWS, 128), F32)
    for e in range(N_SEQ):
        part = jnp.sum(jnp.where(own == e, products, 0.0), axis=1, keepdims=True)
        d_gates = jnp.where(lane == e, part, d_gates)
    d_logits = gates * (d_gates - jnp.sum(gates * d_gates, axis=1, keepdims=True))
    d_normed = dot(chosen, d_rows_ref[...], 1, 0)
    for e in range(N_SEQ):
        d_normed = d_normed + d_logits[:, e : e + 1] * gain_ref[e : e + 1, :]
    n, inverse = norm_parts(residual_ref[...])
    d_residual = d_out.astype(F32) + norm_back(n, inverse, gain_ref[5:6, :], d_normed)
    d_residual_ref[...] = d_residual
    d_branch = d_residual.astype(BF16)
    for d, (ref, w_ref) in enumerate(zip((m0, m1, m2, m3), (w0, w1, w2, w3))):
        group = lax.rem(me - d + N_SEQ, N_SEQ)
        ref[...] = dot(d_branch, w_ref[int(paired)], 1, 1).astype(BF16)
        back_ref[group] = dot(gathered[d][...], d_branch, 0, 0).astype(BF16)
    grad_ref[...] = back_ref[...].reshape(D, D)
    high, low = two_parts(d_logits)
    small = dot(normed_ref[...], high, 0, 0) + dot(normed_ref[...], low, 0, 0)
    column = (lax.broadcasted_iota(jnp.int32, (ROWS, 128), 1) == 5).astype(BF16)
    high, low = two_parts(d_normed * n)
    small = small + dot(high, column, 0, 0) + dot(low, column, 0, 0)
    small_ref[...] = small[:, 0:64]


def middle_back(me, d_out, blocks, gathered, chosen, gates, residual, normed, gains, w_back, paired):
    outs = call(
        partial(middle_back_kernel, paired),
        [
            shape((ROWS, D), F32),
            shape((D, 64), F32),
            shape((D, D), BF16),
        ]
        + [shape((ROWS, 192), BF16)] * 4,
        [me, d_out, *blocks, *gathered, chosen, gates, residual, normed, gains, *w_back],
        "middle_back",
        scalars=1,
        scratch=[pltpu.VMEM((320, D), BF16)] * 2 + [pltpu.VMEM((N_SEQ, 192, D), BF16)],
    )
    return *outs[:3], outs[3:]


def finish_kernel(further, d_residual_ref, x_ref, gain_ref, b0, b1, b2, b3, *refs):
    d_normed = b0[...].astype(F32) + b1[...].astype(F32) + b2[...].astype(F32) + b3[...].astype(F32)
    n, inverse = norm_parts(x_ref[...].astype(F32))
    total = d_residual_ref[...] + norm_back(n, inverse, gain_ref[4:5, :], d_normed)
    if not further:
        refs[0][...] = total.astype(BF16)
        return
    high_ref, low_ref, out_ref, *sent = refs
    d_out = total.astype(BF16)
    out_ref[...] = d_out
    rows = dot(high_ref[...], d_out, 0, 0) + dot(low_ref[...], d_out, 0, 0)
    for d in range(N_SEQ):
        sent[d][...] = rows[CAP * d : CAP * (d + 1)].astype(BF16)


def finish(d_residual, x, gains, blocks, weights):
    further = weights is not None
    outs = call(
        partial(finish_kernel, further),
        [shape((ROWS, D), BF16)] + [shape((CAP, D), BF16)] * (4 if further else 0),
        [d_residual, x, gains, *blocks] + (list(weights) if further else []),
        "finish",
    )
    return outs[0], outs[1:]


def attention_weights(x_blocks, w_qkv, w_proj, w_route, gain_attn, gain_ffn):
    mine = w_qkv.reshape(12, 3, N_SEQ, 192).transpose(2, 0, 1, 3).reshape(N_SEQ, 12, 576)
    small = jnp.concatenate(
        [w_route, gain_attn[:, None], gain_ffn[:, None], jnp.zeros((12, 58), BF16)], axis=1
    )
    mine = jnp.concatenate([mine, jnp.broadcast_to(small, (N_SEQ, 12, 64))], axis=2)
    arrived = lax.all_to_all(mine, "seq", 0, 0, tiled=True).reshape(48, 640)
    back = w_proj.reshape(12, N_SEQ, 192).transpose(1, 0, 2).reshape(48, 192)
    pack = jnp.concatenate([arrived, back], axis=1)
    near = jnp.stack(from_ring(tie(pack, x_blocks), "x"))
    far = from_ring(near, "z")
    return far, *unpack(far)


def both_layers(mine):
    core = lax.axis_index("section")
    other = swap(mine)
    return [jnp.where(core == s, mine, other) for s in range(2)]


def half_packs(w_in, w_out):
    core = lax.axis_index("section")
    first = w_in.reshape(48, N_SHARD, 4, 48).transpose(2, 0, 1, 3).reshape(4, 48, 768)
    second = w_out.reshape(4, 48, 768)
    quarters = jnp.stack([first, second], axis=1).reshape(2, 4, 48, 768)
    mine = pick(quarters, core)
    arrived = swap(pick(quarters, 1 - core))
    return [jnp.where(core == s, mine, arrived) for s in range(2)]


def shards(images_in, out_grad, routes, w_qkv, w_proj, w_route, gain_attn, gain_ffn, w_in, w_out):
    core = lax.axis_index("section")
    me = lax.axis_index("seq").astype(jnp.int32).reshape(1)
    core_index = core.astype(jnp.int32).reshape(1)
    own_routes = routes[0, :, 0]
    mine = pick(own_routes, core)
    arrived = swap(pick(own_routes, 1 - core))
    route_of = (jnp.where(core == 0, mine, arrived), jnp.where(core == 0, arrived, mine))
    x0 = pick(images_in, core)[0]
    d_last = pick(out_grad, core)[0]
    halves = half_packs(w_in[0, 0], w_out[0, 0])
    x_blocks = [x0] + [turn(x0, -d) for d in (1, 2, 3)]
    far, rows, back_rows = attention_weights(
        x_blocks, w_qkv[0], w_proj[0], w_route[0], gain_attn[0], gain_ffn[0]
    )
    own = lax.all_gather(tie(halves[0], far), "shard", axis=0, tiled=False)
    attn_rows = both_layers(rows)
    back_rows = both_layers(back_rows)
    attn_rows[0], attn_rows[1], back_rows[0], back_rows[1] = lax.optimization_barrier(
        (attn_rows[0], attn_rows[1], back_rows[0], back_rows[1])
    )
    w_mix = [v[:, :576] for v in attn_rows]
    routers = [jnp.pad(v[:, 576:], ((0, 0), (0, 64))) for v in attn_rows]
    tables = [v[:, 576:584].T.astype(F32) for v in attn_rows]
    back_rows = jnp.stack(back_rows)
    w_back = [back_rows] + [turn(back_rows, d) for d in (1, 2, 3)]
    experts = [None, None]

    saved = []
    x = x0
    layer_outs = []
    for s in range(2):
        if s == 1:
            x_blocks = [x] + [turn(x, -d) for d in (1, 2, 3)]
        mixture, x_all, packed, logs = attend(x_blocks, w_mix[s], tables[s])
        if s == 0:
            w_back, mixture = lax.optimization_barrier((w_back, mixture))
        else:
            later, mixture[0] = lax.optimization_barrier((later, mixture[0]))
            experts[1] = (later, swap(later))
        gathered = send_out(mixture)
        d_out = d_last if s == 1 else None
        residual, normed, gates, chosen, high, low, buffer = middle(
            me, x, gathered, w_back, routers[s], tables[s], route_of[s], d_out
        )
        blocks = send_out(buffer)
        kept = (x, x_all, packed, logs, gathered, residual, normed, gates, chosen, high, low, blocks)
        if s == 0:
            own, blocks[1] = lax.optimization_barrier((own, blocks[1]))
            experts[0] = (own, swap(own))
            later = lax.all_gather(tie(halves[1], own), "shard", axis=0, tiled=False)
            returned = send_back(expert_run(blocks, experts[s]))
            x = combine(residual, high, low, returned)
            layer_outs.append(x)
            saved.append((kept, returned))
        else:
            saved.append((kept, None))

    d_out = d_last
    d_buffer = None
    in_grads = [None, None]
    expert_sums = [None, None]
    attn_grads = [None, None]
    for s in (1, 0):
        kept, returned = saved[s]
        x, x_all, packed, logs, gathered, residual, normed, gates, chosen, high, low, blocks = kept
        if s == 1:
            sent, *states = expert_back(blocks, experts[s], True)
            arrived = send_back(sent)
            layer_outs.append(combine(residual, high, low, [v[0] for v in arrived]))
        else:
            sent, *states = expert_back([*blocks, *send_out(d_buffer)], experts[s], False)
            arrived = [*returned, *send_back(sent)]
        d_residual, small, grad_back, d_mixture = middle_back(
            me, d_out, arrived, gathered, chosen, gates, residual, normed, tables[s], w_back, s == 1
        )
        d_heads = send_back(d_mixture)
        rows, d_result, act_own, act_other, dh_own, dh_other = states
        both = expert_grads(core_index, rows, d_result, act_own, dh_own, act_other, dh_other)
        both = both.reshape(2 * N_SHARD, 4, 48, D)
        expert_sums[s] = lax.psum_scatter(both, ("section", "shard"), scatter_dimension=0, tiled=True)[0]
        d_normed, grad_mix = attend_back(x_all, w_mix[s], tables[s], packed, logs, d_heads, small)
        d_parts = send_out(d_normed)
        keep = jnp.where(core == 0, grad_mix, grad_back)
        give = jnp.where(core == 0, grad_back, grad_mix)
        attn_grads[s] = (keep.astype(F32) + swap(give).astype(F32)).astype(BF16)
        weights = saved[0][0][9:11] if s == 1 else None
        d_out, d_buffer = finish(d_residual, x, tables[s], d_parts, weights)
        in_grads[s] = d_out

    pair = jnp.concatenate(attn_grads, axis=1).reshape(N_SEQ * N_SHARD, 12, 2 * D)
    pair = tie(pair, d_parts)
    arrived = lax.all_to_all(pair, ("seq", "shard"), 0, 0, tiled=True)
    attn_sum = jnp.sum(arrived.reshape(N_SEQ, N_SHARD, 12, 2 * D).astype(F32), axis=1)
    attn_sums = [attn_sum[:, :, :D], attn_sum[:, :, D:]]

    def settle(pair):
        keep = jnp.where(core == 0, pair[0], pair[1])
        give = jnp.where(core == 0, pair[1], pair[0])
        return keep, swap(give)

    def in_order(keep, got):
        return jnp.where(core == 0, jnp.stack([keep, got]), jnp.stack([got, keep]))

    layer_out = in_order(*settle(layer_outs))
    in_grad = in_order(*settle(in_grads))
    grad_in, grad_out = reorder(core_index, *settle(expert_sums))
    attn_sum = in_order(*settle(attn_sums))
    mix = attn_sum[0]
    back = jnp.sum(attn_sum[1], axis=0)
    grad_qkv = mix[:, :, :576].reshape(N_SEQ, 12, 3, 192).transpose(1, 2, 0, 3).reshape(12, 3 * D)
    small = jnp.sum(mix[:, :, 576:640], axis=0)
    return (
        layer_out[None, :, None],
        in_grad[None, :, None],
        grad_qkv[None],
        back[None],
        small[None, :, 0:4],
        small[None, :, 4],
        small[None, :, 5],
        grad_in[None],
        grad_out[None],
    )


def solution(mesh):
    def run(*args):
        outs = shards(*args)
        outs = list(outs)
        outs[7] = outs[7][:, None]
        outs[8] = outs[8][:, None]
        return tuple(outs)

    return jax.shard_map(
        run,
        mesh=mesh,
        in_specs=(
            P(None, "shard", "seq", None),
            P(None, "shard", "seq", None),
            P("section", None, "shard", "seq", None),
            P("section", ("seq", "shard"), None),
            P("section", ("seq", "shard"), None),
            P("section", ("seq", "shard"), None),
            P("section", ("seq", "shard")),
            P("section", ("seq", "shard")),
            P("section", "seq", "shard", None),
            P("section", "seq", "shard", None),
        ),
        out_specs=(
            P("section", None, "shard", "seq", None),
            P("section", None, "shard", "seq", None),
            P("section", ("seq", "shard"), None),
            P("section", ("seq", "shard"), None),
            P("section", ("seq", "shard"), None),
            P("section", ("seq", "shard")),
            P("section", ("seq", "shard")),
            P("section", "seq", "shard", None),
            P("section", "seq", "shard", None),
        ),
        check_vma=False,
    )
```

```python
from functools import partial

import jax
import jax.numpy as jnp
from jax import lax
from jax.experimental import pallas as pl
from jax.experimental.pallas import tpu as pltpu
from jax.sharding import PartitionSpec as P

D = 768
FF = 3072
HEAD_DIM = 64
CAP = 80
N_SEQ = 4
N_SHARD = 16
GROUP = 3
ROWS = 144
SEQ = 576
WIDE = 1472
LIMIT = 56 * 1024 * 1024
EPSILON = 1e-06
F32 = jnp.float32
BF16 = jnp.bfloat16


def dot(a, b, ca, cb):
    return lax.dot_general(a, b, (((ca,), (cb,)), ((), ())), preferred_element_type=F32)


def swap(v):
    return lax.ppermute(v, "section", [(0, 1), (1, 0)])


def turn(v, d):
    return lax.ppermute(v, "seq", [(i, (i + d) % N_SEQ) for i in range(N_SEQ)])


def hop(v, axis, d):
    route = []
    for z in range(4):
        for x in range(4):
            to = ((z + d) % 4) * 4 + x if axis == "z" else z * 4 + (x + d) % 4
            route.append((z * 4 + x, to))
    return lax.ppermute(v, "shard", route)


def from_ring(v, axis):
    return [v] + [hop(v, axis, -d) for d in (1, 2, 3)]


def pick(v, i):
    return lax.dynamic_index_in_dim(v, i, 0, keepdims=False)


def tie(value, other):
    return lax.optimization_barrier((value, other))[0]


def norm_parts(values):
    centred = values - jnp.mean(values, axis=-1, keepdims=True)
    inverse = lax.rsqrt(jnp.mean(centred * centred, axis=-1, keepdims=True) + EPSILON)
    return centred * inverse, inverse


def norm_back(n, inverse, gain, dy):
    gdy = dy * gain
    return (
        gdy
        - jnp.mean(gdy, axis=-1, keepdims=True)
        - n * jnp.mean(gdy * n, axis=-1, keepdims=True)
    ) * inverse


def two_parts(v):
    high = v.astype(BF16)
    return high, (v - high.astype(F32)).astype(BF16)


def gather_tokens(x):
    return jnp.concatenate([x] + [turn(x, -d) for d in (1, 2, 3)], axis=0)


def send_out(blocks):
    return [blocks[0]] + [turn(blocks[d], d) for d in (1, 2, 3)]


def send_back(blocks):
    return [blocks[0]] + [turn(blocks[d], -d) for d in (1, 2, 3)]


def vmem():
    return pl.BlockSpec(memory_space=pltpu.VMEM)


def smem():
    return pl.BlockSpec(memory_space=pltpu.SMEM)


def shape(dims, kind):
    return jax.ShapeDtypeStruct(dims, kind)


def call(body, outs, ins, name, scalars=0, scratch=()):
    specs = [smem()] * scalars + [vmem()] * (len(ins) - scalars)
    return pl.pallas_call(
        body,
        out_shape=outs,
        in_specs=specs,
        out_specs=[vmem()] * len(outs),
        scratch_shapes=list(scratch),
        name=name,
        compiler_params=pltpu.CompilerParams(vmem_limit_bytes=LIMIT),
    )(*ins)


def attend_kernel(x0, x1, x2, x3, w_ref, gain_ref, m0, m1, m2, m3, x_ref, packed_ref, log_ref):
    for d, ref in enumerate((x0, x1, x2, x3)):
        x_ref[ROWS * d : ROWS * (d + 1)] = ref[...]
    n, _ = norm_parts(x_ref[...].astype(F32))
    normed = (n * gain_ref[4:5, :]).astype(BF16)
    packed_ref[...] = dot(normed, w_ref[:, 0:576], 1, 0).astype(BF16)
    lane = lax.broadcasted_iota(jnp.int32, (SEQ, 128), 1)
    logs = jnp.zeros((SEQ, 128), F32)
    outs = []
    for h in range(GROUP):
        query = packed_ref[:, 64 * h : 64 * h + 64]
        key = packed_ref[:, 192 + 64 * h : 256 + 64 * h]
        value = packed_ref[:, 384 + 64 * h : 448 + 64 * h]
        scores = dot(query, key, 1, 1) * HEAD_DIM ** (-0.5)
        top = jnp.max(scores, axis=1, keepdims=True)
        exponent = jnp.exp(scores - top)
        total = jnp.sum(exponent, axis=1, keepdims=True)
        outs.append((dot(exponent.astype(BF16), value, 1, 0) / total).astype(BF16))
        logs = jnp.where(lane == h, top + jnp.log(total), logs)
    log_ref[...] = logs
    mixture = jnp.concatenate(outs, axis=1)
    for d, ref in enumerate((m0, m1, m2, m3)):
        ref[...] = mixture[ROWS * d : ROWS * (d + 1)]


def attend(x_blocks, w_mix, gains):
    outs = call(
        attend_kernel,
        [shape((ROWS, 192), BF16)] * 4
        + [shape((SEQ, D), BF16), shape((SEQ, 576), BF16), shape((SEQ, 128), F32)],
        [*x_blocks, w_mix, gains],
        "attention",
    )
    return list(outs[:4]), *outs[4:]


def attend_back_kernel(
    x_ref, w_ref, gain_ref, packed_ref, log_ref, d0, d1, d2, d3, small_ref,
    n0, n1, n2, n3, grad_ref, d_packed_ref, d_mix_ref,
):
    for d, ref in enumerate((d0, d1, d2, d3)):
        d_mix_ref[ROWS * d : ROWS * (d + 1)] = ref[...]
    scaling = HEAD_DIM ** (-0.5)
    parts = [[], [], []]
    for h in range(GROUP):
        query = packed_ref[:, 64 * h : 64 * h + 64]
        key = packed_ref[:, 192 + 64 * h : 256 + 64 * h]
        value = packed_ref[:, 384 + 64 * h : 448 + 64 * h]
        d_out = d_mix_ref[:, 64 * h : 64 * h + 64]
        attention = jnp.exp(dot(query, key, 1, 1) * scaling - log_ref[:, h : h + 1])
        parts[2].append(dot(attention.astype(BF16), d_out, 0, 0).astype(BF16))
        d_att = dot(d_out, value, 1, 1)
        centre = jnp.sum(attention * d_att, axis=1, keepdims=True)
        d_scores = (attention * (d_att - centre) * scaling).astype(BF16)
        parts[0].append(dot(d_scores, key, 1, 0).astype(BF16))
        parts[1].append(dot(d_scores, query, 0, 0).astype(BF16))
    d_packed_ref[...] = jnp.concatenate(parts[0] + parts[1] + parts[2], axis=1)
    n, _ = norm_parts(x_ref[...].astype(F32))
    normed = (n * gain_ref[4:5, :]).astype(BF16)
    d_packed = d_packed_ref[...]
    d_normed = dot(d_packed, w_ref[:, 0:576], 1, 1)
    for d, ref in enumerate((n0, n1, n2, n3)):
        ref[...] = d_normed[ROWS * d : ROWS * (d + 1)].astype(BF16)
    column = (lax.broadcasted_iota(jnp.int32, (SEQ, 64), 1) == 4).astype(BF16)
    high, low = two_parts(d_normed * n)
    small = small_ref[...] + dot(high, column, 0, 0) + dot(low, column, 0, 0)
    grad = dot(normed, d_packed, 0, 0)
    grad = jnp.concatenate([grad, small, jnp.zeros((D, 128), F32)], axis=1)
    grad_ref[...] = grad.astype(BF16)


def attend_back(x_all, w_mix, gains, packed, logs, d_heads, small):
    outs = call(
        attend_back_kernel,
        [shape((ROWS, D), BF16)] * 4 + [shape((D, D), BF16)],
        [x_all, w_mix, gains, packed, logs, *d_heads, small],
        "attention_back",
        scratch=[pltpu.VMEM((SEQ, 576), BF16), pltpu.VMEM((SEQ, 192), BF16)],
    )
    return outs[:4], outs[4]


def order_rows(first, second):
    i = lax.broadcasted_iota(jnp.int32, (D, 1), 0)
    outer = lax.div(i, 12 * first)
    left = i - 12 * first * outer
    inner = lax.div(left, 12)
    source = inner * (12 * second) + outer * 12 + left - 12 * inner
    return (lax.broadcasted_iota(jnp.int32, (D, D), 1) == source).astype(BF16)


def unpack_kernel(where_ref, b0, b1, b2, b3, rows_ref, back_ref, all_ref):
    z, x = where_ref[0], where_ref[1]
    for dz, ref in enumerate((b0, b1, b2, b3)):
        for dx in range(4):
            all_ref[lax.rem(z + dz, 4) * 4 + lax.rem(x + dx, 4)] = ref[dx]
    whole = all_ref[...].reshape(D, 832)
    ordered = dot(order_rows(N_SHARD, N_SEQ), whole, 1, 0).astype(BF16)
    rows_ref[...] = ordered[:, :640]
    for chunk in range(N_SEQ):
        back_ref[:, 192 * chunk : 192 * (chunk + 1)] = ordered[192 * chunk : 192 * (chunk + 1), 640:]


def unpack(blocks):
    i = lax.axis_index("shard").astype(jnp.int32)
    return call(
        unpack_kernel,
        [shape((D, 640), BF16), shape((192, D), BF16)],
        [jnp.stack([i // 4, lax.rem(i, 4)]), *blocks],
        "unpack",
        scalars=1,
        scratch=[pltpu.VMEM((N_SHARD, 48, 832), BF16)],
    )


def reorder_kernel(core_ref, keep_ref, got_ref, in_ref, out_ref):
    def write(halves):
        columns = []
        for shard in range(N_SHARD):
            for p in range(4):
                block = halves[p // 2][2 * (p % 2)]
                columns.append(block[:, 48 * shard : 48 * (shard + 1)])
        in_ref[...] = jnp.concatenate(columns, axis=1).astype(F32)
        for p in range(4):
            out_ref[48 * p : 48 * (p + 1)] = halves[p // 2][2 * (p % 2) + 1].astype(F32)

    @pl.when(core_ref[0] == 0)
    def _():
        write((keep_ref, got_ref))

    @pl.when(core_ref[0] == 1)
    def _():
        write((got_ref, keep_ref))


def reorder(core, keep, got):
    return call(
        reorder_kernel,
        [shape((48, FF), F32), shape((192, D), F32)],
        [core, keep, got],
        "reorder",
        scalars=1,
    )


def middle_kernel(
    layer, me_ref, x_ref, g0, g1, g2, g3, w0, w1, w2, w3, router_ref, gain_ref, route_ref, *refs
):
    me = me_ref[0]
    extra = layer == 1
    if extra:
        d_out_ref, *refs = refs
    residual_ref, normed_ref, gates_ref, chosen_ref, high_ref, low_ref, *sent = refs
    residual = x_ref[...].astype(F32)
    for ref, w_ref in zip((g0, g1, g2, g3), (w0, w1, w2, w3)):
        residual = residual + dot(ref[...], w_ref[...], 1, 0)
    residual_ref[...] = residual
    n, _ = norm_parts(residual)
    normed = (n * gain_ref[5:6, :]).astype(BF16)
    normed_ref[...] = normed
    lane = lax.broadcasted_iota(jnp.int32, (ROWS, 64), 1)
    logits = jnp.where(lane < 4, dot(normed, router_ref[:, 576:640], 1, 0), -1e30)
    logits = logits - jnp.max(logits, axis=1, keepdims=True)
    gates = jnp.exp(logits)
    gates = gates / jnp.sum(gates, axis=1, keepdims=True)
    gates_ref[...] = gates
    routes = route_ref[...]
    relative = lax.rem(routes - me + N_SEQ, N_SEQ)
    named = (lane == relative[:, 0:1]) | (lane == relative[:, 1:2])
    row = lax.broadcasted_iota(jnp.int32, (ROWS, ROWS), 0)
    column = lax.broadcasted_iota(jnp.int32, (ROWS, ROWS), 1)
    before = (row > column).astype(BF16)
    rank = dot(before, named.astype(BF16), 1, 0)
    slot = lax.broadcasted_iota(jnp.int32, (ROWS, 320), 1)
    own = jnp.where(slot >= 160, jnp.where(slot >= 240, 3, 2), jnp.where(slot >= 80, 1, 0))
    place = (slot - CAP * own).astype(F32)
    wanted = jnp.full((ROWS, 320), -1.0, F32)
    spread = jnp.zeros((ROWS, 320), F32)
    position = jnp.where(named, rank, -1.0)
    for e in range(N_SEQ):
        wanted = jnp.where(own == e, position[:, e : e + 1], wanted)
        spread = jnp.where(lax.rem(own + me, N_SEQ) == e, gates[:, e : e + 1], spread)
    taken = wanted == place
    chosen = taken.astype(BF16)
    high, low = two_parts(jnp.where(taken, spread, 0.0))
    chosen_ref[...] = chosen
    high_ref[...] = high
    low_ref[...] = low
    buffer = dot(chosen, normed, 0, 0).astype(BF16)
    if not extra:
        for d in range(N_SEQ):
            sent[d][...] = buffer[CAP * d : CAP * (d + 1)]
    else:
        d_out = d_out_ref[...]
        d_buffer = (dot(high, d_out, 0, 0) + dot(low, d_out, 0, 0)).astype(BF16)
        for d in range(N_SEQ):
            sent[d][0] = buffer[CAP * d : CAP * (d + 1)]
            sent[d][1] = d_buffer[CAP * d : CAP * (d + 1)]


def middle(me, x, gathered, w_back, router, gains, route_ids, d_out):
    extra = d_out is not None
    sent = (2, CAP, D) if extra else (CAP, D)
    outs = call(
        partial(middle_kernel, int(extra)),
        [
            shape((ROWS, D), F32),
            shape((ROWS, D), BF16),
            shape((ROWS, 64), F32),
            shape((ROWS, 320), BF16),
            shape((ROWS, 320), BF16),
            shape((ROWS, 320), BF16),
        ]
        + [shape(sent, BF16)] * 4,
        [me, x, *gathered, *w_back, router, gains, route_ids] + ([d_out] if extra else []),
        "middle",
        scalars=1,
    )
    return *outs[:6], outs[6:]


def gelu_of(hidden):
    cdf = 0.5 + 0.5 * lax.erf(hidden * 0.7071067811865476)
    return hidden * cdf, cdf


def quarter(ref, i):
    return ref[:, i].reshape(768, D)


def expert_kernel(r0, r1, r2, r3, own_ref, other_ref, o0, o1, o2, o3, rows_ref, total):
    @pl.when(pl.program_id(0) == 0)
    def _():
        for d, ref in enumerate((r0, r1, r2, r3)):
            rows_ref[CAP * d : CAP * (d + 1)] = ref[...]
        total[...] = jnp.zeros_like(total)

    rows = rows_ref[...]
    for pack in (own_ref, other_ref):
        hidden = dot(rows, quarter(pack, 0), 1, 0)
        active = gelu_of(hidden)[0].astype(BF16)
        total[...] += dot(active, quarter(pack, 1), 1, 0)

    @pl.when(pl.program_id(0) == 1)
    def _():
        for d, ref in enumerate((o0, o1, o2, o3)):
            ref[...] = total[CAP * d : CAP * (d + 1)].astype(BF16)


def whole_block(dims):
    return pl.BlockSpec(dims, lambda i: (0,) * len(dims))


def pack_block():
    return pl.BlockSpec((N_SHARD, 2, 48, 768), lambda i: (0, i, 0, 0))


def grid_call(body, outs, out_specs, ins, in_specs, name, scratch):
    return pl.pallas_call(
        body,
        grid=(2,),
        out_shape=outs,
        in_specs=in_specs,
        out_specs=out_specs,
        scratch_shapes=scratch,
        name=name,
        compiler_params=pltpu.CompilerParams(
            vmem_limit_bytes=LIMIT, dimension_semantics=("arbitrary",)
        ),
    )(*ins)


def expert_run(blocks, packs):
    return grid_call(
        expert_kernel,
        [shape((CAP, D), BF16)] * 4,
        [whole_block((CAP, D))] * 4,
        [*blocks, *packs],
        [whole_block((CAP, D))] * 4 + [pack_block()] * 2,
        "expert",
        [pltpu.VMEM((320, D), BF16), pltpu.VMEM((320, D), F32)],
    )


def expert_back_kernel(forward, me_ref, *refs):
    me = me_ref[0]
    ins, (own_ref, other_ref), refs = refs[: 4 if forward else 8], refs[4 if forward else 8 :][:2], refs[6 if forward else 10 :]
    sent, refs = (refs[0], refs[1:]) if forward else (refs[:4], refs[4:])
    rows_out, d_result_out, act_own, act_other, dh_own, dh_other, d_total, total = refs
    step = pl.program_id(0)

    @pl.when(step == 0)
    def _():
        for d in range(N_SEQ):
            there = pl.ds(CAP * d, CAP)
            rows_out[there] = ins[d][0] if forward else ins[d][...]
            d_result_out[there] = ins[d][1] if forward else ins[4 + d][...]
        d_total[...] = jnp.zeros_like(d_total)
        if forward:
            total[...] = jnp.zeros_like(total)

    rows = rows_out[...]
    d_result = d_result_out[...]
    for pack, act_ref, dh_ref in ((own_ref, act_own, dh_own), (other_ref, act_other, dh_other)):
        hidden = dot(rows, quarter(pack, 0), 1, 0)
        value, cdf = gelu_of(hidden)
        active = value.astype(BF16)
        act_ref[...] = active
        slope = cdf + hidden * jnp.exp(-0.5 * hidden * hidden) * 0.3989422804014327
        d_hidden = (dot(d_result, quarter(pack, 1), 1, 1) * slope).astype(BF16)
        dh_ref[...] = d_hidden
        d_total[...] += dot(d_hidden, quarter(pack, 0), 1, 1)
        if forward:
            total[...] += dot(active, quarter(pack, 1), 1, 0)

    @pl.when(step == 1)
    def _():
        for d in range(N_SEQ):
            there = pl.ds(CAP * d, CAP)
            if forward:
                to = lax.rem(me - d + N_SEQ, N_SEQ)
                sent[to, 0] = total[there].astype(BF16)
                sent[to, 1] = d_total[there].astype(BF16)
            else:
                sent[d][...] = d_total[there].astype(BF16)


def expert_back(me, blocks, packs, forward):
    count, sent = (1, (N_SEQ, 2, CAP, D)) if forward else (4, (CAP, D))
    half = pl.BlockSpec((320, 768), lambda i: (0, i))
    block = whole_block((2, CAP, D)) if forward else whole_block((CAP, D))
    outs = grid_call(
        partial(expert_back_kernel, forward),
        [shape(sent, BF16)] * count + [shape((320, D), BF16)] * 2 + [shape((320, 1536), BF16)] * 4,
        [whole_block(sent)] * count + [whole_block((320, D))] * 2 + [half] * 4,
        [me, *blocks, *packs],
        [smem()] + [block] * len(blocks) + [pack_block()] * 2,
        "expert_back",
        [pltpu.VMEM((320, D), F32)] * 2,
    )
    return outs[:count], *outs[count:]


def expert_grads_kernel(
    core_ref, rows_ref, d_result_ref, act_own, dh_own, act_other, dh_other, out_ref, turned_ref
):
    @pl.when((pl.program_id(0) == 0) & (pl.program_id(1) == 0))
    def _():
        turned_ref[...] = rows_ref[...].T

    for place, act_ref, dh_ref in ((0, act_own, dh_own), (1, act_other, dh_other)):
        @pl.when(pl.program_id(0) == place)
        def _():
            grad = dot(turned_ref[...], dh_ref[...], 1, 0).astype(BF16)
            out_ref[0, :, 0] = grad.reshape(N_SHARD, 48, 768)
            grad = dot(act_ref[...], d_result_ref[...], 0, 0).astype(BF16)
            out_ref[0, :, 1] = grad.reshape(N_SHARD, 48, 768)


def expert_grads(core, rows, d_result, act_own, dh_own, act_other, dh_other):
    whole = pl.BlockSpec((320, D), lambda h, i, c: (0, 0))
    mine = pl.BlockSpec((320, 768), lambda h, i, c: (0, jnp.where(h == 0, i, 1)))
    theirs = pl.BlockSpec((320, 768), lambda h, i, c: (0, jnp.where(h == 0, 0, i)))
    return pl.pallas_call(
        expert_grads_kernel,
        out_shape=shape((2, N_SHARD, 4, 48, D), BF16),
        grid_spec=pltpu.PrefetchScalarGridSpec(
            num_scalar_prefetch=1,
            grid=(2, 2),
            in_specs=[whole, whole, mine, mine, theirs, theirs],
            out_specs=pl.BlockSpec(
                (1, N_SHARD, 2, 48, D), lambda h, i, c: (jnp.where(h == 0, c[0], 1 - c[0]), 0, i, 0, 0)
            ),
            scratch_shapes=[pltpu.VMEM((D, 320), BF16)],
        ),
        name="expert_grads",
        compiler_params=pltpu.CompilerParams(
            vmem_limit_bytes=LIMIT, dimension_semantics=("arbitrary", "arbitrary")
        ),
    )(core, rows, d_result, act_own, dh_own, act_other, dh_other)


def combine_kernel(whole, me_ref, residual_ref, high_ref, low_ref, *refs):
    *blocks, out_ref, rows_ref = refs
    for d in range(N_SEQ):
        rows = blocks[0][lax.rem(me_ref[0] + d, N_SEQ), 0] if whole else blocks[d][...]
        rows_ref[CAP * d : CAP * (d + 1)] = rows
    rows = rows_ref[...]
    total = residual_ref[...] + dot(high_ref[...], rows, 1, 0) + dot(low_ref[...], rows, 1, 0)
    out_ref[...] = total.astype(BF16)


def combine(me, residual, high, low, blocks):
    return call(
        partial(combine_kernel, len(blocks) == 1),
        [shape((ROWS, D), BF16)],
        [me, residual, high, low, *blocks],
        "combine",
        scalars=1,
        scratch=[pltpu.VMEM((320, D), BF16)],
    )[0]


def middle_back_kernel(paired, me_ref, d_out_ref, *refs):
    me = me_ref[0]
    count = 1 if paired else 8
    blocks, refs = refs[:count], refs[count:]
    gathered, refs = refs[:4], refs[4:]
    (
        chosen_ref, gates_ref, residual_ref, normed_ref, gain_ref, w0, w1, w2, w3,
        d_residual_ref, small_ref, grad_ref, m0, m1, m2, m3, rows_ref, d_rows_ref, back_ref,
    ) = refs
    for d in range(N_SEQ):
        there = pl.ds(CAP * d, CAP)
        origin = lax.rem(me + d, N_SEQ)
        rows_ref[there] = blocks[0][origin, 0] if paired else blocks[d][...]
        d_rows_ref[there] = blocks[0][origin, 1] if paired else blocks[4 + d][...]
    d_out = d_out_ref[...]
    chosen = chosen_ref[...]
    gates = gates_ref[...]
    products = dot(d_out, rows_ref[...], 1, 1) * chosen.astype(F32)
    slot = lax.broadcasted_iota(jnp.int32, (ROWS, 320), 1)
    own = jnp.where(slot >= 160, jnp.where(slot >= 240, 3, 2), jnp.where(slot >= 80, 1, 0))
    own = lax.rem(own + me, N_SEQ)
    lane = lax.broadcasted_iota(jnp.int32, (ROWS, 64), 1)
    d_gates = jnp.zeros((ROWS, 64), F32)
    for e in range(N_SEQ):
        part = jnp.sum(jnp.where(own == e, products, 0.0), axis=1, keepdims=True)
        d_gates = jnp.where(lane == e, part, d_gates)
    d_logits = gates * (d_gates - jnp.sum(gates * d_gates, axis=1, keepdims=True))
    d_normed = dot(chosen, d_rows_ref[...], 1, 0)
    for e in range(N_SEQ):
        d_normed = d_normed + d_logits[:, e : e + 1] * gain_ref[e : e + 1, :]
    n, inverse = norm_parts(residual_ref[...])
    d_residual = d_out.astype(F32) + norm_back(n, inverse, gain_ref[5:6, :], d_normed)
    d_residual_ref[...] = d_residual
    d_branch = d_residual.astype(BF16)
    for d, (ref, w_ref) in enumerate(zip((m0, m1, m2, m3), (w0, w1, w2, w3))):
        group = lax.rem(me - d + N_SEQ, N_SEQ)
        ref[...] = dot(d_branch, w_ref[...], 1, 1).astype(BF16)
        back_ref[group] = dot(gathered[d][...], d_branch, 0, 0).astype(BF16)
    grad_ref[...] = back_ref[...].reshape(D, D)
    high, low = two_parts(d_logits)
    small = dot(normed_ref[...], high, 0, 0) + dot(normed_ref[...], low, 0, 0)
    column = (lax.broadcasted_iota(jnp.int32, (ROWS, 64), 1) == 5).astype(BF16)
    high, low = two_parts(d_normed * n)
    small = small + dot(high, column, 0, 0) + dot(low, column, 0, 0)
    small_ref[...] = small


def middle_back(me, d_out, blocks, gathered, chosen, gates, residual, normed, gains, w_back, paired):
    outs = call(
        partial(middle_back_kernel, paired),
        [
            shape((ROWS, D), F32),
            shape((D, 64), F32),
            shape((D, D), BF16),
        ]
        + [shape((ROWS, 192), BF16)] * 4,
        [me, d_out, *blocks, *gathered, chosen, gates, residual, normed, gains, *w_back],
        "middle_back",
        scalars=1,
        scratch=[pltpu.VMEM((320, D), BF16)] * 2 + [pltpu.VMEM((N_SEQ, 192, D), BF16)],
    )
    return *outs[:3], outs[3:]


def finish_kernel(further, d_residual_ref, x_ref, gain_ref, b0, b1, b2, b3, *refs):
    d_normed = b0[...].astype(F32) + b1[...].astype(F32) + b2[...].astype(F32) + b3[...].astype(F32)
    n, inverse = norm_parts(x_ref[...].astype(F32))
    total = d_residual_ref[...] + norm_back(n, inverse, gain_ref[4:5, :], d_normed)
    if not further:
        refs[0][...] = total.astype(BF16)
        return
    high_ref, low_ref, out_ref, *sent = refs
    d_out = total.astype(BF16)
    out_ref[...] = d_out
    rows = dot(high_ref[...], d_out, 0, 0) + dot(low_ref[...], d_out, 0, 0)
    for d in range(N_SEQ):
        sent[d][...] = rows[CAP * d : CAP * (d + 1)].astype(BF16)


def finish(d_residual, x, gains, blocks, weights):
    further = weights is not None
    outs = call(
        partial(finish_kernel, further),
        [shape((ROWS, D), BF16)] + [shape((CAP, D), BF16)] * (4 if further else 0),
        [d_residual, x, gains, *blocks] + (list(weights) if further else []),
        "finish",
    )
    return outs[0], outs[1:]


def attention_weights(x, w_qkv, w_proj, w_route, gain_attn, gain_ffn):
    mine = w_qkv.reshape(12, 3, N_SEQ, 192).transpose(2, 0, 1, 3).reshape(N_SEQ, 12, 576)
    small = jnp.concatenate(
        [w_route, gain_attn[:, None], gain_ffn[:, None], jnp.zeros((12, 58), BF16)], axis=1
    )
    mine = jnp.concatenate([mine, jnp.broadcast_to(small, (N_SEQ, 12, 64))], axis=2)
    mine, x = lax.optimization_barrier((mine, x))
    x_blocks = [x] + [turn(x, -d) for d in (1, 2, 3)]
    arrived = lax.all_to_all(mine, "seq", 0, 0, tiled=True).reshape(48, 640)
    back = w_proj.reshape(12, N_SEQ, 192).transpose(1, 0, 2).reshape(48, 192)
    pack = jnp.concatenate([arrived, back], axis=1)
    near = jnp.stack(from_ring(pack, "x"))
    near, x_blocks = lax.optimization_barrier((near, x_blocks))
    far = from_ring(near, "z")
    return far, x_blocks, *unpack(far)


def both_layers(mine):
    core = lax.axis_index("section")
    other = swap(mine)
    return [jnp.where(core == s, mine, other) for s in range(2)]


def half_packs(w_in, w_out):
    core = lax.axis_index("section")
    first = w_in.reshape(48, N_SHARD, 4, 48).transpose(2, 0, 1, 3).reshape(4, 48, 768)
    second = w_out.reshape(4, 48, 768)
    quarters = jnp.stack([first, second], axis=1).reshape(2, 4, 48, 768)
    mine = pick(quarters, core)
    arrived = swap(pick(quarters, 1 - core))
    return [jnp.where(core == s, mine, arrived) for s in range(2)]


def shards(images_in, out_grad, routes, w_qkv, w_proj, w_route, gain_attn, gain_ffn, w_in, w_out):
    core = lax.axis_index("section")
    me = lax.axis_index("seq").astype(jnp.int32).reshape(1)
    core_index = core.astype(jnp.int32).reshape(1)
    own_routes = routes[0, :, 0]
    mine = pick(own_routes, core)
    arrived = swap(pick(own_routes, 1 - core))
    route_of = (jnp.where(core == 0, mine, arrived), jnp.where(core == 0, arrived, mine))
    x0 = pick(images_in, core)[0]
    d_last = pick(out_grad, core)[0]
    halves = half_packs(w_in[0, 0], w_out[0, 0])
    far, x_blocks, rows, back_rows = attention_weights(
        x0, w_qkv[0], w_proj[0], w_route[0], gain_attn[0], gain_ffn[0]
    )
    own = lax.all_gather(tie(halves[0], far), "shard", axis=0, tiled=False)
    attn_rows = both_layers(rows)
    back_rows = both_layers(back_rows)
    attn_rows[0], attn_rows[1], back_rows[0], back_rows[1] = lax.optimization_barrier(
        (attn_rows[0], attn_rows[1], back_rows[0], back_rows[1])
    )
    tables = [v[:, 576:584].T.astype(F32) for v in attn_rows]
    w_back = [[back_rows[0]] + [turn(back_rows[0], d) for d in (1, 2, 3)], None]
    experts = [None, None]

    saved = []
    x = x0
    layer_outs = []
    for s in range(2):
        if s == 1:
            x_blocks = [x] + [turn(x, -d) for d in (1, 2, 3)]
        mixture, x_all, packed, logs = attend(x_blocks, attn_rows[s], tables[s])
        if s == 0:
            w_back[0], mixture = lax.optimization_barrier((w_back[0], mixture))
        else:
            later, mixture[0] = lax.optimization_barrier((later, mixture[0]))
            experts[1] = (later, swap(later))
        gathered = send_out(mixture)
        if s == 0:
            later_back = tie(back_rows[1], gathered)
            w_back[1] = [later_back] + [turn(later_back, d) for d in (1, 2, 3)]
        d_out = d_last if s == 1 else None
        residual, normed, gates, chosen, high, low, buffer = middle(
            me, x, gathered, w_back[s], attn_rows[s], tables[s], route_of[s], d_out
        )
        blocks = send_out(buffer)
        kept = (x, x_all, packed, logs, gathered, residual, normed, gates, chosen, high, low, blocks)
        if s == 0:
            own = tie(own, buffer[0])
            experts[0] = (own, swap(own))
            later = lax.all_gather(tie(halves[1], own), "shard", axis=0, tiled=False)
            result = expert_run(blocks, experts[s])
            w_back[1], result = lax.optimization_barrier((w_back[1], result))
            returned = send_back(result)
            x = combine(me, residual, high, low, returned)
            layer_outs.append(x)
            saved.append((kept, returned))
        else:
            saved.append((kept, None))

    d_out = d_last
    d_buffer = None
    in_grads = [None, None]
    expert_sums = [None, None]
    attn_grads = [None, None]
    for s in (1, 0):
        kept, returned = saved[s]
        x, x_all, packed, logs, gathered, residual, normed, gates, chosen, high, low, blocks = kept
        if s == 1:
            sent, *states = expert_back(me, blocks, experts[s], True)
            arrived = [lax.all_to_all(sent[0], "seq", 0, 0, tiled=True)]
            layer_outs.append(combine(me, residual, high, low, arrived))
        else:
            sent, *states = expert_back(me, [*blocks, *send_out(d_buffer)], experts[s], False)
            arrived = [*returned, *send_back(sent)]
        d_residual, small, grad_back, d_mixture = middle_back(
            me, d_out, arrived, gathered, chosen, gates, residual, normed, tables[s], w_back[s], s == 1
        )
        d_heads = send_back(d_mixture)
        rows, d_result, act_own, act_other, dh_own, dh_other = states
        both = expert_grads(core_index, rows, d_result, act_own, dh_own, act_other, dh_other)
        both = both.reshape(2 * N_SHARD, 4, 48, D)
        expert_sums[s] = lax.psum_scatter(both, ("section", "shard"), scatter_dimension=0, tiled=True)[0]
        d_normed, grad_mix = attend_back(x_all, attn_rows[s], tables[s], packed, logs, d_heads, small)
        d_parts = send_out(d_normed)
        keep = jnp.where(core == 0, grad_mix, grad_back)
        give = jnp.where(core == 0, grad_back, grad_mix)
        attn_grads[s] = (keep.astype(F32) + swap(give).astype(F32)).astype(BF16)
        weights = saved[0][0][9:11] if s == 1 else None
        d_out, d_buffer = finish(d_residual, x, tables[s], d_parts, weights)
        in_grads[s] = d_out

    pair = jnp.concatenate(attn_grads, axis=1).reshape(N_SEQ * N_SHARD, 12, 12, 128)
    pair = pair.transpose(0, 2, 1, 3).reshape(N_SEQ * N_SHARD, 144, 128)
    pair = tie(pair, d_parts)
    arrived = lax.all_to_all(pair, ("seq", "shard"), 0, 0, tiled=True)
    attn_sum = jnp.sum(arrived.reshape(N_SEQ, N_SHARD, 144, 128).astype(F32), axis=1)
    attn_sum = attn_sum.reshape(N_SEQ, 12, 12, 128).transpose(0, 2, 1, 3).reshape(N_SEQ, 12, 2 * D)
    attn_sums = [attn_sum[:, :, :D], attn_sum[:, :, D:]]

    def settle(pair):
        keep = jnp.where(core == 0, pair[0], pair[1])
        give = jnp.where(core == 0, pair[1], pair[0])
        return keep, swap(give)

    def in_order(keep, got):
        return jnp.where(core == 0, jnp.stack([keep, got]), jnp.stack([got, keep]))

    layer_out = in_order(*settle(layer_outs))
    in_grad = in_order(*settle(in_grads))
    grad_in, grad_out = reorder(core_index, *settle(expert_sums))
    attn_sum = in_order(*settle(attn_sums))
    mix = attn_sum[0]
    back = jnp.sum(attn_sum[1], axis=0)
    grad_qkv = mix[:, :, :576].reshape(N_SEQ, 12, 3, 192).transpose(1, 2, 0, 3).reshape(12, 3 * D)
    small = jnp.sum(mix[:, :, 576:640], axis=0)
    return (
        layer_out[None, :, None],
        in_grad[None, :, None],
        grad_qkv[None],
        back[None],
        small[None, :, 0:4],
        small[None, :, 4],
        small[None, :, 5],
        grad_in[None],
        grad_out[None],
    )


def solution(mesh):
    def run(*args):
        outs = shards(*args)
        outs = list(outs)
        outs[7] = outs[7][:, None]
        outs[8] = outs[8][:, None]
        return tuple(outs)

    return jax.shard_map(
        run,
        mesh=mesh,
        in_specs=(
            P(None, "shard", "seq", None),
            P(None, "shard", "seq", None),
            P("section", None, "shard", "seq", None),
            P("section", ("seq", "shard"), None),
            P("section", ("seq", "shard"), None),
            P("section", ("seq", "shard"), None),
            P("section", ("seq", "shard")),
            P("section", ("seq", "shard")),
            P("section", "seq", "shard", None),
            P("section", "seq", "shard", None),
        ),
        out_specs=(
            P("section", None, "shard", "seq", None),
            P("section", None, "shard", "seq", None),
            P("section", ("seq", "shard"), None),
            P("section", ("seq", "shard"), None),
            P("section", ("seq", "shard"), None),
            P("section", ("seq", "shard")),
            P("section", ("seq", "shard")),
            P("section", "seq", "shard", None),
            P("section", "seq", "shard", None),
        ),
        check_vma=False,
    )
```

```python
from functools import partial

import jax
import jax.numpy as jnp
from jax import lax
from jax.experimental import pallas as pl
from jax.experimental.pallas import tpu as pltpu
from jax.sharding import PartitionSpec as P

D = 768
FF = 3072
HEAD_DIM = 64
CAP = 80
N_SEQ = 4
N_SHARD = 16
GROUP = 3
ROWS = 144
SEQ = 576
WIDE = 1472
LIMIT = 56 * 1024 * 1024
EPSILON = 1e-06
F32 = jnp.float32
BF16 = jnp.bfloat16


def dot(a, b, ca, cb):
    return lax.dot_general(a, b, (((ca,), (cb,)), ((), ())), preferred_element_type=F32)


def swap(v):
    return lax.ppermute(v, "section", [(0, 1), (1, 0)])


def turn(v, d):
    return lax.ppermute(v, "seq", [(i, (i + d) % N_SEQ) for i in range(N_SEQ)])


def hop(v, axis, d):
    route = []
    for z in range(4):
        for x in range(4):
            to = ((z + d) % 4) * 4 + x if axis == "z" else z * 4 + (x + d) % 4
            route.append((z * 4 + x, to))
    return lax.ppermute(v, "shard", route)


def from_ring(v, axis):
    return [v] + [hop(v, axis, -d) for d in (1, 2, 3)]


def pick(v, i):
    return lax.dynamic_index_in_dim(v, i, 0, keepdims=False)


def tie(value, other):
    return lax.optimization_barrier((value, other))[0]


def norm_parts(values):
    centred = values - jnp.mean(values, axis=-1, keepdims=True)
    inverse = lax.rsqrt(jnp.mean(centred * centred, axis=-1, keepdims=True) + EPSILON)
    return centred * inverse, inverse


def norm_back(n, inverse, gain, dy):
    gdy = dy * gain
    return (
        gdy
        - jnp.mean(gdy, axis=-1, keepdims=True)
        - n * jnp.mean(gdy * n, axis=-1, keepdims=True)
    ) * inverse


def two_parts(v):
    high = v.astype(BF16)
    return high, (v - high.astype(F32)).astype(BF16)


def gather_tokens(x):
    return jnp.concatenate([x] + [turn(x, -d) for d in (1, 2, 3)], axis=0)


def send_out(blocks):
    return [blocks[0]] + [turn(blocks[d], d) for d in (1, 2, 3)]


def send_back(blocks):
    return [blocks[0]] + [turn(blocks[d], -d) for d in (1, 2, 3)]


def vmem():
    return pl.BlockSpec(memory_space=pltpu.VMEM)


def smem():
    return pl.BlockSpec(memory_space=pltpu.SMEM)


def shape(dims, kind):
    return jax.ShapeDtypeStruct(dims, kind)


def call(body, outs, ins, name, scalars=0, scratch=()):
    specs = [smem()] * scalars + [vmem()] * (len(ins) - scalars)
    return pl.pallas_call(
        body,
        out_shape=outs,
        in_specs=specs,
        out_specs=[vmem()] * len(outs),
        scratch_shapes=list(scratch),
        name=name,
        compiler_params=pltpu.CompilerParams(vmem_limit_bytes=LIMIT),
    )(*ins)


def attend_kernel(x0, x1, x2, x3, w_ref, gain_ref, m0, m1, m2, m3, x_ref, packed_ref, log_ref):
    for d, ref in enumerate((x0, x1, x2, x3)):
        x_ref[ROWS * d : ROWS * (d + 1)] = ref[...]
    n, _ = norm_parts(x_ref[...].astype(F32))
    normed = (n * gain_ref[4:5, :]).astype(BF16)
    packed_ref[...] = dot(normed, w_ref[:, 0:576], 1, 0).astype(BF16)
    lane = lax.broadcasted_iota(jnp.int32, (SEQ, 128), 1)
    logs = jnp.zeros((SEQ, 128), F32)
    outs = []
    for h in range(GROUP):
        query = packed_ref[:, 64 * h : 64 * h + 64]
        key = packed_ref[:, 192 + 64 * h : 256 + 64 * h]
        value = packed_ref[:, 384 + 64 * h : 448 + 64 * h]
        scores = dot(query, key, 1, 1) * HEAD_DIM ** (-0.5)
        top = jnp.max(scores, axis=1, keepdims=True)
        exponent = jnp.exp(scores - top)
        total = jnp.sum(exponent, axis=1, keepdims=True)
        outs.append((dot(exponent.astype(BF16), value, 1, 0) / total).astype(BF16))
        logs = jnp.where(lane == h, top + jnp.log(total), logs)
    log_ref[...] = logs
    mixture = jnp.concatenate(outs, axis=1)
    for d, ref in enumerate((m0, m1, m2, m3)):
        ref[...] = mixture[ROWS * d : ROWS * (d + 1)]


def attend(x_blocks, w_mix, gains):
    outs = call(
        attend_kernel,
        [shape((ROWS, 192), BF16)] * 4
        + [shape((SEQ, D), BF16), shape((SEQ, 576), BF16), shape((SEQ, 128), F32)],
        [*x_blocks, w_mix, gains],
        "attention",
    )
    return list(outs[:4]), *outs[4:]


def attend_back_kernel(
    x_ref, w_ref, gain_ref, packed_ref, log_ref, d0, d1, d2, d3, small_ref,
    n0, n1, n2, n3, grad_ref, d_packed_ref, d_mix_ref,
):
    for d, ref in enumerate((d0, d1, d2, d3)):
        d_mix_ref[ROWS * d : ROWS * (d + 1)] = ref[...]
    scaling = HEAD_DIM ** (-0.5)
    parts = [[], [], []]
    for h in range(GROUP):
        query = packed_ref[:, 64 * h : 64 * h + 64]
        key = packed_ref[:, 192 + 64 * h : 256 + 64 * h]
        value = packed_ref[:, 384 + 64 * h : 448 + 64 * h]
        d_out = d_mix_ref[:, 64 * h : 64 * h + 64]
        attention = jnp.exp(dot(query, key, 1, 1) * scaling - log_ref[:, h : h + 1])
        parts[2].append(dot(attention.astype(BF16), d_out, 0, 0).astype(BF16))
        d_att = dot(d_out, value, 1, 1)
        centre = jnp.sum(attention * d_att, axis=1, keepdims=True)
        d_scores = (attention * (d_att - centre) * scaling).astype(BF16)
        parts[0].append(dot(d_scores, key, 1, 0).astype(BF16))
        parts[1].append(dot(d_scores, query, 0, 0).astype(BF16))
    d_packed_ref[...] = jnp.concatenate(parts[0] + parts[1] + parts[2], axis=1)
    n, _ = norm_parts(x_ref[...].astype(F32))
    normed = (n * gain_ref[4:5, :]).astype(BF16)
    d_packed = d_packed_ref[...]
    d_normed = dot(d_packed, w_ref[:, 0:576], 1, 1)
    for d, ref in enumerate((n0, n1, n2, n3)):
        ref[...] = d_normed[ROWS * d : ROWS * (d + 1)].astype(BF16)
    column = (lax.broadcasted_iota(jnp.int32, (SEQ, 64), 1) == 4).astype(BF16)
    high, low = two_parts(d_normed * n)
    small = small_ref[...] + dot(high, column, 0, 0) + dot(low, column, 0, 0)
    grad = dot(normed, d_packed, 0, 0)
    grad = jnp.concatenate([grad, small, jnp.zeros((D, 128), F32)], axis=1)
    grad_ref[...] = grad.astype(BF16)


def attend_back(x_all, w_mix, gains, packed, logs, d_heads, small):
    outs = call(
        attend_back_kernel,
        [shape((ROWS, D), BF16)] * 4 + [shape((D, D), BF16)],
        [x_all, w_mix, gains, packed, logs, *d_heads, small],
        "attention_back",
        scratch=[pltpu.VMEM((SEQ, 576), BF16), pltpu.VMEM((SEQ, 192), BF16)],
    )
    return outs[:4], outs[4]


def order_rows(first, second):
    i = lax.broadcasted_iota(jnp.int32, (D, 1), 0)
    outer = lax.div(i, 12 * first)
    left = i - 12 * first * outer
    inner = lax.div(left, 12)
    source = inner * (12 * second) + outer * 12 + left - 12 * inner
    return (lax.broadcasted_iota(jnp.int32, (D, D), 1) == source).astype(BF16)


def unpack_kernel(where_ref, b0, b1, b2, b3, rows_ref, back_ref, all_ref):
    z, x = where_ref[0], where_ref[1]
    for dz, ref in enumerate((b0, b1, b2, b3)):
        for dx in range(4):
            all_ref[lax.rem(z + dz, 4) * 4 + lax.rem(x + dx, 4)] = ref[dx]
    whole = all_ref[...].reshape(D, 832)
    ordered = dot(order_rows(N_SHARD, N_SEQ), whole, 1, 0).astype(BF16)
    rows_ref[...] = ordered[:, :640]
    for chunk in range(N_SEQ):
        back_ref[:, 192 * chunk : 192 * (chunk + 1)] = ordered[192 * chunk : 192 * (chunk + 1), 640:]


def unpack(blocks):
    i = lax.axis_index("shard").astype(jnp.int32)
    return call(
        unpack_kernel,
        [shape((D, 640), BF16), shape((192, D), BF16)],
        [jnp.stack([i // 4, lax.rem(i, 4)]), *blocks],
        "unpack",
        scalars=1,
        scratch=[pltpu.VMEM((N_SHARD, 48, 832), BF16)],
    )


def reorder_kernel(core_ref, keep_ref, got_ref, in_ref, out_ref):
    def write(halves):
        columns = []
        for shard in range(N_SHARD):
            for p in range(4):
                block = halves[p // 2][2 * (p % 2)]
                columns.append(block[:, 48 * shard : 48 * (shard + 1)])
        in_ref[...] = jnp.concatenate(columns, axis=1).astype(F32)
        for p in range(4):
            out_ref[48 * p : 48 * (p + 1)] = halves[p // 2][2 * (p % 2) + 1].astype(F32)

    @pl.when(core_ref[0] == 0)
    def _():
        write((keep_ref, got_ref))

    @pl.when(core_ref[0] == 1)
    def _():
        write((got_ref, keep_ref))


def reorder(core, keep, got):
    return call(
        reorder_kernel,
        [shape((48, FF), F32), shape((192, D), F32)],
        [core, keep, got],
        "reorder",
        scalars=1,
    )


def middle_kernel(
    layer, me_ref, x_ref, g0, g1, g2, g3, w0, w1, w2, w3, router_ref, gain_ref, route_ref, *refs
):
    me = me_ref[0]
    extra = layer == 1
    if extra:
        d_out_ref, *refs = refs
    residual_ref, normed_ref, gates_ref, chosen_ref, high_ref, low_ref, *sent = refs
    residual = x_ref[...].astype(F32)
    for ref, w_ref in zip((g0, g1, g2, g3), (w0, w1, w2, w3)):
        residual = residual + dot(ref[...], w_ref[...], 1, 0)
    residual_ref[...] = residual
    n, _ = norm_parts(residual)
    normed = (n * gain_ref[5:6, :]).astype(BF16)
    normed_ref[...] = normed
    lane = lax.broadcasted_iota(jnp.int32, (ROWS, 64), 1)
    logits = jnp.where(lane < 4, dot(normed, router_ref[:, 576:640], 1, 0), -1e30)
    logits = logits - jnp.max(logits, axis=1, keepdims=True)
    gates = jnp.exp(logits)
    gates = gates / jnp.sum(gates, axis=1, keepdims=True)
    gates_ref[...] = gates
    routes = route_ref[...]
    relative = lax.rem(routes - me + N_SEQ, N_SEQ)
    named = (lane == relative[:, 0:1]) | (lane == relative[:, 1:2])
    row = lax.broadcasted_iota(jnp.int32, (ROWS, ROWS), 0)
    column = lax.broadcasted_iota(jnp.int32, (ROWS, ROWS), 1)
    before = (row > column).astype(BF16)
    rank = dot(before, named.astype(BF16), 1, 0)
    slot = lax.broadcasted_iota(jnp.int32, (ROWS, 320), 1)
    own = jnp.where(slot >= 160, jnp.where(slot >= 240, 3, 2), jnp.where(slot >= 80, 1, 0))
    place = (slot - CAP * own).astype(F32)
    wanted = jnp.full((ROWS, 320), -1.0, F32)
    spread = jnp.zeros((ROWS, 320), F32)
    position = jnp.where(named, rank, -1.0)
    for e in range(N_SEQ):
        wanted = jnp.where(own == e, position[:, e : e + 1], wanted)
        spread = jnp.where(lax.rem(own + me, N_SEQ) == e, gates[:, e : e + 1], spread)
    taken = wanted == place
    chosen = taken.astype(BF16)
    high, low = two_parts(jnp.where(taken, spread, 0.0))
    chosen_ref[...] = chosen
    high_ref[...] = high
    low_ref[...] = low
    buffer = dot(chosen, normed, 0, 0).astype(BF16)
    if not extra:
        for d in range(N_SEQ):
            sent[d][...] = buffer[CAP * d : CAP * (d + 1)]
    else:
        d_out = d_out_ref[...]
        d_buffer = (dot(high, d_out, 0, 0) + dot(low, d_out, 0, 0)).astype(BF16)
        for d in range(N_SEQ):
            sent[d][0] = buffer[CAP * d : CAP * (d + 1)]
            sent[d][1] = d_buffer[CAP * d : CAP * (d + 1)]


def middle(me, x, gathered, w_back, router, gains, route_ids, d_out):
    extra = d_out is not None
    sent = (2, CAP, D) if extra else (CAP, D)
    outs = call(
        partial(middle_kernel, int(extra)),
        [
            shape((ROWS, D), F32),
            shape((ROWS, D), BF16),
            shape((ROWS, 64), F32),
            shape((ROWS, 320), BF16),
            shape((ROWS, 320), BF16),
            shape((ROWS, 320), BF16),
        ]
        + [shape(sent, BF16)] * 4,
        [me, x, *gathered, *w_back, router, gains, route_ids] + ([d_out] if extra else []),
        "middle",
        scalars=1,
    )
    return *outs[:6], outs[6:]


def gelu_of(hidden):
    cdf = 0.5 + 0.5 * lax.erf(hidden * 0.7071067811865476)
    return hidden * cdf, cdf


def quarter(ref, i):
    return ref[:, i].reshape(768, D)


def expert_kernel(r0, r1, r2, r3, own_ref, other_ref, o0, o1, o2, o3, rows_ref, total):
    @pl.when(pl.program_id(0) == 0)
    def _():
        for d, ref in enumerate((r0, r1, r2, r3)):
            rows_ref[CAP * d : CAP * (d + 1)] = ref[...]
        total[...] = jnp.zeros_like(total)

    rows = rows_ref[...]
    for pack in (own_ref, other_ref):
        hidden = dot(rows, quarter(pack, 0), 1, 0)
        active = gelu_of(hidden)[0].astype(BF16)
        total[...] += dot(active, quarter(pack, 1), 1, 0)

    @pl.when(pl.program_id(0) == 1)
    def _():
        for d, ref in enumerate((o0, o1, o2, o3)):
            ref[...] = total[CAP * d : CAP * (d + 1)].astype(BF16)


def whole_block(dims):
    return pl.BlockSpec(dims, lambda i: (0,) * len(dims))


def pack_block():
    return pl.BlockSpec((N_SHARD, 2, 48, 768), lambda i: (0, i, 0, 0))


def grid_call(body, outs, out_specs, ins, in_specs, name, scratch):
    return pl.pallas_call(
        body,
        grid=(2,),
        out_shape=outs,
        in_specs=in_specs,
        out_specs=out_specs,
        scratch_shapes=scratch,
        name=name,
        compiler_params=pltpu.CompilerParams(
            vmem_limit_bytes=LIMIT, dimension_semantics=("arbitrary",)
        ),
    )(*ins)


def expert_run(blocks, packs):
    return grid_call(
        expert_kernel,
        [shape((CAP, D), BF16)] * 4,
        [whole_block((CAP, D))] * 4,
        [*blocks, *packs],
        [whole_block((CAP, D))] * 4 + [pack_block()] * 2,
        "expert",
        [pltpu.VMEM((320, D), BF16), pltpu.VMEM((320, D), F32)],
    )


def expert_back_kernel(forward, *refs):
    ins, (own_ref, other_ref), refs = refs[: 4 if forward else 8], refs[4 if forward else 8 :][:2], refs[6 if forward else 10 :]
    sent, refs = refs[:4], refs[4:]
    rows_out, d_result_out, act_own, act_other, dh_own, dh_other, d_total, total = refs
    step = pl.program_id(0)

    @pl.when(step == 0)
    def _():
        for d in range(N_SEQ):
            there = pl.ds(CAP * d, CAP)
            rows_out[there] = ins[d][0] if forward else ins[d][...]
            d_result_out[there] = ins[d][1] if forward else ins[4 + d][...]
        d_total[...] = jnp.zeros_like(d_total)
        if forward:
            total[...] = jnp.zeros_like(total)

    rows = rows_out[...]
    d_result = d_result_out[...]
    for pack, act_ref, dh_ref in ((own_ref, act_own, dh_own), (other_ref, act_other, dh_other)):
        hidden = dot(rows, quarter(pack, 0), 1, 0)
        value, cdf = gelu_of(hidden)
        active = value.astype(BF16)
        act_ref[...] = active
        slope = cdf + hidden * jnp.exp(-0.5 * hidden * hidden) * 0.3989422804014327
        d_hidden = (dot(d_result, quarter(pack, 1), 1, 1) * slope).astype(BF16)
        dh_ref[...] = d_hidden
        d_total[...] += dot(d_hidden, quarter(pack, 0), 1, 1)
        if forward:
            total[...] += dot(active, quarter(pack, 1), 1, 0)

    @pl.when(step == 1)
    def _():
        for d in range(N_SEQ):
            there = pl.ds(CAP * d, CAP)
            if forward:
                sent[d][0] = total[there].astype(BF16)
                sent[d][1] = d_total[there].astype(BF16)
            else:
                sent[d][...] = d_total[there].astype(BF16)


def expert_back(blocks, packs, forward):
    half = pl.BlockSpec((320, 768), lambda i: (0, i))
    block = whole_block((2, CAP, D)) if forward else whole_block((CAP, D))
    sent = (2, CAP, D) if forward else (CAP, D)
    outs = grid_call(
        partial(expert_back_kernel, forward),
        [shape(sent, BF16)] * 4 + [shape((320, D), BF16)] * 2 + [shape((320, 1536), BF16)] * 4,
        [whole_block(sent)] * 4 + [whole_block((320, D))] * 2 + [half] * 4,
        [*blocks, *packs],
        [block] * len(blocks) + [pack_block()] * 2,
        "expert_back",
        [pltpu.VMEM((320, D), F32)] * 2,
    )
    return outs[:4], *outs[4:]


def expert_grads_kernel(
    core_ref, rows_ref, d_result_ref, act_own, dh_own, act_other, dh_other, out_ref, turned_ref
):
    @pl.when((pl.program_id(0) == 0) & (pl.program_id(1) == 0))
    def _():
        turned_ref[...] = rows_ref[...].T

    for place, act_ref, dh_ref in ((0, act_own, dh_own), (1, act_other, dh_other)):
        @pl.when(pl.program_id(0) == place)
        def _():
            grad = dot(turned_ref[...], dh_ref[...], 1, 0).astype(BF16)
            out_ref[0, :, 0] = grad.reshape(N_SHARD, 48, 768)
            grad = dot(act_ref[...], d_result_ref[...], 0, 0).astype(BF16)
            out_ref[0, :, 1] = grad.reshape(N_SHARD, 48, 768)


def expert_grads(core, rows, d_result, act_own, dh_own, act_other, dh_other):
    whole = pl.BlockSpec((320, D), lambda h, i, c: (0, 0))
    mine = pl.BlockSpec((320, 768), lambda h, i, c: (0, jnp.where(h == 0, i, 1)))
    theirs = pl.BlockSpec((320, 768), lambda h, i, c: (0, jnp.where(h == 0, 0, i)))
    return pl.pallas_call(
        expert_grads_kernel,
        out_shape=shape((2, N_SHARD, 4, 48, D), BF16),
        grid_spec=pltpu.PrefetchScalarGridSpec(
            num_scalar_prefetch=1,
            grid=(2, 2),
            in_specs=[whole, whole, mine, mine, theirs, theirs],
            out_specs=pl.BlockSpec(
                (1, N_SHARD, 2, 48, D), lambda h, i, c: (jnp.where(h == 0, c[0], 1 - c[0]), 0, i, 0, 0)
            ),
            scratch_shapes=[pltpu.VMEM((D, 320), BF16)],
        ),
        name="expert_grads",
        compiler_params=pltpu.CompilerParams(
            vmem_limit_bytes=LIMIT, dimension_semantics=("arbitrary", "arbitrary")
        ),
    )(core, rows, d_result, act_own, dh_own, act_other, dh_other)


def expert_grad_kernel(rows_ref, d_result_ref, act_ref, dh_ref, *refs):
    *extra, out_ref = refs
    for i, grad in enumerate((
        dot(rows_ref[...], dh_ref[...], 0, 0),
        dot(act_ref[...], d_result_ref[...], 0, 0),
    )):
        grad = grad.reshape(N_SHARD, 48, 768)
        if extra:
            grad = grad + extra[0][:, i].astype(F32)
        out_ref[:, i] = grad.astype(BF16)


def expert_grad(rows, d_result, active, d_hidden, extra=()):
    half = pl.BlockSpec((320, 768), lambda i: (0, i))
    return grid_call(
        expert_grad_kernel,
        [shape((N_SHARD, 4, 48, 768), BF16)],
        [pack_block()],
        [rows, d_result, active, d_hidden, *extra],
        [whole_block((320, D))] * 2 + [half] * 2 + [pack_block()] * len(extra),
        "expert_grad",
        [],
    )[0]


def combine_kernel(residual_ref, high_ref, low_ref, r0, r1, r2, r3, out_ref, rows_ref):
    for d, ref in enumerate((r0, r1, r2, r3)):
        rows_ref[CAP * d : CAP * (d + 1)] = ref[...]
    rows = rows_ref[...]
    total = residual_ref[...] + dot(high_ref[...], rows, 1, 0) + dot(low_ref[...], rows, 1, 0)
    out_ref[...] = total.astype(BF16)


def combine(residual, high, low, blocks):
    return call(
        combine_kernel,
        [shape((ROWS, D), BF16)],
        [residual, high, low, *blocks],
        "combine",
        scratch=[pltpu.VMEM((320, D), BF16)],
    )[0]


def middle_back_kernel(paired, me_ref, d_out_ref, *refs):
    me = me_ref[0]
    count = 4 if paired else 8
    blocks, refs = refs[:count], refs[count:]
    gathered, refs = refs[:4], refs[4:]
    (
        chosen_ref, gates_ref, residual_ref, normed_ref, gain_ref, w0, w1, w2, w3,
        d_residual_ref, small_ref, grad_ref, m0, m1, m2, m3, rows_ref, d_rows_ref, back_ref,
    ) = refs
    for d in range(N_SEQ):
        there = pl.ds(CAP * d, CAP)
        rows_ref[there] = blocks[d][0] if paired else blocks[d][...]
        d_rows_ref[there] = blocks[d][1] if paired else blocks[4 + d][...]
    d_out = d_out_ref[...]
    chosen = chosen_ref[...]
    gates = gates_ref[...]
    products = dot(d_out, rows_ref[...], 1, 1) * chosen.astype(F32)
    slot = lax.broadcasted_iota(jnp.int32, (ROWS, 320), 1)
    own = jnp.where(slot >= 160, jnp.where(slot >= 240, 3, 2), jnp.where(slot >= 80, 1, 0))
    own = lax.rem(own + me, N_SEQ)
    lane = lax.broadcasted_iota(jnp.int32, (ROWS, 64), 1)
    d_gates = jnp.zeros((ROWS, 64), F32)
    for e in range(N_SEQ):
        part = jnp.sum(jnp.where(own == e, products, 0.0), axis=1, keepdims=True)
        d_gates = jnp.where(lane == e, part, d_gates)
    d_logits = gates * (d_gates - jnp.sum(gates * d_gates, axis=1, keepdims=True))
    d_normed = dot(chosen, d_rows_ref[...], 1, 0)
    for e in range(N_SEQ):
        d_normed = d_normed + d_logits[:, e : e + 1] * gain_ref[e : e + 1, :]
    n, inverse = norm_parts(residual_ref[...])
    d_residual = d_out.astype(F32) + norm_back(n, inverse, gain_ref[5:6, :], d_normed)
    d_residual_ref[...] = d_residual
    d_branch = d_residual.astype(BF16)
    for d, (ref, w_ref) in enumerate(zip((m0, m1, m2, m3), (w0, w1, w2, w3))):
        group = lax.rem(me - d + N_SEQ, N_SEQ)
        ref[...] = dot(d_branch, w_ref[...], 1, 1).astype(BF16)
        back_ref[group] = dot(gathered[d][...], d_branch, 0, 0).astype(BF16)
    grad_ref[...] = back_ref[...].reshape(D, D)
    high, low = two_parts(d_logits)
    small = dot(normed_ref[...], high, 0, 0) + dot(normed_ref[...], low, 0, 0)
    column = (lax.broadcasted_iota(jnp.int32, (ROWS, 64), 1) == 5).astype(BF16)
    high, low = two_parts(d_normed * n)
    small = small + dot(high, column, 0, 0) + dot(low, column, 0, 0)
    small_ref[...] = small


def middle_back(me, d_out, blocks, gathered, chosen, gates, residual, normed, gains, w_back, paired):
    outs = call(
        partial(middle_back_kernel, paired),
        [
            shape((ROWS, D), F32),
            shape((D, 64), F32),
            shape((D, D), BF16),
        ]
        + [shape((ROWS, 192), BF16)] * 4,
        [me, d_out, *blocks, *gathered, chosen, gates, residual, normed, gains, *w_back],
        "middle_back",
        scalars=1,
        scratch=[pltpu.VMEM((320, D), BF16)] * 2 + [pltpu.VMEM((N_SEQ, 192, D), BF16)],
    )
    return *outs[:3], outs[3:]


def finish_kernel(further, d_residual_ref, x_ref, gain_ref, b0, b1, b2, b3, *refs):
    d_normed = b0[...].astype(F32) + b1[...].astype(F32) + b2[...].astype(F32) + b3[...].astype(F32)
    n, inverse = norm_parts(x_ref[...].astype(F32))
    total = d_residual_ref[...] + norm_back(n, inverse, gain_ref[4:5, :], d_normed)
    if not further:
        refs[0][...] = total.astype(BF16)
        return
    high_ref, low_ref, out_ref, *sent = refs
    d_out = total.astype(BF16)
    out_ref[...] = d_out
    rows = dot(high_ref[...], d_out, 0, 0) + dot(low_ref[...], d_out, 0, 0)
    for d in range(N_SEQ):
        sent[d][...] = rows[CAP * d : CAP * (d + 1)].astype(BF16)


def finish(d_residual, x, gains, blocks, weights):
    further = weights is not None
    outs = call(
        partial(finish_kernel, further),
        [shape((ROWS, D), BF16)] + [shape((CAP, D), BF16)] * (4 if further else 0),
        [d_residual, x, gains, *blocks] + (list(weights) if further else []),
        "finish",
    )
    return outs[0], outs[1:]


def attention_weights(x_blocks, w_qkv, w_proj, w_route, gain_attn, gain_ffn):
    mine = w_qkv.reshape(12, 3, N_SEQ, 192).transpose(2, 0, 1, 3).reshape(N_SEQ, 12, 576)
    small = jnp.concatenate(
        [w_route, gain_attn[:, None], gain_ffn[:, None], jnp.zeros((12, 58), BF16)], axis=1
    )
    mine = jnp.concatenate([mine, jnp.broadcast_to(small, (N_SEQ, 12, 64))], axis=2)
    arrived = lax.all_to_all(mine, "seq", 0, 0, tiled=True).reshape(48, 640)
    back = w_proj.reshape(12, N_SEQ, 192).transpose(1, 0, 2).reshape(48, 192)
    pack = jnp.concatenate([arrived, back], axis=1)
    near = jnp.stack(from_ring(tie(pack, x_blocks), "x"))
    far = from_ring(near, "z")
    return far, *unpack(far)


def both_layers(mine):
    core = lax.axis_index("section")
    other = swap(mine)
    return [jnp.where(core == s, mine, other) for s in range(2)]


def half_packs(w_in, w_out):
    core = lax.axis_index("section")
    first = w_in.reshape(48, N_SHARD, 4, 48).transpose(2, 0, 1, 3).reshape(4, 48, 768)
    second = w_out.reshape(4, 48, 768)
    quarters = jnp.stack([first, second], axis=1).reshape(2, 4, 48, 768)
    mine = pick(quarters, core)
    arrived = swap(pick(quarters, 1 - core))
    return [jnp.where(core == s, mine, arrived) for s in range(2)]


def shards(images_in, out_grad, routes, w_qkv, w_proj, w_route, gain_attn, gain_ffn, w_in, w_out):
    core = lax.axis_index("section")
    me = lax.axis_index("seq").astype(jnp.int32).reshape(1)
    core_index = core.astype(jnp.int32).reshape(1)
    own_routes = routes[0, :, 0]
    mine = pick(own_routes, core)
    arrived = swap(pick(own_routes, 1 - core))
    route_of = (jnp.where(core == 0, mine, arrived), jnp.where(core == 0, arrived, mine))
    x0 = pick(images_in, core)[0]
    d_last = pick(out_grad, core)[0]
    halves = half_packs(w_in[0, 0], w_out[0, 0])
    x_blocks = [x0] + [turn(x0, -d) for d in (1, 2, 3)]
    far, rows, back_rows = attention_weights(
        x_blocks, w_qkv[0], w_proj[0], w_route[0], gain_attn[0], gain_ffn[0]
    )
    own = lax.all_gather(tie(halves[0], far), "shard", axis=0, tiled=False)
    attn_rows = both_layers(rows)
    back_rows = both_layers(back_rows)
    attn_rows[0], attn_rows[1], back_rows[0], back_rows[1] = lax.optimization_barrier(
        (attn_rows[0], attn_rows[1], back_rows[0], back_rows[1])
    )
    tables = [v[:, 576:584].T.astype(F32) for v in attn_rows]
    w_back = [[back_rows[0]] + [turn(back_rows[0], d) for d in (1, 2, 3)], None]
    experts = [None, None]

    saved = []
    x = x0
    layer_outs = []
    for s in range(2):
        if s == 1:
            x_blocks = [x] + [turn(x, -d) for d in (1, 2, 3)]
        mixture, x_all, packed, logs = attend(x_blocks, attn_rows[s], tables[s])
        if s == 0:
            w_back[0], mixture = lax.optimization_barrier((w_back[0], mixture))
        else:
            later, mixture[0] = lax.optimization_barrier((later, mixture[0]))
            experts[1] = (later, swap(later))
        gathered = send_out(mixture)
        d_out = d_last if s == 1 else None
        residual, normed, gates, chosen, high, low, buffer = middle(
            me, x, gathered, w_back[s], attn_rows[s], tables[s], route_of[s], d_out
        )
        blocks = send_out(buffer)
        kept = (x, x_all, packed, logs, gathered, residual, normed, gates, chosen, high, low, blocks)
        if s == 0:
            own = tie(own, blocks)
            experts[0] = (own, swap(own))
            later = lax.all_gather(tie(halves[1], own), "shard", axis=0, tiled=False)
            later_back = tie(back_rows[1], blocks)
            w_back[1] = [later_back] + [turn(later_back, d) for d in (1, 2, 3)]
            result = expert_run(blocks, experts[s])
            w_back[1], result = lax.optimization_barrier((w_back[1], result))
            returned = send_back(result)
            x = combine(residual, high, low, returned)
            layer_outs.append(x)
            saved.append((kept, returned))
        else:
            saved.append((kept, None))

    d_out = d_last
    d_buffer = None
    in_grads = [None, None]
    expert_sums = [None, None]
    attn_grads = [None, None]
    for s in (1, 0):
        kept, returned = saved[s]
        x, x_all, packed, logs, gathered, residual, normed, gates, chosen, high, low, blocks = kept
        if s == 1:
            sent, *states = expert_back(blocks, experts[s], True)
            arrived = send_back(sent)
            layer_outs.append(combine(residual, high, low, [v[0] for v in arrived]))
        else:
            sent, *states = expert_back([*blocks, *send_out(d_buffer)], experts[s], False)
            arrived = [*returned, *send_back(sent)]
        d_residual, small, grad_back, d_mixture = middle_back(
            me, d_out, arrived, gathered, chosen, gates, residual, normed, tables[s], w_back[s], s == 1
        )
        d_heads = send_back(d_mixture)
        rows, d_result, act_own, act_other, dh_own, dh_other = states
        if s == 1:
            both = expert_grads(core_index, rows, d_result, act_own, dh_own, act_other, dh_other)
            both = both.reshape(2 * N_SHARD, 4, 48, D)
            group = ("section", "shard")
        else:
            other = swap(expert_grad(rows, d_result, act_other, dh_other))
            both = expert_grad(rows, d_result, act_own, dh_own, (other,))
            group = "shard"
        expert_sums[s] = lax.psum_scatter(both, group, scatter_dimension=0, tiled=True)[0]
        d_normed, grad_mix = attend_back(x_all, attn_rows[s], tables[s], packed, logs, d_heads, small)
        d_parts = send_out(d_normed)
        keep = jnp.where(core == 0, grad_mix, grad_back)
        give = jnp.where(core == 0, grad_back, grad_mix)
        attn_grads[s] = (keep.astype(F32) + swap(give).astype(F32)).astype(BF16)
        weights = saved[0][0][9:11] if s == 1 else None
        d_out, d_buffer = finish(d_residual, x, tables[s], d_parts, weights)
        in_grads[s] = d_out

    pair = jnp.concatenate(attn_grads, axis=1).reshape(N_SEQ * N_SHARD, 12, 12, 128)
    pair = pair.transpose(0, 2, 1, 3).reshape(N_SEQ * N_SHARD, 144, 128)
    pair = tie(pair, d_parts)
    arrived = lax.all_to_all(pair, ("seq", "shard"), 0, 0, tiled=True)
    attn_sum = jnp.sum(arrived.reshape(N_SEQ, N_SHARD, 144, 128).astype(F32), axis=1)
    attn_sum = attn_sum.reshape(N_SEQ, 12, 12, 128).transpose(0, 2, 1, 3).reshape(N_SEQ, 12, 2 * D)
    attn_sums = [attn_sum[:, :, :D], attn_sum[:, :, D:]]

    def settle(pair):
        keep = jnp.where(core == 0, pair[0], pair[1])
        give = jnp.where(core == 0, pair[1], pair[0])
        return keep, swap(give)

    def in_order(keep, got):
        return jnp.where(core == 0, jnp.stack([keep, got]), jnp.stack([got, keep]))

    layer_out = in_order(*settle(layer_outs))
    in_grad = in_order(*settle(in_grads))
    grad_in, grad_out = reorder(core_index, *settle(expert_sums))
    attn_sum = in_order(*settle(attn_sums))
    mix = attn_sum[0]
    back = jnp.sum(attn_sum[1], axis=0)
    grad_qkv = mix[:, :, :576].reshape(N_SEQ, 12, 3, 192).transpose(1, 2, 0, 3).reshape(12, 3 * D)
    small = jnp.sum(mix[:, :, 576:640], axis=0)
    return (
        layer_out[None, :, None],
        in_grad[None, :, None],
        grad_qkv[None],
        back[None],
        small[None, :, 0:4],
        small[None, :, 4],
        small[None, :, 5],
        grad_in[None],
        grad_out[None],
    )


def solution(mesh):
    def run(*args):
        outs = shards(*args)
        outs = list(outs)
        outs[7] = outs[7][:, None]
        outs[8] = outs[8][:, None]
        return tuple(outs)

    return jax.shard_map(
        run,
        mesh=mesh,
        in_specs=(
            P(None, "shard", "seq", None),
            P(None, "shard", "seq", None),
            P("section", None, "shard", "seq", None),
            P("section", ("seq", "shard"), None),
            P("section", ("seq", "shard"), None),
            P("section", ("seq", "shard"), None),
            P("section", ("seq", "shard")),
            P("section", ("seq", "shard")),
            P("section", "seq", "shard", None),
            P("section", "seq", "shard", None),
        ),
        out_specs=(
            P("section", None, "shard", "seq", None),
            P("section", None, "shard", "seq", None),
            P("section", ("seq", "shard"), None),
            P("section", ("seq", "shard"), None),
            P("section", ("seq", "shard"), None),
            P("section", ("seq", "shard")),
            P("section", ("seq", "shard")),
            P("section", "seq", "shard", None),
            P("section", "seq", "shard", None),
        ),
        check_vma=False,
    )
```

```python
from functools import partial

import jax
import jax.numpy as jnp
from jax import lax
from jax.experimental import pallas as pl
from jax.experimental.pallas import tpu as pltpu
from jax.sharding import PartitionSpec as P

D = 768
FF = 3072
HEAD_DIM = 64
CAP = 80
N_SEQ = 4
N_SHARD = 16
GROUP = 3
ROWS = 144
SEQ = 576
WIDE = 1472
LIMIT = 56 * 1024 * 1024
EPSILON = 1e-06
F32 = jnp.float32
BF16 = jnp.bfloat16


def dot(a, b, ca, cb):
    return lax.dot_general(a, b, (((ca,), (cb,)), ((), ())), preferred_element_type=F32)


def swap(v):
    return lax.ppermute(v, "section", [(0, 1), (1, 0)])


def turn(v, d):
    return lax.ppermute(v, "seq", [(i, (i + d) % N_SEQ) for i in range(N_SEQ)])


def hop(v, axis, d):
    route = []
    for z in range(4):
        for x in range(4):
            to = ((z + d) % 4) * 4 + x if axis == "z" else z * 4 + (x + d) % 4
            route.append((z * 4 + x, to))
    return lax.ppermute(v, "shard", route)


def from_ring(v, axis):
    return [v] + [hop(v, axis, -d) for d in (1, 2, 3)]


def pick(v, i):
    return lax.dynamic_index_in_dim(v, i, 0, keepdims=False)


def tie(value, other):
    return lax.optimization_barrier((value, other))[0]


def norm_parts(values):
    centred = values - jnp.mean(values, axis=-1, keepdims=True)
    inverse = lax.rsqrt(jnp.mean(centred * centred, axis=-1, keepdims=True) + EPSILON)
    return centred * inverse, inverse


def norm_back(n, inverse, gain, dy):
    gdy = dy * gain
    return (
        gdy
        - jnp.mean(gdy, axis=-1, keepdims=True)
        - n * jnp.mean(gdy * n, axis=-1, keepdims=True)
    ) * inverse


def two_parts(v):
    high = v.astype(BF16)
    return high, (v - high.astype(F32)).astype(BF16)


def gather_tokens(x):
    return jnp.concatenate([x] + [turn(x, -d) for d in (1, 2, 3)], axis=0)


def send_out(blocks):
    return [blocks[0]] + [turn(blocks[d], d) for d in (1, 2, 3)]


def send_back(blocks):
    return [blocks[0]] + [turn(blocks[d], -d) for d in (1, 2, 3)]


def vmem():
    return pl.BlockSpec(memory_space=pltpu.VMEM)


def smem():
    return pl.BlockSpec(memory_space=pltpu.SMEM)


def shape(dims, kind):
    return jax.ShapeDtypeStruct(dims, kind)


def call(body, outs, ins, name, scalars=0, scratch=()):
    specs = [smem()] * scalars + [vmem()] * (len(ins) - scalars)
    return pl.pallas_call(
        body,
        out_shape=outs,
        in_specs=specs,
        out_specs=[vmem()] * len(outs),
        scratch_shapes=list(scratch),
        name=name,
        compiler_params=pltpu.CompilerParams(vmem_limit_bytes=LIMIT),
    )(*ins)


def attend_kernel(x0, x1, x2, x3, w_ref, gain_ref, m0, m1, m2, m3, x_ref, packed_ref, log_ref):
    for d, ref in enumerate((x0, x1, x2, x3)):
        x_ref[ROWS * d : ROWS * (d + 1)] = ref[...]
    n, _ = norm_parts(x_ref[...].astype(F32))
    normed = (n * gain_ref[4:5, :]).astype(BF16)
    packed_ref[...] = dot(normed, w_ref[:, 0:576], 1, 0).astype(BF16)
    lane = lax.broadcasted_iota(jnp.int32, (SEQ, 128), 1)
    logs = jnp.zeros((SEQ, 128), F32)
    outs = []
    for h in range(GROUP):
        query = packed_ref[:, 64 * h : 64 * h + 64]
        key = packed_ref[:, 192 + 64 * h : 256 + 64 * h]
        value = packed_ref[:, 384 + 64 * h : 448 + 64 * h]
        scores = dot(query, key, 1, 1) * HEAD_DIM ** (-0.5)
        top = jnp.max(scores, axis=1, keepdims=True)
        exponent = jnp.exp(scores - top)
        total = jnp.sum(exponent, axis=1, keepdims=True)
        outs.append((dot(exponent.astype(BF16), value, 1, 0) / total).astype(BF16))
        logs = jnp.where(lane == h, top + jnp.log(total), logs)
    log_ref[...] = logs
    mixture = jnp.concatenate(outs, axis=1)
    for d, ref in enumerate((m0, m1, m2, m3)):
        ref[...] = mixture[ROWS * d : ROWS * (d + 1)]


def attend(x_blocks, w_mix, gains):
    outs = call(
        attend_kernel,
        [shape((ROWS, 192), BF16)] * 4
        + [shape((SEQ, D), BF16), shape((SEQ, 576), BF16), shape((SEQ, 128), F32)],
        [*x_blocks, w_mix, gains],
        "attention",
    )
    return list(outs[:4]), *outs[4:]


def attend_back_kernel(
    x_ref, w_ref, gain_ref, packed_ref, log_ref, d0, d1, d2, d3, small_ref,
    n0, n1, n2, n3, grad_ref, d_packed_ref, d_mix_ref,
):
    for d, ref in enumerate((d0, d1, d2, d3)):
        d_mix_ref[ROWS * d : ROWS * (d + 1)] = ref[...]
    scaling = HEAD_DIM ** (-0.5)
    parts = [[], [], []]
    for h in range(GROUP):
        query = packed_ref[:, 64 * h : 64 * h + 64]
        key = packed_ref[:, 192 + 64 * h : 256 + 64 * h]
        value = packed_ref[:, 384 + 64 * h : 448 + 64 * h]
        d_out = d_mix_ref[:, 64 * h : 64 * h + 64]
        attention = jnp.exp(dot(query, key, 1, 1) * scaling - log_ref[:, h : h + 1])
        parts[2].append(dot(attention.astype(BF16), d_out, 0, 0).astype(BF16))
        d_att = dot(d_out, value, 1, 1)
        centre = jnp.sum(attention * d_att, axis=1, keepdims=True)
        d_scores = (attention * (d_att - centre) * scaling).astype(BF16)
        parts[0].append(dot(d_scores, key, 1, 0).astype(BF16))
        parts[1].append(dot(d_scores, query, 0, 0).astype(BF16))
    d_packed_ref[...] = jnp.concatenate(parts[0] + parts[1] + parts[2], axis=1)
    n, _ = norm_parts(x_ref[...].astype(F32))
    normed = (n * gain_ref[4:5, :]).astype(BF16)
    d_packed = d_packed_ref[...]
    d_normed = dot(d_packed, w_ref[:, 0:576], 1, 1)
    for d, ref in enumerate((n0, n1, n2, n3)):
        ref[...] = d_normed[ROWS * d : ROWS * (d + 1)].astype(BF16)
    column = (lax.broadcasted_iota(jnp.int32, (SEQ, 64), 1) == 4).astype(BF16)
    high, low = two_parts(d_normed * n)
    small = small_ref[...] + dot(high, column, 0, 0) + dot(low, column, 0, 0)
    grad = dot(normed, d_packed, 0, 0)
    grad = jnp.concatenate([grad, small, jnp.zeros((D, 128), F32)], axis=1)
    grad_ref[...] = grad.astype(BF16)


def attend_back(x_all, w_mix, gains, packed, logs, d_heads, small):
    outs = call(
        attend_back_kernel,
        [shape((ROWS, D), BF16)] * 4 + [shape((D, D), BF16)],
        [x_all, w_mix, gains, packed, logs, *d_heads, small],
        "attention_back",
        scratch=[pltpu.VMEM((SEQ, 576), BF16), pltpu.VMEM((SEQ, 192), BF16)],
    )
    return outs[:4], outs[4]


def order_rows(first, second):
    i = lax.broadcasted_iota(jnp.int32, (D, 1), 0)
    outer = lax.div(i, 12 * first)
    left = i - 12 * first * outer
    inner = lax.div(left, 12)
    source = inner * (12 * second) + outer * 12 + left - 12 * inner
    return (lax.broadcasted_iota(jnp.int32, (D, D), 1) == source).astype(BF16)


def unpack_kernel(where_ref, b0, b1, b2, b3, rows_ref, back_ref, all_ref):
    z, x = where_ref[0], where_ref[1]
    for dz, ref in enumerate((b0, b1, b2, b3)):
        for dx in range(4):
            all_ref[lax.rem(z + dz, 4) * 4 + lax.rem(x + dx, 4)] = ref[dx]
    whole = all_ref[...].reshape(D, 832)
    ordered = dot(order_rows(N_SHARD, N_SEQ), whole, 1, 0).astype(BF16)
    rows_ref[...] = ordered[:, :640]
    for chunk in range(N_SEQ):
        back_ref[:, 192 * chunk : 192 * (chunk + 1)] = ordered[192 * chunk : 192 * (chunk + 1), 640:]


def unpack(blocks):
    i = lax.axis_index("shard").astype(jnp.int32)
    return call(
        unpack_kernel,
        [shape((D, 640), BF16), shape((192, D), BF16)],
        [jnp.stack([i // 4, lax.rem(i, 4)]), *blocks],
        "unpack",
        scalars=1,
        scratch=[pltpu.VMEM((N_SHARD, 48, 832), BF16)],
    )


def reorder_kernel(core_ref, keep_ref, got_ref, in_ref, out_ref):
    def write(halves):
        columns = []
        for shard in range(N_SHARD):
            for p in range(4):
                block = halves[p // 2][2 * (p % 2)]
                columns.append(block[:, 48 * shard : 48 * (shard + 1)])
        in_ref[...] = jnp.concatenate(columns, axis=1).astype(F32)
        for p in range(4):
            out_ref[48 * p : 48 * (p + 1)] = halves[p // 2][2 * (p % 2) + 1].astype(F32)

    @pl.when(core_ref[0] == 0)
    def _():
        write((keep_ref, got_ref))

    @pl.when(core_ref[0] == 1)
    def _():
        write((got_ref, keep_ref))


def reorder(core, keep, got):
    return call(
        reorder_kernel,
        [shape((48, FF), F32), shape((192, D), F32)],
        [core, keep, got],
        "reorder",
        scalars=1,
    )


def middle_kernel(
    layer, me_ref, x_ref, g0, g1, g2, g3, w0, w1, w2, w3, router_ref, gain_ref, route_ref, *refs
):
    me = me_ref[0]
    extra = layer == 1
    if extra:
        d_out_ref, *refs = refs
    residual_ref, normed_ref, gates_ref, chosen_ref, high_ref, low_ref, *sent = refs
    residual = x_ref[...].astype(F32)
    for ref, w_ref in zip((g0, g1, g2, g3), (w0, w1, w2, w3)):
        residual = residual + dot(ref[...], w_ref[...], 1, 0)
    residual_ref[...] = residual
    n, _ = norm_parts(residual)
    normed = (n * gain_ref[5:6, :]).astype(BF16)
    normed_ref[...] = normed
    lane = lax.broadcasted_iota(jnp.int32, (ROWS, 64), 1)
    logits = jnp.where(lane < 4, dot(normed, router_ref[:, 576:640], 1, 0), -1e30)
    logits = logits - jnp.max(logits, axis=1, keepdims=True)
    gates = jnp.exp(logits)
    gates = gates / jnp.sum(gates, axis=1, keepdims=True)
    gates_ref[...] = gates
    routes = route_ref[...]
    relative = lax.rem(routes - me + N_SEQ, N_SEQ)
    named = (lane == relative[:, 0:1]) | (lane == relative[:, 1:2])
    row = lax.broadcasted_iota(jnp.int32, (ROWS, ROWS), 0)
    column = lax.broadcasted_iota(jnp.int32, (ROWS, ROWS), 1)
    before = (row > column).astype(BF16)
    rank = dot(before, named.astype(BF16), 1, 0)
    slot = lax.broadcasted_iota(jnp.int32, (ROWS, 320), 1)
    own = jnp.where(slot >= 160, jnp.where(slot >= 240, 3, 2), jnp.where(slot >= 80, 1, 0))
    place = (slot - CAP * own).astype(F32)
    wanted = jnp.full((ROWS, 320), -1.0, F32)
    spread = jnp.zeros((ROWS, 320), F32)
    position = jnp.where(named, rank, -1.0)
    for e in range(N_SEQ):
        wanted = jnp.where(own == e, position[:, e : e + 1], wanted)
        spread = jnp.where(lax.rem(own + me, N_SEQ) == e, gates[:, e : e + 1], spread)
    taken = wanted == place
    chosen = taken.astype(BF16)
    high, low = two_parts(jnp.where(taken, spread, 0.0))
    chosen_ref[...] = chosen
    high_ref[...] = high
    low_ref[...] = low
    buffer = dot(chosen, normed, 0, 0).astype(BF16)
    if not extra:
        for d in range(N_SEQ):
            sent[d][...] = buffer[CAP * d : CAP * (d + 1)]
    else:
        d_out = d_out_ref[...]
        d_buffer = (dot(high, d_out, 0, 0) + dot(low, d_out, 0, 0)).astype(BF16)
        for d in range(N_SEQ):
            sent[d][0] = buffer[CAP * d : CAP * (d + 1)]
            sent[d][1] = d_buffer[CAP * d : CAP * (d + 1)]


def middle(me, x, gathered, w_back, router, gains, route_ids, d_out):
    extra = d_out is not None
    sent = (2, CAP, D) if extra else (CAP, D)
    outs = call(
        partial(middle_kernel, int(extra)),
        [
            shape((ROWS, D), F32),
            shape((ROWS, D), BF16),
            shape((ROWS, 64), F32),
            shape((ROWS, 320), BF16),
            shape((ROWS, 320), BF16),
            shape((ROWS, 320), BF16),
        ]
        + [shape(sent, BF16)] * 4,
        [me, x, *gathered, *w_back, router, gains, route_ids] + ([d_out] if extra else []),
        "middle",
        scalars=1,
    )
    return *outs[:6], outs[6:]


def gelu_of(hidden):
    cdf = 0.5 + 0.5 * lax.erf(hidden * 0.7071067811865476)
    return hidden * cdf, cdf


def quarter(ref, i):
    return ref[:, i].reshape(768, D)


def expert_first_kernel(r0, r1, r2, r3, pack, rows_ref, total):
    @pl.when(pl.program_id(0) == 0)
    def _():
        for d, ref in enumerate((r0, r1, r2, r3)):
            rows_ref[CAP * d : CAP * (d + 1)] = ref[...]
        total[...] = jnp.zeros_like(total)

    active = gelu_of(dot(rows_ref[...], quarter(pack, 0), 1, 0))[0].astype(BF16)
    total[...] += dot(active, quarter(pack, 1), 1, 0)


def expert_second_kernel(rows_ref, first_ref, pack, o0, o1, o2, o3, total):
    @pl.when(pl.program_id(0) == 0)
    def _():
        total[...] = first_ref[...]

    active = gelu_of(dot(rows_ref[...], quarter(pack, 0), 1, 0))[0].astype(BF16)
    total[...] += dot(active, quarter(pack, 1), 1, 0)

    @pl.when(pl.program_id(0) == 1)
    def _():
        for d, ref in enumerate((o0, o1, o2, o3)):
            ref[...] = total[CAP * d : CAP * (d + 1)].astype(BF16)


def whole_block(dims):
    return pl.BlockSpec(dims, lambda i: (0,) * len(dims))


def pack_block():
    return pl.BlockSpec((N_SHARD, 2, 48, 768), lambda i: (0, i, 0, 0))


def grid_call(body, outs, out_specs, ins, in_specs, name, scratch):
    return pl.pallas_call(
        body,
        grid=(2,),
        out_shape=outs,
        in_specs=in_specs,
        out_specs=out_specs,
        scratch_shapes=scratch,
        name=name,
        compiler_params=pltpu.CompilerParams(
            vmem_limit_bytes=LIMIT, dimension_semantics=("arbitrary",)
        ),
    )(*ins)


def expert_run(blocks, own, other):
    rows, first = grid_call(
        expert_first_kernel,
        [shape((320, D), BF16), shape((320, D), F32)],
        [whole_block((320, D))] * 2,
        [*blocks, own],
        [whole_block((CAP, D))] * 4 + [pack_block()],
        "expert_first",
        [],
    )
    return grid_call(
        expert_second_kernel,
        [shape((CAP, D), BF16)] * 4,
        [whole_block((CAP, D))] * 4,
        [rows, first, other],
        [whole_block((320, D))] * 2 + [pack_block()],
        "expert_second",
        [pltpu.VMEM((320, D), F32)],
    )


def expert_back_kernel(forward, *refs):
    ins, (own_ref, other_ref), refs = refs[: 4 if forward else 8], refs[4 if forward else 8 :][:2], refs[6 if forward else 10 :]
    sent, refs = refs[:4], refs[4:]
    rows_out, d_result_out, act_own, act_other, dh_own, dh_other, d_total, total = refs
    step = pl.program_id(0)

    @pl.when(step == 0)
    def _():
        for d in range(N_SEQ):
            there = pl.ds(CAP * d, CAP)
            rows_out[there] = ins[d][0] if forward else ins[d][...]
            d_result_out[there] = ins[d][1] if forward else ins[4 + d][...]
        d_total[...] = jnp.zeros_like(d_total)
        if forward:
            total[...] = jnp.zeros_like(total)

    rows = rows_out[...]
    d_result = d_result_out[...]
    for pack, act_ref, dh_ref in ((own_ref, act_own, dh_own), (other_ref, act_other, dh_other)):
        hidden = dot(rows, quarter(pack, 0), 1, 0)
        value, cdf = gelu_of(hidden)
        active = value.astype(BF16)
        act_ref[...] = active
        slope = cdf + hidden * jnp.exp(-0.5 * hidden * hidden) * 0.3989422804014327
        d_hidden = (dot(d_result, quarter(pack, 1), 1, 1) * slope).astype(BF16)
        dh_ref[...] = d_hidden
        d_total[...] += dot(d_hidden, quarter(pack, 0), 1, 1)
        if forward:
            total[...] += dot(active, quarter(pack, 1), 1, 0)

    @pl.when(step == 1)
    def _():
        for d in range(N_SEQ):
            there = pl.ds(CAP * d, CAP)
            if forward:
                sent[d][0] = total[there].astype(BF16)
                sent[d][1] = d_total[there].astype(BF16)
            else:
                sent[d][...] = d_total[there].astype(BF16)


def expert_back(blocks, packs, forward):
    half = pl.BlockSpec((320, 768), lambda i: (0, i))
    block = whole_block((2, CAP, D)) if forward else whole_block((CAP, D))
    sent = (2, CAP, D) if forward else (CAP, D)
    outs = grid_call(
        partial(expert_back_kernel, forward),
        [shape(sent, BF16)] * 4 + [shape((320, D), BF16)] * 2 + [shape((320, 1536), BF16)] * 4,
        [whole_block(sent)] * 4 + [whole_block((320, D))] * 2 + [half] * 4,
        [*blocks, *packs],
        [block] * len(blocks) + [pack_block()] * 2,
        "expert_back",
        [pltpu.VMEM((320, D), F32)] * 2,
    )
    return outs[:4], *outs[4:]


def expert_grads_kernel(
    core_ref, rows_ref, d_result_ref, act_own, dh_own, act_other, dh_other, out_ref, turned_ref
):
    @pl.when((pl.program_id(0) == 0) & (pl.program_id(1) == 0))
    def _():
        turned_ref[...] = rows_ref[...].T

    for place, act_ref, dh_ref in ((0, act_own, dh_own), (1, act_other, dh_other)):
        @pl.when(pl.program_id(0) == place)
        def _():
            grad = dot(turned_ref[...], dh_ref[...], 1, 0).astype(BF16)
            out_ref[0, :, 0] = grad.reshape(N_SHARD, 48, 768)
            grad = dot(act_ref[...], d_result_ref[...], 0, 0).astype(BF16)
            out_ref[0, :, 1] = grad.reshape(N_SHARD, 48, 768)


def expert_grads(core, rows, d_result, act_own, dh_own, act_other, dh_other):
    whole = pl.BlockSpec((320, D), lambda h, i, c: (0, 0))
    mine = pl.BlockSpec((320, 768), lambda h, i, c: (0, jnp.where(h == 0, i, 1)))
    theirs = pl.BlockSpec((320, 768), lambda h, i, c: (0, jnp.where(h == 0, 0, i)))
    return pl.pallas_call(
        expert_grads_kernel,
        out_shape=shape((2, N_SHARD, 4, 48, D), BF16),
        grid_spec=pltpu.PrefetchScalarGridSpec(
            num_scalar_prefetch=1,
            grid=(2, 2),
            in_specs=[whole, whole, mine, mine, theirs, theirs],
            out_specs=pl.BlockSpec(
                (1, N_SHARD, 2, 48, D), lambda h, i, c: (jnp.where(h == 0, c[0], 1 - c[0]), 0, i, 0, 0)
            ),
            scratch_shapes=[pltpu.VMEM((D, 320), BF16)],
        ),
        name="expert_grads",
        compiler_params=pltpu.CompilerParams(
            vmem_limit_bytes=LIMIT, dimension_semantics=("arbitrary", "arbitrary")
        ),
    )(core, rows, d_result, act_own, dh_own, act_other, dh_other)


def expert_grad_kernel(rows_ref, d_result_ref, act_ref, dh_ref, *refs):
    *extra, out_ref = refs
    for i, grad in enumerate((
        dot(rows_ref[...], dh_ref[...], 0, 0),
        dot(act_ref[...], d_result_ref[...], 0, 0),
    )):
        grad = grad.reshape(N_SHARD, 48, 768)
        if extra:
            grad = grad + extra[0][:, i].astype(F32)
        out_ref[:, i] = grad.astype(BF16)


def expert_grad(rows, d_result, active, d_hidden, extra=()):
    half = pl.BlockSpec((320, 768), lambda i: (0, i))
    return grid_call(
        expert_grad_kernel,
        [shape((N_SHARD, 4, 48, 768), BF16)],
        [pack_block()],
        [rows, d_result, active, d_hidden, *extra],
        [whole_block((320, D))] * 2 + [half] * 2 + [pack_block()] * len(extra),
        "expert_grad",
        [],
    )[0]


def combine_kernel(residual_ref, high_ref, low_ref, r0, r1, r2, r3, out_ref, rows_ref):
    for d, ref in enumerate((r0, r1, r2, r3)):
        rows_ref[CAP * d : CAP * (d + 1)] = ref[...]
    rows = rows_ref[...]
    total = residual_ref[...] + dot(high_ref[...], rows, 1, 0) + dot(low_ref[...], rows, 1, 0)
    out_ref[...] = total.astype(BF16)


def combine(residual, high, low, blocks):
    return call(
        combine_kernel,
        [shape((ROWS, D), BF16)],
        [residual, high, low, *blocks],
        "combine",
        scratch=[pltpu.VMEM((320, D), BF16)],
    )[0]


def middle_back_kernel(paired, me_ref, d_out_ref, *refs):
    me = me_ref[0]
    count = 4 if paired else 8
    blocks, refs = refs[:count], refs[count:]
    gathered, refs = refs[:4], refs[4:]
    (
        chosen_ref, gates_ref, residual_ref, normed_ref, gain_ref, w0, w1, w2, w3,
        d_residual_ref, small_ref, grad_ref, m0, m1, m2, m3, rows_ref, d_rows_ref, back_ref,
    ) = refs
    for d in range(N_SEQ):
        there = pl.ds(CAP * d, CAP)
        rows_ref[there] = blocks[d][0] if paired else blocks[d][...]
        d_rows_ref[there] = blocks[d][1] if paired else blocks[4 + d][...]
    d_out = d_out_ref[...]
    chosen = chosen_ref[...]
    gates = gates_ref[...]
    products = dot(d_out, rows_ref[...], 1, 1) * chosen.astype(F32)
    slot = lax.broadcasted_iota(jnp.int32, (ROWS, 320), 1)
    own = jnp.where(slot >= 160, jnp.where(slot >= 240, 3, 2), jnp.where(slot >= 80, 1, 0))
    own = lax.rem(own + me, N_SEQ)
    lane = lax.broadcasted_iota(jnp.int32, (ROWS, 64), 1)
    d_gates = jnp.zeros((ROWS, 64), F32)
    for e in range(N_SEQ):
        part = jnp.sum(jnp.where(own == e, products, 0.0), axis=1, keepdims=True)
        d_gates = jnp.where(lane == e, part, d_gates)
    d_logits = gates * (d_gates - jnp.sum(gates * d_gates, axis=1, keepdims=True))
    d_normed = dot(chosen, d_rows_ref[...], 1, 0)
    for e in range(N_SEQ):
        d_normed = d_normed + d_logits[:, e : e + 1] * gain_ref[e : e + 1, :]
    n, inverse = norm_parts(residual_ref[...])
    d_residual = d_out.astype(F32) + norm_back(n, inverse, gain_ref[5:6, :], d_normed)
    d_residual_ref[...] = d_residual
    d_branch = d_residual.astype(BF16)
    for d, (ref, w_ref) in enumerate(zip((m0, m1, m2, m3), (w0, w1, w2, w3))):
        group = lax.rem(me - d + N_SEQ, N_SEQ)
        ref[...] = dot(d_branch, w_ref[...], 1, 1).astype(BF16)
        back_ref[group] = dot(gathered[d][...], d_branch, 0, 0).astype(BF16)
    grad_ref[...] = back_ref[...].reshape(D, D)
    high, low = two_parts(d_logits)
    small = dot(normed_ref[...], high, 0, 0) + dot(normed_ref[...], low, 0, 0)
    column = (lax.broadcasted_iota(jnp.int32, (ROWS, 64), 1) == 5).astype(BF16)
    high, low = two_parts(d_normed * n)
    small = small + dot(high, column, 0, 0) + dot(low, column, 0, 0)
    small_ref[...] = small


def middle_back(me, d_out, blocks, gathered, chosen, gates, residual, normed, gains, w_back, paired):
    outs = call(
        partial(middle_back_kernel, paired),
        [
            shape((ROWS, D), F32),
            shape((D, 64), F32),
            shape((D, D), BF16),
        ]
        + [shape((ROWS, 192), BF16)] * 4,
        [me, d_out, *blocks, *gathered, chosen, gates, residual, normed, gains, *w_back],
        "middle_back",
        scalars=1,
        scratch=[pltpu.VMEM((320, D), BF16)] * 2 + [pltpu.VMEM((N_SEQ, 192, D), BF16)],
    )
    return *outs[:3], outs[3:]


def finish_kernel(further, d_residual_ref, x_ref, gain_ref, b0, b1, b2, b3, *refs):
    d_normed = b0[...].astype(F32) + b1[...].astype(F32) + b2[...].astype(F32) + b3[...].astype(F32)
    n, inverse = norm_parts(x_ref[...].astype(F32))
    total = d_residual_ref[...] + norm_back(n, inverse, gain_ref[4:5, :], d_normed)
    if not further:
        refs[0][...] = total.astype(BF16)
        return
    high_ref, low_ref, out_ref, *sent = refs
    d_out = total.astype(BF16)
    out_ref[...] = d_out
    rows = dot(high_ref[...], d_out, 0, 0) + dot(low_ref[...], d_out, 0, 0)
    for d in range(N_SEQ):
        sent[d][...] = rows[CAP * d : CAP * (d + 1)].astype(BF16)


def finish(d_residual, x, gains, blocks, weights):
    further = weights is not None
    outs = call(
        partial(finish_kernel, further),
        [shape((ROWS, D), BF16)] + [shape((CAP, D), BF16)] * (4 if further else 0),
        [d_residual, x, gains, *blocks] + (list(weights) if further else []),
        "finish",
    )
    return outs[0], outs[1:]


def attention_weights(x_blocks, w_qkv, w_proj, w_route, gain_attn, gain_ffn):
    mine = w_qkv.reshape(12, 3, N_SEQ, 192).transpose(2, 0, 1, 3).reshape(N_SEQ, 12, 576)
    small = jnp.concatenate(
        [w_route, gain_attn[:, None], gain_ffn[:, None], jnp.zeros((12, 58), BF16)], axis=1
    )
    mine = jnp.concatenate([mine, jnp.broadcast_to(small, (N_SEQ, 12, 64))], axis=2)
    arrived = lax.all_to_all(mine, "seq", 0, 0, tiled=True).reshape(48, 640)
    back = w_proj.reshape(12, N_SEQ, 192).transpose(1, 0, 2).reshape(48, 192)
    pack = jnp.concatenate([arrived, back], axis=1)
    near = jnp.stack(from_ring(tie(pack, x_blocks), "x"))
    far = from_ring(near, "z")
    return far, *unpack(far)


def both_layers(mine):
    core = lax.axis_index("section")
    other = swap(mine)
    return [jnp.where(core == s, mine, other) for s in range(2)]


def half_packs(w_in, w_out):
    core = lax.axis_index("section")
    first = w_in.reshape(48, N_SHARD, 4, 48).transpose(2, 0, 1, 3).reshape(4, 48, 768)
    second = w_out.reshape(4, 48, 768)
    quarters = jnp.stack([first, second], axis=1).reshape(2, 4, 48, 768)
    mine = pick(quarters, core)
    arrived = swap(pick(quarters, 1 - core))
    return [jnp.where(core == s, mine, arrived) for s in range(2)]


def shards(images_in, out_grad, routes, w_qkv, w_proj, w_route, gain_attn, gain_ffn, w_in, w_out):
    core = lax.axis_index("section")
    me = lax.axis_index("seq").astype(jnp.int32).reshape(1)
    core_index = core.astype(jnp.int32).reshape(1)
    own_routes = routes[0, :, 0]
    mine = pick(own_routes, core)
    arrived = swap(pick(own_routes, 1 - core))
    route_of = (jnp.where(core == 0, mine, arrived), jnp.where(core == 0, arrived, mine))
    x0 = pick(images_in, core)[0]
    d_last = pick(out_grad, core)[0]
    halves = half_packs(w_in[0, 0], w_out[0, 0])
    x_blocks = [x0] + [turn(x0, -d) for d in (1, 2, 3)]
    far, rows, back_rows = attention_weights(
        x_blocks, w_qkv[0], w_proj[0], w_route[0], gain_attn[0], gain_ffn[0]
    )
    own = lax.all_gather(tie(halves[0], far), "shard", axis=0, tiled=False)
    attn_rows = both_layers(rows)
    back_rows = both_layers(back_rows)
    attn_rows[0], attn_rows[1], back_rows[0], back_rows[1] = lax.optimization_barrier(
        (attn_rows[0], attn_rows[1], back_rows[0], back_rows[1])
    )
    tables = [v[:, 576:584].T.astype(F32) for v in attn_rows]
    w_back = [[back_rows[0]] + [turn(back_rows[0], d) for d in (1, 2, 3)], None]
    experts = [None, None]

    saved = []
    x = x0
    layer_outs = []
    for s in range(2):
        if s == 1:
            x_blocks = [x] + [turn(x, -d) for d in (1, 2, 3)]
        mixture, x_all, packed, logs = attend(x_blocks, attn_rows[s], tables[s])
        if s == 0:
            w_back[0], mixture = lax.optimization_barrier((w_back[0], mixture))
        else:
            later, mixture[0] = lax.optimization_barrier((later, mixture[0]))
            experts[1] = (later, swap(later))
        gathered = send_out(mixture)
        d_out = d_last if s == 1 else None
        residual, normed, gates, chosen, high, low, buffer = middle(
            me, x, gathered, w_back[s], attn_rows[s], tables[s], route_of[s], d_out
        )
        blocks = send_out(buffer)
        kept = (x, x_all, packed, logs, gathered, residual, normed, gates, chosen, high, low, blocks)
        if s == 0:
            own = tie(own, blocks)
            experts[0] = (own, swap(own))
            later = lax.all_gather(tie(halves[1], own), "shard", axis=0, tiled=False)
            later_back = tie(back_rows[1], blocks)
            w_back[1] = [later_back] + [turn(later_back, d) for d in (1, 2, 3)]
            result = expert_run(blocks, *experts[s])
            w_back[1], result = lax.optimization_barrier((w_back[1], result))
            returned = send_back(result)
            x = combine(residual, high, low, returned)
            layer_outs.append(x)
            saved.append((kept, returned))
        else:
            saved.append((kept, None))

    d_out = d_last
    d_buffer = None
    in_grads = [None, None]
    expert_sums = [None, None]
    attn_grads = [None, None]
    for s in (1, 0):
        kept, returned = saved[s]
        x, x_all, packed, logs, gathered, residual, normed, gates, chosen, high, low, blocks = kept
        if s == 1:
            sent, *states = expert_back(blocks, experts[s], True)
            arrived = send_back(sent)
            layer_outs.append(combine(residual, high, low, [v[0] for v in arrived]))
        else:
            sent, *states = expert_back([*blocks, *send_out(d_buffer)], experts[s], False)
            back = send_back(sent)
            arrived = [*returned, *back]
        d_residual, small, grad_back, d_mixture = middle_back(
            me, d_out, arrived, gathered, chosen, gates, residual, normed, tables[s], w_back[s], s == 1
        )
        d_heads = send_back(d_mixture)
        rows, d_result, act_own, act_other, dh_own, dh_other = states
        if s == 1:
            both = expert_grads(core_index, rows, d_result, act_own, dh_own, act_other, dh_other)
            both = both.reshape(2 * N_SHARD, 4, 48, D)
            group = ("section", "shard")
        else:
            other = swap(expert_grad(rows, d_result, act_other, dh_other))
            both = expert_grad(rows, d_result, act_own, dh_own, (tie(other, back),))
            group = "shard"
        expert_sums[s] = lax.psum_scatter(both, group, scatter_dimension=0, tiled=True)[0]
        d_normed, grad_mix = attend_back(x_all, attn_rows[s], tables[s], packed, logs, d_heads, small)
        d_parts = send_out(d_normed)
        keep = jnp.where(core == 0, grad_mix, grad_back)
        give = jnp.where(core == 0, grad_back, grad_mix)
        attn_grads[s] = (keep.astype(F32) + swap(give).astype(F32)).astype(BF16)
        weights = saved[0][0][9:11] if s == 1 else None
        d_out, d_buffer = finish(d_residual, x, tables[s], d_parts, weights)
        in_grads[s] = d_out

    pair = jnp.concatenate(attn_grads, axis=1).reshape(N_SEQ * N_SHARD, 12, 12, 128)
    pair = pair.transpose(0, 2, 1, 3).reshape(N_SEQ * N_SHARD, 144, 128)
    pair = tie(pair, d_parts)
    arrived = lax.all_to_all(pair, ("seq", "shard"), 0, 0, tiled=True)
    attn_sum = jnp.sum(arrived.reshape(N_SEQ, N_SHARD, 144, 128).astype(F32), axis=1)
    attn_sums = [attn_sum[:, :72], attn_sum[:, 72:]]

    def settle(pair):
        keep = jnp.where(core == 0, pair[0], pair[1])
        give = jnp.where(core == 0, pair[1], pair[0])
        return keep, swap(give)

    def in_order(keep, got):
        return jnp.where(core == 0, jnp.stack([keep, got]), jnp.stack([got, keep]))

    layer_out = in_order(*settle(layer_outs))
    in_grad = in_order(*settle(in_grads))
    grad_in, grad_out = reorder(core_index, *settle(expert_sums))
    attn_sum = in_order(*settle(attn_sums)).reshape(2, N_SEQ, 6, 12, 128)
    attn_sum = attn_sum.transpose(0, 1, 3, 2, 4).reshape(2, N_SEQ, 12, D)
    mix = attn_sum[0]
    back = jnp.sum(attn_sum[1], axis=0)
    grad_qkv = mix[:, :, :576].reshape(N_SEQ, 12, 3, 192).transpose(1, 2, 0, 3).reshape(12, 3 * D)
    small = jnp.sum(mix[:, :, 576:640], axis=0)
    return (
        layer_out[None, :, None],
        in_grad[None, :, None],
        grad_qkv[None],
        back[None],
        small[None, :, 0:4],
        small[None, :, 4],
        small[None, :, 5],
        grad_in[None],
        grad_out[None],
    )


def solution(mesh):
    def run(*args):
        outs = shards(*args)
        outs = list(outs)
        outs[7] = outs[7][:, None]
        outs[8] = outs[8][:, None]
        return tuple(outs)

    return jax.shard_map(
        run,
        mesh=mesh,
        in_specs=(
            P(None, "shard", "seq", None),
            P(None, "shard", "seq", None),
            P("section", None, "shard", "seq", None),
            P("section", ("seq", "shard"), None),
            P("section", ("seq", "shard"), None),
            P("section", ("seq", "shard"), None),
            P("section", ("seq", "shard")),
            P("section", ("seq", "shard")),
            P("section", "seq", "shard", None),
            P("section", "seq", "shard", None),
        ),
        out_specs=(
            P("section", None, "shard", "seq", None),
            P("section", None, "shard", "seq", None),
            P("section", ("seq", "shard"), None),
            P("section", ("seq", "shard"), None),
            P("section", ("seq", "shard"), None),
            P("section", ("seq", "shard")),
            P("section", ("seq", "shard")),
            P("section", "seq", "shard", None),
            P("section", "seq", "shard", None),
        ),
        check_vma=False,
    )
```

```python
from functools import partial

import jax
import jax.numpy as jnp
from jax import lax
from jax.experimental import pallas as pl
from jax.experimental.pallas import tpu as pltpu
from jax.sharding import PartitionSpec as P

D = 768
FF = 3072
HEAD_DIM = 64
CAP = 80
N_SEQ = 4
N_SHARD = 16
GROUP = 3
ROWS = 144
SEQ = 576
WIDE = 1472
LIMIT = 56 * 1024 * 1024
EPSILON = 1e-06
F32 = jnp.float32
BF16 = jnp.bfloat16


def dot(a, b, ca, cb):
    return lax.dot_general(a, b, (((ca,), (cb,)), ((), ())), preferred_element_type=F32)


def swap(v):
    return lax.ppermute(v, "section", [(0, 1), (1, 0)])


def turn(v, d):
    return lax.ppermute(v, "seq", [(i, (i + d) % N_SEQ) for i in range(N_SEQ)])


def hop(v, axis, d):
    route = []
    for z in range(4):
        for x in range(4):
            to = ((z + d) % 4) * 4 + x if axis == "z" else z * 4 + (x + d) % 4
            route.append((z * 4 + x, to))
    return lax.ppermute(v, "shard", route)


def from_ring(v, axis):
    return [v] + [hop(v, axis, -d) for d in (1, 2, 3)]


def pick(v, i):
    return lax.dynamic_index_in_dim(v, i, 0, keepdims=False)


def tie(value, other):
    return lax.optimization_barrier((value, other))[0]


def norm_parts(values):
    centred = values - jnp.mean(values, axis=-1, keepdims=True)
    inverse = lax.rsqrt(jnp.mean(centred * centred, axis=-1, keepdims=True) + EPSILON)
    return centred * inverse, inverse


def norm_back(n, inverse, gain, dy):
    gdy = dy * gain
    return (
        gdy
        - jnp.mean(gdy, axis=-1, keepdims=True)
        - n * jnp.mean(gdy * n, axis=-1, keepdims=True)
    ) * inverse


def two_parts(v):
    high = v.astype(BF16)
    return high, (v - high.astype(F32)).astype(BF16)


def gather_tokens(x):
    return jnp.concatenate([x] + [turn(x, -d) for d in (1, 2, 3)], axis=0)


def send_out(blocks):
    return [blocks[0]] + [turn(blocks[d], d) for d in (1, 2, 3)]


def send_back(blocks):
    return [blocks[0]] + [turn(blocks[d], -d) for d in (1, 2, 3)]


def vmem():
    return pl.BlockSpec(memory_space=pltpu.VMEM)


def smem():
    return pl.BlockSpec(memory_space=pltpu.SMEM)


def shape(dims, kind):
    return jax.ShapeDtypeStruct(dims, kind)


def call(body, outs, ins, name, scalars=0, scratch=()):
    specs = [smem()] * scalars + [vmem()] * (len(ins) - scalars)
    return pl.pallas_call(
        body,
        out_shape=outs,
        in_specs=specs,
        out_specs=[vmem()] * len(outs),
        scratch_shapes=list(scratch),
        name=name,
        compiler_params=pltpu.CompilerParams(vmem_limit_bytes=LIMIT),
    )(*ins)


def attend_kernel(x0, x1, x2, x3, w_ref, gain_ref, m0, m1, m2, m3, x_ref, packed_ref, log_ref):
    for d, ref in enumerate((x0, x1, x2, x3)):
        x_ref[ROWS * d : ROWS * (d + 1)] = ref[...]
    n, _ = norm_parts(x_ref[...].astype(F32))
    normed = (n * gain_ref[4:5, :]).astype(BF16)
    packed_ref[...] = dot(normed, w_ref[:, 0:576], 1, 0).astype(BF16)
    lane = lax.broadcasted_iota(jnp.int32, (SEQ, 128), 1)
    logs = jnp.zeros((SEQ, 128), F32)
    outs = []
    for h in range(GROUP):
        query = packed_ref[:, 64 * h : 64 * h + 64]
        key = packed_ref[:, 192 + 64 * h : 256 + 64 * h]
        value = packed_ref[:, 384 + 64 * h : 448 + 64 * h]
        scores = dot(query, key, 1, 1) * HEAD_DIM ** (-0.5)
        top = jnp.max(scores, axis=1, keepdims=True)
        exponent = jnp.exp(scores - top)
        total = jnp.sum(exponent, axis=1, keepdims=True)
        outs.append((dot(exponent.astype(BF16), value, 1, 0) / total).astype(BF16))
        logs = jnp.where(lane == h, top + jnp.log(total), logs)
    log_ref[...] = logs
    mixture = jnp.concatenate(outs, axis=1)
    for d, ref in enumerate((m0, m1, m2, m3)):
        ref[...] = mixture[ROWS * d : ROWS * (d + 1)]


def attend(x_blocks, w_mix, gains):
    outs = call(
        attend_kernel,
        [shape((ROWS, 192), BF16)] * 4
        + [shape((SEQ, D), BF16), shape((SEQ, 576), BF16), shape((SEQ, 128), F32)],
        [*x_blocks, w_mix, gains],
        "attention",
    )
    return list(outs[:4]), *outs[4:]


def attend_back_kernel(
    x_ref, w_ref, gain_ref, packed_ref, log_ref, d0, d1, d2, d3, small_ref,
    n0, n1, n2, n3, grad_ref, d_packed_ref, d_mix_ref,
):
    for d, ref in enumerate((d0, d1, d2, d3)):
        d_mix_ref[ROWS * d : ROWS * (d + 1)] = ref[...]
    scaling = HEAD_DIM ** (-0.5)
    parts = [[], [], []]
    for h in range(GROUP):
        query = packed_ref[:, 64 * h : 64 * h + 64]
        key = packed_ref[:, 192 + 64 * h : 256 + 64 * h]
        value = packed_ref[:, 384 + 64 * h : 448 + 64 * h]
        d_out = d_mix_ref[:, 64 * h : 64 * h + 64]
        attention = jnp.exp(dot(query, key, 1, 1) * scaling - log_ref[:, h : h + 1])
        parts[2].append(dot(attention.astype(BF16), d_out, 0, 0).astype(BF16))
        d_att = dot(d_out, value, 1, 1)
        centre = jnp.sum(attention * d_att, axis=1, keepdims=True)
        d_scores = (attention * (d_att - centre) * scaling).astype(BF16)
        parts[0].append(dot(d_scores, key, 1, 0).astype(BF16))
        parts[1].append(dot(d_scores, query, 0, 0).astype(BF16))
    d_packed_ref[...] = jnp.concatenate(parts[0] + parts[1] + parts[2], axis=1)
    n, _ = norm_parts(x_ref[...].astype(F32))
    normed = (n * gain_ref[4:5, :]).astype(BF16)
    d_packed = d_packed_ref[...]
    d_normed = dot(d_packed, w_ref[:, 0:576], 1, 1)
    for d, ref in enumerate((n0, n1, n2, n3)):
        ref[...] = d_normed[ROWS * d : ROWS * (d + 1)].astype(BF16)
    column = (lax.broadcasted_iota(jnp.int32, (SEQ, 64), 1) == 4).astype(BF16)
    high, low = two_parts(d_normed * n)
    small = small_ref[...] + dot(high, column, 0, 0) + dot(low, column, 0, 0)
    grad = dot(normed, d_packed, 0, 0)
    grad = jnp.concatenate([grad, small, jnp.zeros((D, 128), F32)], axis=1)
    grad_ref[...] = grad.astype(BF16)


def attend_back(x_all, w_mix, gains, packed, logs, d_heads, small):
    outs = call(
        attend_back_kernel,
        [shape((ROWS, D), BF16)] * 4 + [shape((D, D), BF16)],
        [x_all, w_mix, gains, packed, logs, *d_heads, small],
        "attention_back",
        scratch=[pltpu.VMEM((SEQ, 576), BF16), pltpu.VMEM((SEQ, 192), BF16)],
    )
    return outs[:4], outs[4]


def order_rows(first, second):
    i = lax.broadcasted_iota(jnp.int32, (D, 1), 0)
    outer = lax.div(i, 12 * first)
    left = i - 12 * first * outer
    inner = lax.div(left, 12)
    source = inner * (12 * second) + outer * 12 + left - 12 * inner
    return (lax.broadcasted_iota(jnp.int32, (D, D), 1) == source).astype(BF16)


def unpack_kernel(where_ref, b0, b1, b2, b3, rows_ref, back_ref, all_ref):
    z, x = where_ref[0], where_ref[1]
    for dz, ref in enumerate((b0, b1, b2, b3)):
        for dx in range(4):
            all_ref[lax.rem(z + dz, 4) * 4 + lax.rem(x + dx, 4)] = ref[dx]
    whole = all_ref[...].reshape(D, 832)
    ordered = dot(order_rows(N_SHARD, N_SEQ), whole, 1, 0).astype(BF16)
    rows_ref[...] = ordered[:, :640]
    for chunk in range(N_SEQ):
        back_ref[:, 192 * chunk : 192 * (chunk + 1)] = ordered[192 * chunk : 192 * (chunk + 1), 640:]


def unpack(blocks):
    i = lax.axis_index("shard").astype(jnp.int32)
    return call(
        unpack_kernel,
        [shape((D, 640), BF16), shape((192, D), BF16)],
        [jnp.stack([i // 4, lax.rem(i, 4)]), *blocks],
        "unpack",
        scalars=1,
        scratch=[pltpu.VMEM((N_SHARD, 48, 832), BF16)],
    )


def reorder_kernel(core_ref, keep_ref, got_ref, in_ref, out_ref):
    def write(halves):
        columns = []
        for shard in range(N_SHARD):
            for p in range(4):
                block = halves[p // 2][2 * (p % 2)]
                columns.append(block[:, 48 * shard : 48 * (shard + 1)])
        in_ref[...] = jnp.concatenate(columns, axis=1).astype(F32)
        for p in range(4):
            out_ref[48 * p : 48 * (p + 1)] = halves[p // 2][2 * (p % 2) + 1].astype(F32)

    @pl.when(core_ref[0] == 0)
    def _():
        write((keep_ref, got_ref))

    @pl.when(core_ref[0] == 1)
    def _():
        write((got_ref, keep_ref))


def reorder(core, keep, got):
    return call(
        reorder_kernel,
        [shape((48, FF), F32), shape((192, D), F32)],
        [core, keep, got],
        "reorder",
        scalars=1,
    )


def middle_kernel(
    layer, me_ref, x_ref, g0, g1, g2, g3, w0, w1, w2, w3, router_ref, gain_ref, route_ref, *refs
):
    me = me_ref[0]
    extra = layer == 1
    if extra:
        d_out_ref, *refs = refs
    residual_ref, normed_ref, gates_ref, chosen_ref, high_ref, low_ref, *sent = refs
    residual = x_ref[...].astype(F32)
    for ref, w_ref in zip((g0, g1, g2, g3), (w0, w1, w2, w3)):
        residual = residual + dot(ref[...], w_ref[...], 1, 0)
    residual_ref[...] = residual
    n, _ = norm_parts(residual)
    normed = (n * gain_ref[5:6, :]).astype(BF16)
    normed_ref[...] = normed
    lane = lax.broadcasted_iota(jnp.int32, (ROWS, 64), 1)
    logits = jnp.where(lane < 4, dot(normed, router_ref[:, 576:640], 1, 0), -1e30)
    logits = logits - jnp.max(logits, axis=1, keepdims=True)
    gates = jnp.exp(logits)
    gates = gates / jnp.sum(gates, axis=1, keepdims=True)
    gates_ref[...] = gates
    routes = route_ref[...]
    relative = lax.rem(routes - me + N_SEQ, N_SEQ)
    named = (lane == relative[:, 0:1]) | (lane == relative[:, 1:2])
    row = lax.broadcasted_iota(jnp.int32, (ROWS, ROWS), 0)
    column = lax.broadcasted_iota(jnp.int32, (ROWS, ROWS), 1)
    before = (row > column).astype(BF16)
    rank = dot(before, named.astype(BF16), 1, 0)
    slot = lax.broadcasted_iota(jnp.int32, (ROWS, 320), 1)
    own = jnp.where(slot >= 160, jnp.where(slot >= 240, 3, 2), jnp.where(slot >= 80, 1, 0))
    place = (slot - CAP * own).astype(F32)
    wanted = jnp.full((ROWS, 320), -1.0, F32)
    spread = jnp.zeros((ROWS, 320), F32)
    position = jnp.where(named, rank, -1.0)
    for e in range(N_SEQ):
        wanted = jnp.where(own == e, position[:, e : e + 1], wanted)
        spread = jnp.where(lax.rem(own + me, N_SEQ) == e, gates[:, e : e + 1], spread)
    taken = wanted == place
    chosen = taken.astype(BF16)
    high, low = two_parts(jnp.where(taken, spread, 0.0))
    chosen_ref[...] = chosen
    high_ref[...] = high
    low_ref[...] = low
    buffer = dot(chosen, normed, 0, 0).astype(BF16)
    if not extra:
        for d in range(N_SEQ):
            sent[d][...] = buffer[CAP * d : CAP * (d + 1)]
    else:
        d_out = d_out_ref[...]
        d_buffer = (dot(high, d_out, 0, 0) + dot(low, d_out, 0, 0)).astype(BF16)
        for d in range(N_SEQ):
            sent[d][0] = buffer[CAP * d : CAP * (d + 1)]
            sent[d][1] = d_buffer[CAP * d : CAP * (d + 1)]


def middle(me, x, gathered, w_back, router, gains, route_ids, d_out):
    extra = d_out is not None
    sent = (2, CAP, D) if extra else (CAP, D)
    outs = call(
        partial(middle_kernel, int(extra)),
        [
            shape((ROWS, D), F32),
            shape((ROWS, D), BF16),
            shape((ROWS, 64), F32),
            shape((ROWS, 320), BF16),
            shape((ROWS, 320), BF16),
            shape((ROWS, 320), BF16),
        ]
        + [shape(sent, BF16)] * 4,
        [me, x, *gathered, *w_back, router, gains, route_ids] + ([d_out] if extra else []),
        "middle",
        scalars=1,
    )
    return *outs[:6], outs[6:]


def gelu_of(hidden):
    cdf = 0.5 + 0.5 * lax.erf(hidden * 0.7071067811865476)
    return hidden * cdf, cdf


def quarter(ref, i):
    return ref[:, i].reshape(768, D)


def expert_first_kernel(r0, r1, r2, r3, pack, rows_ref, total):
    @pl.when(pl.program_id(0) == 0)
    def _():
        for d, ref in enumerate((r0, r1, r2, r3)):
            rows_ref[CAP * d : CAP * (d + 1)] = ref[...]
        total[...] = jnp.zeros_like(total)

    active = gelu_of(dot(rows_ref[...], quarter(pack, 0), 1, 0))[0].astype(BF16)
    total[...] += dot(active, quarter(pack, 1), 1, 0)


def expert_second_kernel(rows_ref, first_ref, pack, o0, o1, o2, o3, total):
    @pl.when(pl.program_id(0) == 0)
    def _():
        total[...] = first_ref[...]

    active = gelu_of(dot(rows_ref[...], quarter(pack, 0), 1, 0))[0].astype(BF16)
    total[...] += dot(active, quarter(pack, 1), 1, 0)

    @pl.when(pl.program_id(0) == 1)
    def _():
        for d, ref in enumerate((o0, o1, o2, o3)):
            ref[...] = total[CAP * d : CAP * (d + 1)].astype(BF16)


def whole_block(dims):
    return pl.BlockSpec(dims, lambda i: (0,) * len(dims))


def pack_block():
    return pl.BlockSpec((N_SHARD, 2, 48, 768), lambda i: (0, i, 0, 0))


def grid_call(body, outs, out_specs, ins, in_specs, name, scratch):
    return pl.pallas_call(
        body,
        grid=(2,),
        out_shape=outs,
        in_specs=in_specs,
        out_specs=out_specs,
        scratch_shapes=scratch,
        name=name,
        compiler_params=pltpu.CompilerParams(
            vmem_limit_bytes=LIMIT, dimension_semantics=("arbitrary",)
        ),
    )(*ins)


def expert_run(blocks, own, other):
    rows, first = grid_call(
        expert_first_kernel,
        [shape((320, D), BF16), shape((320, D), F32)],
        [whole_block((320, D))] * 2,
        [*blocks, own],
        [whole_block((CAP, D))] * 4 + [pack_block()],
        "expert_first",
        [],
    )
    return grid_call(
        expert_second_kernel,
        [shape((CAP, D), BF16)] * 4,
        [whole_block((CAP, D))] * 4,
        [rows, first, other],
        [whole_block((320, D))] * 2 + [pack_block()],
        "expert_second",
        [pltpu.VMEM((320, D), F32)],
    )


def expert_back_kernel(forward, *refs):
    ins, (own_ref, other_ref), refs = refs[: 4 if forward else 8], refs[4 if forward else 8 :][:2], refs[6 if forward else 10 :]
    sent, refs = refs[:4], refs[4:]
    rows_out, d_result_out, act_own, act_other, dh_own, dh_other, d_total, total = refs
    step = pl.program_id(0)

    @pl.when(step == 0)
    def _():
        for d in range(N_SEQ):
            there = pl.ds(CAP * d, CAP)
            rows_out[there] = ins[d][0] if forward else ins[d][...]
            d_result_out[there] = ins[d][1] if forward else ins[4 + d][...]
        d_total[...] = jnp.zeros_like(d_total)
        if forward:
            total[...] = jnp.zeros_like(total)

    rows = rows_out[...]
    d_result = d_result_out[...]
    for pack, act_ref, dh_ref in ((own_ref, act_own, dh_own), (other_ref, act_other, dh_other)):
        hidden = dot(rows, quarter(pack, 0), 1, 0)
        value, cdf = gelu_of(hidden)
        active = value.astype(BF16)
        act_ref[...] = active
        slope = cdf + hidden * jnp.exp(-0.5 * hidden * hidden) * 0.3989422804014327
        d_hidden = (dot(d_result, quarter(pack, 1), 1, 1) * slope).astype(BF16)
        dh_ref[...] = d_hidden
        d_total[...] += dot(d_hidden, quarter(pack, 0), 1, 1)
        if forward:
            total[...] += dot(active, quarter(pack, 1), 1, 0)

    @pl.when(step == 1)
    def _():
        for d in range(N_SEQ):
            there = pl.ds(CAP * d, CAP)
            if forward:
                sent[d][0] = total[there].astype(BF16)
                sent[d][1] = d_total[there].astype(BF16)
            else:
                sent[d][...] = d_total[there].astype(BF16)


def expert_back(blocks, packs, forward):
    half = pl.BlockSpec((320, 768), lambda i: (0, i))
    block = whole_block((2, CAP, D)) if forward else whole_block((CAP, D))
    sent = (2, CAP, D) if forward else (CAP, D)
    outs = grid_call(
        partial(expert_back_kernel, forward),
        [shape(sent, BF16)] * 4 + [shape((320, D), BF16)] * 2 + [shape((320, 1536), BF16)] * 4,
        [whole_block(sent)] * 4 + [whole_block((320, D))] * 2 + [half] * 4,
        [*blocks, *packs],
        [block] * len(blocks) + [pack_block()] * 2,
        "expert_back",
        [pltpu.VMEM((320, D), F32)] * 2,
    )
    return outs[:4], *outs[4:]


def expert_grads_kernel(
    core_ref, rows_ref, d_result_ref, act_own, dh_own, act_other, dh_other, out_ref, turned_ref
):
    @pl.when((pl.program_id(0) == 0) & (pl.program_id(1) == 0))
    def _():
        turned_ref[...] = rows_ref[...].T

    for place, act_ref, dh_ref in ((0, act_own, dh_own), (1, act_other, dh_other)):
        @pl.when(pl.program_id(0) == place)
        def _():
            grad = dot(turned_ref[...], dh_ref[...], 1, 0).astype(BF16)
            out_ref[0, :, 0] = grad.reshape(N_SHARD, 48, 768)
            grad = dot(act_ref[...], d_result_ref[...], 0, 0).astype(BF16)
            out_ref[0, :, 1] = grad.reshape(N_SHARD, 48, 768)


def expert_grads(core, rows, d_result, act_own, dh_own, act_other, dh_other):
    whole = pl.BlockSpec((320, D), lambda h, i, c: (0, 0))
    mine = pl.BlockSpec((320, 768), lambda h, i, c: (0, jnp.where(h == 0, i, 1)))
    theirs = pl.BlockSpec((320, 768), lambda h, i, c: (0, jnp.where(h == 0, 0, i)))
    return pl.pallas_call(
        expert_grads_kernel,
        out_shape=shape((2, N_SHARD, 4, 48, D), BF16),
        grid_spec=pltpu.PrefetchScalarGridSpec(
            num_scalar_prefetch=1,
            grid=(2, 2),
            in_specs=[whole, whole, mine, mine, theirs, theirs],
            out_specs=pl.BlockSpec(
                (1, N_SHARD, 2, 48, D), lambda h, i, c: (jnp.where(h == 0, c[0], 1 - c[0]), 0, i, 0, 0)
            ),
            scratch_shapes=[pltpu.VMEM((D, 320), BF16)],
        ),
        name="expert_grads",
        compiler_params=pltpu.CompilerParams(
            vmem_limit_bytes=LIMIT, dimension_semantics=("arbitrary", "arbitrary")
        ),
    )(core, rows, d_result, act_own, dh_own, act_other, dh_other)


def expert_grad_kernel(rows_ref, d_result_ref, act_ref, dh_ref, *refs):
    *extra, out_ref = refs
    for i, grad in enumerate((
        dot(rows_ref[...], dh_ref[...], 0, 0),
        dot(act_ref[...], d_result_ref[...], 0, 0),
    )):
        grad = grad.reshape(N_SHARD, 48, 768)
        if extra:
            grad = grad + extra[0][:, i].astype(F32)
        out_ref[:, i] = grad.astype(BF16)


def expert_grad(rows, d_result, active, d_hidden, extra=()):
    half = pl.BlockSpec((320, 768), lambda i: (0, i))
    return grid_call(
        expert_grad_kernel,
        [shape((N_SHARD, 4, 48, 768), BF16)],
        [pack_block()],
        [rows, d_result, active, d_hidden, *extra],
        [whole_block((320, D))] * 2 + [half] * 2 + [pack_block()] * len(extra),
        "expert_grad",
        [],
    )[0]


def combine_kernel(residual_ref, high_ref, low_ref, r0, r1, r2, r3, out_ref, rows_ref):
    for d, ref in enumerate((r0, r1, r2, r3)):
        rows_ref[CAP * d : CAP * (d + 1)] = ref[...]
    rows = rows_ref[...]
    total = residual_ref[...] + dot(high_ref[...], rows, 1, 0) + dot(low_ref[...], rows, 1, 0)
    out_ref[...] = total.astype(BF16)


def combine(residual, high, low, blocks):
    return call(
        combine_kernel,
        [shape((ROWS, D), BF16)],
        [residual, high, low, *blocks],
        "combine",
        scratch=[pltpu.VMEM((320, D), BF16)],
    )[0]


def middle_back_kernel(paired, me_ref, d_out_ref, *refs):
    me = me_ref[0]
    count = 4 if paired else 8
    blocks, refs = refs[:count], refs[count:]
    gathered, refs = refs[:4], refs[4:]
    (
        chosen_ref, gates_ref, residual_ref, normed_ref, gain_ref, w0, w1, w2, w3,
        d_residual_ref, small_ref, grad_ref, m0, m1, m2, m3, rows_ref, d_rows_ref, back_ref,
    ) = refs
    for d in range(N_SEQ):
        there = pl.ds(CAP * d, CAP)
        rows_ref[there] = blocks[d][0] if paired else blocks[d][...]
        d_rows_ref[there] = blocks[d][1] if paired else blocks[4 + d][...]
    d_out = d_out_ref[...]
    chosen = chosen_ref[...]
    gates = gates_ref[...]
    products = dot(d_out, rows_ref[...], 1, 1) * chosen.astype(F32)
    slot = lax.broadcasted_iota(jnp.int32, (ROWS, 320), 1)
    own = jnp.where(slot >= 160, jnp.where(slot >= 240, 3, 2), jnp.where(slot >= 80, 1, 0))
    own = lax.rem(own + me, N_SEQ)
    lane = lax.broadcasted_iota(jnp.int32, (ROWS, 64), 1)
    d_gates = jnp.zeros((ROWS, 64), F32)
    for e in range(N_SEQ):
        part = jnp.sum(jnp.where(own == e, products, 0.0), axis=1, keepdims=True)
        d_gates = jnp.where(lane == e, part, d_gates)
    d_logits = gates * (d_gates - jnp.sum(gates * d_gates, axis=1, keepdims=True))
    d_normed = dot(chosen, d_rows_ref[...], 1, 0)
    for e in range(N_SEQ):
        d_normed = d_normed + d_logits[:, e : e + 1] * gain_ref[e : e + 1, :]
    n, inverse = norm_parts(residual_ref[...])
    d_residual = d_out.astype(F32) + norm_back(n, inverse, gain_ref[5:6, :], d_normed)
    d_residual_ref[...] = d_residual
    d_branch = d_residual.astype(BF16)
    for d, (ref, w_ref) in enumerate(zip((m0, m1, m2, m3), (w0, w1, w2, w3))):
        group = lax.rem(me - d + N_SEQ, N_SEQ)
        ref[...] = dot(d_branch, w_ref[...], 1, 1).astype(BF16)
        back_ref[group] = dot(gathered[d][...], d_branch, 0, 0).astype(BF16)
    grad_ref[...] = back_ref[...].reshape(D, D)
    high, low = two_parts(d_logits)
    small = dot(normed_ref[...], high, 0, 0) + dot(normed_ref[...], low, 0, 0)
    column = (lax.broadcasted_iota(jnp.int32, (ROWS, 64), 1) == 5).astype(BF16)
    high, low = two_parts(d_normed * n)
    small = small + dot(high, column, 0, 0) + dot(low, column, 0, 0)
    small_ref[...] = small


def middle_back(me, d_out, blocks, gathered, chosen, gates, residual, normed, gains, w_back, paired):
    outs = call(
        partial(middle_back_kernel, paired),
        [
            shape((ROWS, D), F32),
            shape((D, 64), F32),
            shape((D, D), BF16),
        ]
        + [shape((ROWS, 192), BF16)] * 4,
        [me, d_out, *blocks, *gathered, chosen, gates, residual, normed, gains, *w_back],
        "middle_back",
        scalars=1,
        scratch=[pltpu.VMEM((320, D), BF16)] * 2 + [pltpu.VMEM((N_SEQ, 192, D), BF16)],
    )
    return *outs[:3], outs[3:]


def finish_kernel(further, d_residual_ref, x_ref, gain_ref, b0, b1, b2, b3, *refs):
    d_normed = b0[...].astype(F32) + b1[...].astype(F32) + b2[...].astype(F32) + b3[...].astype(F32)
    n, inverse = norm_parts(x_ref[...].astype(F32))
    total = d_residual_ref[...] + norm_back(n, inverse, gain_ref[4:5, :], d_normed)
    if not further:
        refs[0][...] = total.astype(BF16)
        return
    high_ref, low_ref, out_ref, *sent = refs
    d_out = total.astype(BF16)
    out_ref[...] = d_out
    rows = dot(high_ref[...], d_out, 0, 0) + dot(low_ref[...], d_out, 0, 0)
    for d in range(N_SEQ):
        sent[d][...] = rows[CAP * d : CAP * (d + 1)].astype(BF16)


def finish(d_residual, x, gains, blocks, weights):
    further = weights is not None
    outs = call(
        partial(finish_kernel, further),
        [shape((ROWS, D), BF16)] + [shape((CAP, D), BF16)] * (4 if further else 0),
        [d_residual, x, gains, *blocks] + (list(weights) if further else []),
        "finish",
    )
    return outs[0], outs[1:]


def attention_weights(x, w_qkv, w_proj, w_route, gain_attn, gain_ffn):
    mine = w_qkv.reshape(12, 3, N_SEQ, 192).transpose(2, 0, 1, 3).reshape(N_SEQ, 12, 576)
    small = jnp.concatenate(
        [w_route, gain_attn[:, None], gain_ffn[:, None], jnp.zeros((12, 58), BF16)], axis=1
    )
    mine = jnp.concatenate([mine, jnp.broadcast_to(small, (N_SEQ, 12, 64))], axis=2)
    arrived = lax.all_to_all(mine, "seq", 0, 0, tiled=True).reshape(48, 640)
    back = w_proj.reshape(12, N_SEQ, 192).transpose(1, 0, 2).reshape(48, 192)
    pack = jnp.concatenate([arrived, back], axis=1)
    near, x = lax.optimization_barrier((jnp.stack(from_ring(pack, "x")), x))
    far = from_ring(near, "z")
    x_blocks = [x] + [turn(x, -d) for d in (1, 2, 3)]
    far, x_blocks = lax.optimization_barrier((far, x_blocks))
    return far, x_blocks, *unpack(far)


def both_layers(mine):
    core = lax.axis_index("section")
    other = swap(mine)
    return [jnp.where(core == s, mine, other) for s in range(2)]


def half_packs(w_in, w_out):
    core = lax.axis_index("section")
    first = w_in.reshape(48, N_SHARD, 4, 48).transpose(2, 0, 1, 3).reshape(4, 48, 768)
    second = w_out.reshape(4, 48, 768)
    quarters = jnp.stack([first, second], axis=1).reshape(2, 4, 48, 768)
    mine = pick(quarters, core)
    arrived = swap(pick(quarters, 1 - core))
    return [jnp.where(core == s, mine, arrived) for s in range(2)]


def shards(images_in, out_grad, routes, w_qkv, w_proj, w_route, gain_attn, gain_ffn, w_in, w_out):
    core = lax.axis_index("section")
    me = lax.axis_index("seq").astype(jnp.int32).reshape(1)
    core_index = core.astype(jnp.int32).reshape(1)
    own_routes = routes[0, :, 0]
    mine = pick(own_routes, core)
    arrived = swap(pick(own_routes, 1 - core))
    route_of = (jnp.where(core == 0, mine, arrived), jnp.where(core == 0, arrived, mine))
    x0 = pick(images_in, core)[0]
    d_last = pick(out_grad, core)[0]
    halves = half_packs(w_in[0, 0], w_out[0, 0])
    far, x_blocks, rows, back_rows = attention_weights(
        x0, w_qkv[0], w_proj[0], w_route[0], gain_attn[0], gain_ffn[0]
    )
    own = lax.all_gather(tie(halves[0], far), "shard", axis=0, tiled=False)
    attn_rows = both_layers(rows)
    back_rows = both_layers(back_rows)
    attn_rows[0], attn_rows[1], back_rows[0], back_rows[1] = lax.optimization_barrier(
        (attn_rows[0], attn_rows[1], back_rows[0], back_rows[1])
    )
    tables = [v[:, 576:584].T.astype(F32) for v in attn_rows]
    w_back = [[back_rows[0]] + [turn(back_rows[0], d) for d in (1, 2, 3)], None]
    experts = [None, None]

    saved = []
    x = x0
    layer_outs = []
    for s in range(2):
        if s == 1:
            x_blocks = [x] + [turn(x, -d) for d in (1, 2, 3)]
        mixture, x_all, packed, logs = attend(x_blocks, attn_rows[s], tables[s])
        if s == 0:
            w_back[0], mixture = lax.optimization_barrier((w_back[0], mixture))
        else:
            later, mixture[0] = lax.optimization_barrier((later, mixture[0]))
            experts[1] = (later, swap(later))
        gathered = send_out(mixture)
        d_out = d_last if s == 1 else None
        residual, normed, gates, chosen, high, low, buffer = middle(
            me, x, gathered, w_back[s], attn_rows[s], tables[s], route_of[s], d_out
        )
        blocks = send_out(buffer)
        kept = (x, x_all, packed, logs, gathered, residual, normed, gates, chosen, high, low, blocks)
        if s == 0:
            own = tie(own, blocks)
            experts[0] = (own, swap(own))
            later = lax.all_gather(tie(halves[1], own), "shard", axis=0, tiled=False)
            later_back = tie(back_rows[1], blocks)
            w_back[1] = [later_back] + [turn(later_back, d) for d in (1, 2, 3)]
            result = expert_run(blocks, *experts[s])
            w_back[1], result = lax.optimization_barrier((w_back[1], result))
            returned = send_back(result)
            x = combine(residual, high, low, returned)
            layer_outs.append(x)
            saved.append((kept, returned))
        else:
            saved.append((kept, None))

    d_out = d_last
    d_buffer = None
    in_grads = [None, None]
    expert_sums = [None, None]
    attn_grads = [None, None]
    for s in (1, 0):
        kept, returned = saved[s]
        x, x_all, packed, logs, gathered, residual, normed, gates, chosen, high, low, blocks = kept
        if s == 1:
            sent, *states = expert_back(blocks, experts[s], True)
            arrived = send_back(sent)
            layer_outs.append(combine(residual, high, low, [v[0] for v in arrived]))
        else:
            sent, *states = expert_back([*blocks, *send_out(d_buffer)], experts[s], False)
            back = send_back(sent)
            arrived = [*returned, *back]
        d_residual, small, grad_back, d_mixture = middle_back(
            me, d_out, arrived, gathered, chosen, gates, residual, normed, tables[s], w_back[s], s == 1
        )
        d_heads = send_back(d_mixture)
        rows, d_result, act_own, act_other, dh_own, dh_other = states
        if s == 1:
            both = expert_grads(core_index, rows, d_result, act_own, dh_own, act_other, dh_other)
            both = both.reshape(2 * N_SHARD, 4, 48, D)
            group = ("section", "shard")
        else:
            other = swap(expert_grad(rows, d_result, act_other, dh_other))
            both = expert_grad(rows, d_result, act_own, dh_own, (tie(other, back),))
            group = "shard"
        expert_sums[s] = lax.psum_scatter(both, group, scatter_dimension=0, tiled=True)[0]
        d_normed, grad_mix = attend_back(x_all, attn_rows[s], tables[s], packed, logs, d_heads, small)
        d_parts = send_out(d_normed)
        keep = jnp.where(core == 0, grad_mix, grad_back)
        give = jnp.where(core == 0, grad_back, grad_mix)
        attn_grads[s] = (keep.astype(F32) + swap(give).astype(F32)).astype(BF16)
        weights = saved[0][0][9:11] if s == 1 else None
        d_out, d_buffer = finish(d_residual, x, tables[s], d_parts, weights)
        in_grads[s] = d_out

    pair = jnp.concatenate(attn_grads, axis=1).reshape(N_SEQ * N_SHARD, 12, 12, 128)
    pair = pair.transpose(0, 2, 1, 3).reshape(N_SEQ * N_SHARD, 144, 128)
    pair = tie(pair, d_parts)
    arrived = lax.all_to_all(pair, ("seq", "shard"), 0, 0, tiled=True)
    attn_sum = jnp.sum(arrived.reshape(N_SEQ, N_SHARD, 144, 128).astype(F32), axis=1)
    attn_sums = [attn_sum[:, :72], attn_sum[:, 72:]]

    def settle(pair):
        keep = jnp.where(core == 0, pair[0], pair[1])
        give = jnp.where(core == 0, pair[1], pair[0])
        return keep, swap(give)

    def in_order(keep, got):
        return jnp.where(core == 0, jnp.stack([keep, got]), jnp.stack([got, keep]))

    layer_out = in_order(*settle(layer_outs))
    in_grad = in_order(*settle(in_grads))
    grad_in, grad_out = reorder(core_index, *settle(expert_sums))
    attn_sum = in_order(*settle(attn_sums)).reshape(2, N_SEQ, 6, 12, 128)
    attn_sum = attn_sum.transpose(0, 1, 3, 2, 4).reshape(2, N_SEQ, 12, D)
    mix = attn_sum[0]
    back = jnp.sum(attn_sum[1], axis=0)
    grad_qkv = mix[:, :, :576].reshape(N_SEQ, 12, 3, 192).transpose(1, 2, 0, 3).reshape(12, 3 * D)
    small = jnp.sum(mix[:, :, 576:640], axis=0)
    return (
        layer_out[None, :, None],
        in_grad[None, :, None],
        grad_qkv[None],
        back[None],
        small[None, :, 0:4],
        small[None, :, 4],
        small[None, :, 5],
        grad_in[None],
        grad_out[None],
    )


def solution(mesh):
    def run(*args):
        outs = shards(*args)
        outs = list(outs)
        outs[7] = outs[7][:, None]
        outs[8] = outs[8][:, None]
        return tuple(outs)

    return jax.shard_map(
        run,
        mesh=mesh,
        in_specs=(
            P(None, "shard", "seq", None),
            P(None, "shard", "seq", None),
            P("section", None, "shard", "seq", None),
            P("section", ("seq", "shard"), None),
            P("section", ("seq", "shard"), None),
            P("section", ("seq", "shard"), None),
            P("section", ("seq", "shard")),
            P("section", ("seq", "shard")),
            P("section", "seq", "shard", None),
            P("section", "seq", "shard", None),
        ),
        out_specs=(
            P("section", None, "shard", "seq", None),
            P("section", None, "shard", "seq", None),
            P("section", ("seq", "shard"), None),
            P("section", ("seq", "shard"), None),
            P("section", ("seq", "shard"), None),
            P("section", ("seq", "shard")),
            P("section", ("seq", "shard")),
            P("section", "seq", "shard", None),
            P("section", "seq", "shard", None),
        ),
        check_vma=False,
    )
```
